32 devices in a mesh: seq: 8 (over y, x, core), batch: 4 (over z).
Axes of the slice: x: 2, y: 2, z: 4, core: 2. Of those that a mesh axis runs over, the one named last changes fastest.
Arguments:
- tokens: bfloat16 [16, 2048, 512], P('batch', 'seq'), may hold values from -33 to 33
- lengths: int32 [16], P('batch'), may hold values from 512 to 2048, as said below
- cotangent: bfloat16 [16, 2048, 512], P('batch', 'seq'), may hold values from -6 to 6
- norm_gain: float32 [2, 512], replicated, may hold values from 0.5 to 1.5
- norm_shift: float32 [2, 512], replicated, may hold values from -1.75 to 1.75
- lift_weight: bfloat16 [2, 512, 512], replicated, may hold values from -0.25 to 0.25
- decay_log: float32 [2, 256], replicated, may hold values from -9.5 to -3.4
- phase_log: float32 [2, 256], replicated, may hold values from -7 to 1
- skip_gain: float32 [2, 512], replicated, may hold values from -3 to 3
- mix_weight: bfloat16 [2, 512, 512], replicated, may hold values from -0.25 to 0.25
- glu_weight: bfloat16 [2, 512, 1024], replicated, may hold values from -0.25 to 0.25
- glu_bias: float32 [2, 1024], replicated, may hold values from -1.75 to 1.75
Outputs:
- produced: bfloat16 [16, 2048, 512], P('batch', 'seq')
- input_grad: bfloat16 [16, 2048, 512], P('batch', 'seq')
- grad_norm_gain: float32 [2, 512], replicated
- grad_norm_shift: float32 [2, 512], replicated
- grad_lift: float32 [2, 512, 512], replicated
- grad_decay: float32 [2, 256], replicated
- grad_phase: float32 [2, 256], replicated
- grad_skip: float32 [2, 512], replicated
- grad_mix: float32 [2, 512, 512], replicated
- grad_glu: float32 [2, 512, 1024], replicated
- grad_glu_bias: float32 [2, 1024], replicated
The draws below stay inside these ranges and needn't reach their ends.
Inputs may be any that keep to these rules, and one draw needn't show every extreme that they name: `lengths`: each group of 4 sequences on one index of batch holds one of length 2048, which one drawn from the seed.
All inputs are finite; a program needn't handle non-finite values.
Results may differ from the reference program's by a relative error of at most 0.015.
Values may be sent and summed in bfloat16 or wider, within the bound.
No kernel may reach another device: no remote copies, remote signals or barrier semaphores. Data moves between devices by JAX's collectives and lax.ppermute only.
A program may use at most 192 MiB of HBM per device.

```python
import jax
import jax.numpy as jnp
from jax import lax

D = 512
N = 256
SEQ_DEV = 4
BLOCKS = 2
LEN = 2048
SEQS = 16


def draw_tokens(key, part):
    key = jax.random.fold_in(key, 5)
    noise_key, centre_key = jax.random.split(key, 2)
    ramp = 1.0 + 2.0 * jnp.arange(LEN, dtype=jnp.float32)[None, :, None] / LEN
    centre = jnp.clip(jax.random.normal(centre_key, (1, 1, D), jnp.float32), -2.0, 2.0) * 0.5
    noise = jnp.clip(jax.random.normal(noise_key, (SEQS, LEN, D), jnp.float32), -4.0, 4.0)
    return ((noise + centre) * ramp).astype(jnp.bfloat16)


def draw_lengths(key, part):
    key = jax.random.fold_in(key, 11)
    pick_key, length_key = jax.random.split(key)
    groups = SEQS // SEQ_DEV
    drawn = jax.random.randint(length_key, (groups, SEQ_DEV), LEN // 4, LEN + 1)
    chosen = jax.random.randint(pick_key, (groups, 1), 0, SEQ_DEV)
    whole = jnp.arange(SEQ_DEV, dtype=jnp.int32)[None, :] == chosen
    return jnp.where(whole, LEN, drawn).reshape(SEQS).astype(jnp.int32)


def block_levels(stream_key, extent, cuts, low, top_value):
    level, own = 1.0, jax.random.fold_in(stream_key, 6)
    for dim, blocks in cuts:
        steps = jnp.exp(jax.random.uniform(jax.random.fold_in(own, dim), (blocks,), jnp.float32, low / len(cuts), top_value / len(cuts)))
        level = level * jnp.repeat(steps, extent[dim] // blocks).reshape([-1 if axis == dim else 1 for axis in range(len(extent))])
    return level


def normal_values(key, shape, scale, limit, cuts=(), held_as=jnp.bfloat16):
    gain = block_levels(key, shape, cuts, -0.22, 0.18) if cuts else 1.0
    result = jax.random.normal(key, shape, jnp.float32) * scale * gain
    return jnp.minimum(jnp.maximum(result, -limit), limit).astype(held_as)


def setup_inputs(seed: int = 0) -> dict:
    splits = jax.random.split(jax.random.key(seed), 13)
    return {
        "tokens": draw_tokens(jax.random.fold_in(splits[12], 71), 0),
        "lengths": draw_lengths(jax.random.fold_in(splits[12], 71), 0),
        "cotangent": normal_values(splits[2], (SEQS, LEN, D), 1.0, 6.0, ((0, 4), (1, 8))),
        "norm_gain": jnp.clip(1.0 + 0.1 * jax.random.normal(splits[3], (BLOCKS, D), jnp.float32), 0.5, 1.5),
        "norm_shift": normal_values(splits[4], (BLOCKS, D), 0.3, 1.75, (), jnp.float32),
        "lift_weight": normal_values(splits[5], (BLOCKS, D, 2 * N), D ** -0.5, 0.25),
        "decay_log": jnp.clip(jax.random.uniform(splits[6], (BLOCKS, N), jnp.float32, -9.5, -3.4), -9.5, -3.4),
        "phase_log": jnp.clip(jax.random.uniform(splits[7], (BLOCKS, N), jnp.float32, -7.0, 1.0), -7.0, 1.0),
        "skip_gain": normal_values(splits[8], (BLOCKS, D), 0.5, 3.0, (), jnp.float32),
        "mix_weight": normal_values(splits[9], (BLOCKS, 2 * N, D), (2 * N) ** -0.5, 0.25),
        "glu_weight": normal_values(splits[10], (BLOCKS, D, 2 * D), D ** -0.5, 0.25),
        "glu_bias": normal_values(splits[11], (BLOCKS, 2 * D), 0.3, 1.75, (), jnp.float32),
    }


@jax.custom_vjp
def low(v):
    return lax.optimization_barrier(v.astype(jnp.bfloat16)).astype(jnp.float32)

@jax.custom_vjp
def low_back(v):
    return v

def low_keep(v):
    return (low(v), None)

def low_pass(kept, grad):
    return (grad,)

def back_keep(v):
    return (v, None)

def back_low(kept, grad):
    return (low(grad),)
low.defvjp(low_keep, low_pass)
low_back.defvjp(back_keep, back_low)
norm_eps = 1e-05
highest = lax.Precision.HIGHEST

def complex_step(earlier, later):
    carry_real, carry_imaginary, state_real, state_imaginary = earlier
    factor_real, factor_imaginary, input_real, input_imaginary = later
    return (factor_real * carry_real - factor_imaginary * carry_imaginary, factor_real * carry_imaginary + factor_imaginary * carry_real, factor_real * state_real - factor_imaginary * state_imaginary + input_real, factor_real * state_imaginary + factor_imaginary * state_real + input_imaginary)

def rotation_decay(decay_log, phase_log):
    decay_rate = jnp.exp(decay_log)
    magnitude = jnp.exp(-decay_rate)
    phase_angle = jnp.exp(phase_log)
    return (magnitude * jnp.cos(phase_angle), magnitude * jnp.sin(phase_angle), jnp.sqrt(1.0 - jnp.exp(-2.0 * decay_rate)))

def residual_block(current, valid, weights, backwards):
    norm_gain, norm_shift, lift_weight, decay_log, phase_log, skip_gain, mix_weight, glu_weight, glu_bias = weights
    valid_col = valid[..., None]
    count = jnp.sum(valid)
    average = lax.optimization_barrier(jnp.sum(current * valid_col, axis=(0, 1))) / count
    variance = lax.optimization_barrier(jnp.sum(current * current * valid_col, axis=(0, 1))) / count - average * average
    normed = low((current - average) * lax.rsqrt(variance + norm_eps) * norm_gain + norm_shift)
    lifted = low_back(low(jnp.einsum('sth,hn->stn', normed, lift_weight, precision=highest)))
    state_count = decay_log.shape[0]
    decay_real, decay_imaginary, input_scale = rotation_decay(decay_log, phase_log)
    factor_real = valid_col * decay_real + (1.0 - valid_col)
    factor_imaginary = valid_col * decay_imaginary
    drive = input_scale * valid_col
    scanned = lax.associative_scan(complex_step, (factor_real, factor_imaginary, drive * lifted[..., :state_count], drive * lifted[..., state_count:]), reverse=backwards, axis=1)
    state_low = low_back(low(jnp.concatenate([scanned[2], scanned[3]], axis=-1)))
    mixed = low_back(jnp.einsum('stn,nh->sth', state_low, mix_weight, precision=highest) + skip_gain * normed)
    activated = low(jax.nn.gelu(mixed, approximate=True))
    projected = low_back(jnp.einsum('sth,hj->stj', activated, glu_weight, precision=highest) + glu_bias)
    model_width = current.shape[-1]
    return current + projected[..., :model_width] * jax.nn.sigmoid(projected[..., model_width:])

def reference(tokens, lengths, cotangent, norm_gain, norm_shift, lift_weight, decay_log, phase_log, skip_gain, mix_weight, glu_weight, glu_bias):
    positions = jnp.arange(tokens.shape[1], dtype=jnp.int32)
    valid = (positions[None, :] < lengths[:, None]).astype(jnp.float32)
    params = tuple((entry.astype(jnp.float32) for entry in (norm_gain, norm_shift, lift_weight, decay_log, phase_log, skip_gain, mix_weight, glu_weight, glu_bias)))

    def network(inputs, *weights):
        current = inputs
        for block_index in range(2):
            current = residual_block(current, valid, tuple((entry[block_index] for entry in weights)), block_index == 1)
        return current * valid[..., None]
    produced, pullback = jax.vjp(network, tokens.astype(jnp.float32), *params)
    gradients = pullback(cotangent.astype(jnp.float32))
    return (produced.astype(jnp.bfloat16), gradients[0].astype(jnp.bfloat16), gradients[1], gradients[2], gradients[3], gradients[4], gradients[5], gradients[6], gradients[7], gradients[8], gradients[9])
```

```python
from functools import partial

import jax
import jax.numpy as jnp
from jax import lax
from jax.experimental import pallas as pl
from jax.experimental.pallas import tpu as pltpu
from jax.sharding import PartitionSpec as P

norm_eps = 1e-05
f32 = jnp.float32
bf16 = jnp.bfloat16

CHUNKS = 8
BLOCKS = 4
LANES = 128
VMEM_LIMIT = 24 * 1024 * 1024

in_vmem = pl.BlockSpec(memory_space=pltpu.VMEM)
in_smem = pl.BlockSpec(memory_space=pltpu.SMEM)
in_hbm = pl.BlockSpec(memory_space=pltpu.HBM)


def near(shape, dtype):
    return in_vmem, pltpu.VMEM(shape, dtype)


def far(shape, dtype):
    return in_hbm, pltpu.HBM(shape, dtype)


def moved(shape, dtype):
    return in_vmem, jax.ShapeDtypeStruct(shape, dtype)


def call(kernel, info, inputs, arrays, away, outs, scratch, name):
    arrays = [pltpu.with_memory_space_constraint(a, pltpu.VMEM) for a in arrays]
    away = [pltpu.with_memory_space_constraint(a, pltpu.HBM) for a in away]
    return pl.pallas_call(
        kernel,
        in_specs=[in_smem] + [in_vmem] * (len(inputs) + len(arrays)) + [in_hbm] * len(away),
        out_specs=[spec for spec, _ in outs],
        out_shape=[shape for _, shape in outs],
        scratch_shapes=scratch,
        compiler_params=pltpu.CompilerParams(vmem_limit_bytes=VMEM_LIMIT),
        name=name,
    )(info, *inputs, *arrays, *away)


class Copies:
    def __init__(self, sources, targets, sems):
        self.sources, self.targets, self.sems = sources, targets, sems
        self.size = sources[0].shape[0] // BLOCKS

    def copy(self, n, block):
        here = pl.ds(block * self.size, self.size)
        return pltpu.make_async_copy(self.sources[n].at[here, :], self.targets[n].at[here, :], self.sems.at[n, block])

    def start(self, block):
        for n in range(len(self.sources)):
            self.copy(n, block).start()

    def wait(self, block):
        for n in range(len(self.sources)):
            self.copy(n, block).wait()


def staged(shapes):
    return [pltpu.VMEM(shape, dtype) for shape, dtype in shapes] + [pltpu.SemaphoreType.DMA((len(shapes), BLOCKS))]


def wide(mask, width):
    return jnp.concatenate([mask] * (width // LANES), axis=1)


def dot(a, b):
    return lax.dot_general(a, b, (((1,), (0,)), ((), ())), preferred_element_type=f32)


def dot_t(a, b):
    return lax.dot_general(a, b, (((1,), (1,)), ((), ())), preferred_element_type=f32)


def t_dot(a, b):
    return lax.dot_general(a, b, (((0,), (0,)), ((), ())), preferred_element_type=f32)


def cmul(ar, ai, br, bi):
    return ar * br - ai * bi, ar * bi + ai * br


def order(steps, reverse):
    return range(steps - 1, -1, -1) if reverse else range(steps)


def shuffle_matrix(span, back):
    chunk = span // CHUNKS
    place = lax.broadcasted_iota(jnp.int32, (span, span), 0)
    source = lax.broadcasted_iota(jnp.int32, (span, span), 1)
    if back:
        wanted = (place % chunk) * CHUNKS + place // chunk
    else:
        wanted = (place % CHUNKS) * chunk + place // CHUNKS
    return (source == wanted).astype(f32).astype(bf16)


class Where:
    def __init__(self, info_ref, seqs, span):
        self.seq, self.batch = info_ref[0], info_ref[1]
        self.seqs, self.span = seqs, span
        self.lengths = [info_ref[2 + s] for s in range(seqs)]
        self.lefts = [length - self.seq * span for length in self.lengths]

    def steps_left(self):
        before = (self.span // CHUNKS) * lax.broadcasted_iota(jnp.int32, (CHUNKS, LANES), 0)
        return jnp.concatenate([left - before for left in self.lefts], axis=0)


def valid_rows(left, first, steps):
    return jnp.concatenate([(left > first + t).astype(f32) for t in range(steps)], axis=0)


def shuffle_rows(wide_ref, source_ref):
    steps, seqs, chunks, width = wide_ref.shape
    shuffle = shuffle_matrix(steps * chunks, False)
    for s in range(seqs):
        wide_ref[:, s] = dot(shuffle, source_ref[s]).reshape(steps, chunks, width)


def enter_kernel(info_ref, tokens_ref, rows_ref, sums_ref, wide_ref, acc_ref):
    seqs, span, width = tokens_ref.shape
    where = Where(info_ref, seqs, span)
    step = lax.broadcasted_iota(jnp.int32, (span, 1), 0)
    total = jnp.zeros((1, width), f32)
    squares = jnp.zeros((1, width), f32)
    count = jnp.zeros((1, 1), f32)
    for s in range(seqs):
        valid = (step < where.lefts[s]).astype(f32)
        x = tokens_ref[s].astype(f32)
        masked = x * valid
        total += jnp.sum(masked, axis=0, keepdims=True)
        squares += jnp.sum(masked * x, axis=0, keepdims=True)
        count += jnp.sum(valid, axis=0, keepdims=True)
    tail = jnp.broadcast_to(count, (1, LANES))
    acc_ref[0:1, :] = jnp.concatenate([total, tail], axis=1)
    acc_ref[1:2, :] = jnp.concatenate([squares, tail], axis=1)
    for j in range(sums_ref.shape[0]):
        sums_ref[j] = acc_ref[...]
    shuffle_rows(wide_ref, tokens_ref)
    rows_ref[...] = wide_ref[...].reshape(seqs * span, width).astype(bf16)


def enter(info, tokens, devices):
    seqs, span, width = tokens.shape
    return call(
        enter_kernel,
        info,
        (tokens,),
        (),
        (),
        [near((seqs * span, width), bf16), moved((devices, 2, width + LANES), f32)],
        [pltpu.VMEM((span // CHUNKS, seqs, CHUNKS, width), f32), pltpu.VMEM((2, width + LANES), f32)],
        "enter",
    )


def power_kernel(span, seqs, info_ref, decay_ref, phase_ref, lam_ref, scale_ref, *outs):
    blocks, states = decay_ref.shape
    groups = states // LANES
    group = outs[0].shape[1]
    total, limit = outs[1].shape[0], span // CHUNKS
    where = Where(info_ref, seqs, span)
    rate = jnp.exp(decay_ref[...])
    size, angle = jnp.exp(-rate), jnp.exp(phase_ref[...])
    lam_ref[:, :states] = size * jnp.cos(angle)
    lam_ref[:, states:] = size * jnp.sin(angle)
    scale_ref[...] = jnp.sqrt(1.0 - jnp.exp(-2.0 * rate))
    chunk_left = where.steps_left()
    line = lax.broadcasted_iota(jnp.int32, (total, LANES), 0)
    span_left = jnp.zeros((total, LANES), jnp.int32)
    for s, length in enumerate(where.lengths):
        span_left = jnp.where(line % seqs == s, length - span * (line // seqs), span_left)
    for k in range(blocks):
        for back in (0, 1):
            table_ref, leap_ref = outs[4 * k + 2 * back : 4 * k + 2 * back + 2]
            shift = 0 if not back else (-1 if k == 0 else 1)
            chunk_count = jnp.clip(chunk_left + shift, 0, limit)
            span_count = jnp.clip(span_left + shift, 0, span)
            for low in range(groups):
                real_lanes = slice(low * LANES, (low + 1) * LANES)
                imag_lanes = slice((groups + low) * LANES, (groups + low + 1) * LANES)
                br, bi = lam_ref[k : k + 1, real_lanes], lam_ref[k : k + 1, imag_lanes]
                if back:
                    bi = -bi
                cr = jnp.ones((group, LANES), f32)
                ci = jnp.zeros((group, LANES), f32)
                pr = jnp.ones((total, LANES), f32)
                pi = jnp.zeros((total, LANES), f32)
                for bit in range(span.bit_length()):
                    if (1 << bit) <= limit:
                        nr, ni = cmul(cr, ci, br, bi)
                        odd = (chunk_count & (1 << bit)) != 0
                        cr, ci = jnp.where(odd, nr, cr), jnp.where(odd, ni, ci)
                    nr, ni = cmul(pr, pi, br, bi)
                    odd = (span_count & (1 << bit)) != 0
                    pr, pi = jnp.where(odd, nr, pr), jnp.where(odd, ni, pi)
                    br, bi = cmul(br, bi, br, bi)
                table_ref[low] = cr
                table_ref[groups + low] = ci
                leap_ref[:, real_lanes] = pr
                leap_ref[:, imag_lanes] = pi


def power_tables(info, decay_log, phase_log, seqs, seq_devices, span):
    blocks, states = decay_log.shape
    outs = [near((blocks, 2 * states), f32), near((blocks, states), f32)]
    for _ in range(2 * blocks):
        outs.append(near((2 * states // LANES, seqs * CHUNKS, LANES), f32))
        outs.append(near((seq_devices * seqs, 2 * states), f32))
    return call(partial(power_kernel, span, seqs), info, (), (decay_log, phase_log), (), outs, [], "powers")


def stretch_part(ends_ref, power_ref, reverse, seqs):
    groups = ends_ref.shape[0] // 2
    reals, imags = [], []
    for low in range(groups):
        real = jnp.zeros((seqs, LANES), f32)
        imag = jnp.zeros((seqs, LANES), f32)
        for c in order(CHUNKS, reverse):
            here = pl.ds(c, seqs, stride=CHUNKS)
            real, imag = cmul(power_ref[low, here, :], power_ref[groups + low, here, :], real, imag)
            real += ends_ref[low, here, :]
            imag += ends_ref[groups + low, here, :]
        reals.append(real)
        imags.append(imag)
    return jnp.concatenate(reals + imags, axis=1)


def chunk_starts(start_ref, place, parts_ref, leaps_ref, ends_ref, power_ref, reverse):
    devices, seqs, width = parts_ref.shape
    states = width // 2
    groups = states // LANES
    real = jnp.zeros((seqs, states), f32)
    imag = jnp.zeros((seqs, states), f32)
    for j in order(devices, reverse):
        ahead = (j > place) if reverse else (j < place)
        leap, part = leaps_ref[seqs * j : seqs * (j + 1), :], parts_ref[j]
        next_real, next_imag = cmul(leap[:, :states], leap[:, states:], real, imag)
        real = jnp.where(ahead, next_real + part[:, :states], real)
        imag = jnp.where(ahead, next_imag + part[:, states:], imag)
    for low in range(groups):
        hr = real[:, low * LANES : (low + 1) * LANES]
        hi = imag[:, low * LANES : (low + 1) * LANES]
        for c in order(CHUNKS, reverse):
            here = pl.ds(c, seqs, stride=CHUNKS)
            start_ref[low, here, :] = hr
            start_ref[groups + low, here, :] = hi
            hr, hi = cmul(power_ref[low, here, :], power_ref[groups + low, here, :], hr, hi)
            hr += ends_ref[low, here, :]
            hi += ends_ref[groups + low, here, :]


def scan_block(h_ref, drive, left, lam, conjugate, shift, first, steps, reverse, out_ref=None):
    groups, group, _ = h_ref.shape
    groups = groups // 2
    masks = [left > first + t + shift for t in range(steps)]
    for low in range(groups):
        real_lanes = slice(low * LANES, (low + 1) * LANES)
        imag_lanes = slice((groups + low) * LANES, (groups + low + 1) * LANES)
        hr, hi = h_ref[low], h_ref[groups + low]
        lr, li = lam[:, real_lanes], lam[:, imag_lanes]
        if conjugate:
            li = -li
        for t in order(steps, reverse):
            ur, ui = drive(t, real_lanes, imag_lanes)
            nr, ni = cmul(lr, li, hr, hi)
            hr = jnp.where(masks[t], nr, hr) + ur
            hi = jnp.where(masks[t], ni, hi) + ui
            if out_ref is not None:
                out_ref[t * group : (t + 1) * group, real_lanes] = hr
                out_ref[t * group : (t + 1) * group, imag_lanes] = hi
        h_ref[low] = hr
        h_ref[groups + low] = hi


def input_drive(lifted, scale, left, first, steps):
    group = left.shape[0]
    masks = [left > first + t for t in range(steps)]

    def drive(t, real_lanes, imag_lanes):
        here = slice(t * group, (t + 1) * group)
        factor = jnp.where(masks[t], scale[:, real_lanes], 0.0)
        return factor * lifted[here, real_lanes], factor * lifted[here, imag_lanes]

    return drive


def blocks_of(rows, group, reverse):
    size = rows // BLOCKS
    for block in order(BLOCKS, reverse):
        yield block, block * (size // group), slice(block * size, (block + 1) * size)


def lift_kernel(k, seqs, info_ref, sums_ref, *refs):
    reverse = k == 1
    if k == 0:
        x_ref, refs = refs[0], refs[1:]
    else:
        count_ref, x_ref = refs[:2]
        refs = refs[2:]
    gain_ref, shift_ref, weight_ref, lam_ref, scale_ref, power_ref = refs[:6]
    normed_ref, lifted_ref, ends_ref, part_ref, stats_ref = refs[6:11]
    rows, width = x_ref.shape
    group = ends_ref.shape[1]
    steps = rows // BLOCKS // group
    where = Where(info_ref, seqs, rows // seqs)
    sums = jnp.sum(sums_ref[...], axis=0)
    if k == 0:
        kept_count_ref = refs[11]
        kept_count_ref[...] = jnp.broadcast_to(sums[0:1, width:], kept_count_ref.shape)
        count = sums[0:1, width : width + 1]
    else:
        count = count_ref[0:1, 0:1]
    average = sums[0:1, :width] / count
    root = lax.rsqrt(sums[1:2, :width] / count - average * average + norm_eps)
    stats_ref[0:1, :] = average
    stats_ref[1:2, :] = root
    gain, shift = gain_ref[k : k + 1, :], shift_ref[k : k + 1, :]
    lam, scale = lam_ref[k : k + 1, :], scale_ref[k : k + 1, :]
    left = where.steps_left()
    ends_ref[...] = jnp.zeros_like(ends_ref)
    for _, first, now in blocks_of(rows, group, reverse):
        normed = ((x_ref[now, :].astype(f32) - average) * root * gain + shift).astype(bf16)
        normed_ref[now, :] = normed
        lifted = dot(normed, weight_ref[k]).astype(bf16)
        lifted_ref[now, :] = lifted
        drive = input_drive(lifted.astype(f32), scale, left, first, steps)
        scan_block(ends_ref, drive, left, lam, False, 0, first, steps, reverse)
    part = stretch_part(ends_ref, power_ref, reverse, seqs)
    for j in range(part_ref.shape[0]):
        part_ref[j] = part


def lift(k, seqs, seq_devices, info, sums, arrays):
    rows, width = arrays[0 if k == 0 else 1].shape
    table = arrays[-1].shape
    states = table[0] * LANES
    outs = [
        near((rows, width), bf16),
        near((rows, states), bf16),
        near(table, f32),
        moved((seq_devices, seqs, states), f32),
        near((2, width), f32),
    ]
    if k == 0:
        outs.append(near((8, LANES), f32))
    return call(partial(lift_kernel, k, seqs), info, (sums,), arrays, (), outs, [], "lift")


def mix_kernel(k, info_ref, parts_ref, *refs):
    reverse = k == 1
    (leaps_ref, ends_ref, power_ref, lifted_ref, normed_ref, x_ref) = refs[:6]
    (mix_ref, skip_ref, glu_ref, bias_ref, lam_ref, scale_ref) = refs[6:12]
    refs = refs[12:]
    if reverse:
        state_ref, activated_ref, slope_ref, gate_ref, gate_slope_ref, masked_out = refs[:6]
        h_ref, states_ref, masked_ref, sems = refs[6:]
        copies = Copies([masked_ref], [masked_out], sems)
    else:
        next_ref, sums_ref = refs[:2]
        away, refs = refs[2:8], refs[8:]
        h_ref, states_ref, acc_ref = refs[:3]
        here = refs[3:9]
        state_ref, activated_ref, slope_ref, gate_ref, gate_slope_ref, low_next_ref = here
        copies = Copies(here, away, refs[9])
    seqs = parts_ref.shape[1]
    rows, width = x_ref.shape
    group = ends_ref.shape[1]
    steps = rows // BLOCKS // group
    where = Where(info_ref, seqs, rows // seqs)
    chunk_starts(h_ref, where.seq, parts_ref, leaps_ref, ends_ref, power_ref, reverse)
    left = where.steps_left()
    skip, bias = skip_ref[k : k + 1, :], bias_ref[k : k + 1, :]
    lam, scale = lam_ref[k : k + 1, :], scale_ref[k : k + 1, :]
    total = jnp.zeros((1, width), f32)
    squares = jnp.zeros((1, width), f32)
    for block, first, now in blocks_of(rows, group, reverse):
        drive = input_drive(lifted_ref[now, :].astype(f32), scale, left, first, steps)
        scan_block(h_ref, drive, left, lam, False, 0, first, steps, reverse, states_ref)
        state = states_ref[...].astype(bf16)
        state_ref[now, :] = state
        mixed = dot(state, mix_ref[k]) + skip * normed_ref[now, :].astype(f32)
        base, cube = 0.7978845608028654, 0.044715
        square = mixed * mixed
        bend = jnp.tanh(mixed * (base + (base * cube) * square))
        half = 0.5 + 0.5 * bend
        activated = (mixed * half).astype(bf16)
        activated_ref[now, :] = activated
        slope_ref[now, :] = (
            half + mixed * (half - half * half) * (2.0 * base + (6.0 * base * cube) * square)
        ).astype(bf16)
        projected = dot(activated, glu_ref[k]) + bias
        gate = 0.5 + 0.5 * jnp.tanh(0.5 * projected[:, width:])
        gated = projected[:, :width] * gate
        gate_ref[now, :] = gate.astype(bf16)
        gate_slope_ref[now, :] = (gated - gated * gate).astype(bf16)
        after = x_ref[now, :].astype(f32) + gated
        masked = after * wide(valid_rows(left, first, steps), width)
        if reverse:
            masked_ref[now, :] = masked.astype(bf16)
        else:
            next_ref[now, :] = after
            low_next_ref[now, :] = after.astype(bf16)
            total += jnp.sum(masked, axis=0, keepdims=True)
            squares += jnp.sum(masked * after, axis=0, keepdims=True)
        copies.start(block)
    if not reverse:
        acc_ref[0:1, :] = total
        acc_ref[1:2, :] = squares
        for j in range(sums_ref.shape[0]):
            sums_ref[j] = acc_ref[...]
    for block in range(BLOCKS):
        copies.wait(block)


def mix(k, info, parts, arrays, devices):
    rows, width = arrays[5].shape
    states = arrays[3].shape[1]
    wide_shape, state_shape = ((rows, width), bf16), ((rows, states), bf16)
    scratch = [pltpu.VMEM(arrays[2].shape, f32), pltpu.VMEM((rows // BLOCKS, states), f32)]
    if k == 1:
        outs = [near(*state_shape)] + [near(*wide_shape)] * 4 + [far(*wide_shape)]
        scratch += staged([wide_shape])
    else:
        outs = [near((rows, width), f32), moved((devices, 2, width), f32), far(*state_shape)] + [far(*wide_shape)] * 5
        scratch += [pltpu.VMEM((2, width), f32)] + staged([state_shape] + [wide_shape] * 5)
    return call(partial(mix_kernel, k), info, (parts,), arrays, (), outs, scratch, "mix")


def glu_back_kernel(k, seqs, info_ref, *refs):
    reverse = k == 0
    if k == 1:
        cot_ref, normed_ref, slope_ref, gate_ref, gate_slope_ref = refs[:5]
        refs = refs[5:]
    else:
        sums_ref, back_normed_ref, stats_ref, gain_ref, count_ref = refs[:5]
        refs = refs[5:]
    glu_ref, mix_ref, lam_ref, power_ref = refs[:4]
    refs = refs[4:]
    if k == 0:
        away, refs = refs[:6], refs[6:]
    (projected_ref, mixed_ref, dh_ref, bias_grad_ref, skip_grad_ref, ends_ref, part_ref) = refs[:7]
    refs = refs[7:]
    rows, width = mixed_ref.shape
    group = ends_ref.shape[1]
    size = rows // BLOCKS
    steps = size // group
    where = Where(info_ref, seqs, rows // seqs)
    if k == 1:
        back_out, wide_ref, back_ref, sems = refs
        copies = Copies([back_ref], [back_out], sems)
        shuffle_rows(wide_ref, cot_ref)
    else:
        back_ref, total_ref = refs[:2]
        here = refs[2:8]
        x_ref, before_ref, normed_ref, slope_ref, gate_ref, gate_slope_ref = here
        copies = Copies(away, here, refs[8])
        for block in order(BLOCKS, reverse):
            copies.start(block)
        sums = jnp.sum(sums_ref[...], axis=0)
        total_ref[...] = sums
        count = count_ref[0:1, 0:1]
        gain_sum, shift_sum = sums[0:1], sums[1:2]
        average, root = stats_ref[0:1, :], stats_ref[1:2, :]
        gain = gain_ref[1:2, :]
    left = where.steps_left()
    lam = lam_ref[k : k + 1, :]
    ends_ref[...] = jnp.zeros_like(ends_ref)
    bias_grad = jnp.zeros((1, 2 * width), f32)
    skip_grad = jnp.zeros((1, width), f32)
    for block, first, now in blocks_of(rows, group, reverse):
        valid = wide(valid_rows(left, first, steps), width)
        if k == 1:
            back = wide_ref[first : first + steps].reshape(size, width) * valid
        else:
            copies.wait(block)
            centered = (x_ref[now, :].astype(f32) - average) * root
            back_normed = back_normed_ref[now, :].astype(f32)
            back = before_ref[now, :].astype(f32) + (root * gain) * (
                back_normed - valid * ((shift_sum + centered * gain_sum) / count)
            )
        back_ref[now, :] = back.astype(bf16)
        if k == 1:
            copies.start(block)
        value_back = (back * gate_ref[now, :].astype(f32)).astype(bf16)
        gate_back = (back * gate_slope_ref[now, :].astype(f32)).astype(bf16)
        back_projected = jnp.concatenate([value_back, gate_back], axis=1)
        projected_ref[now, :] = back_projected
        bias_grad += jnp.sum(back_projected.astype(f32), axis=0, keepdims=True)
        back_activated = dot_t(back_projected, glu_ref[k])
        back_mixed = (slope_ref[now, :].astype(f32) * back_activated).astype(bf16)
        mixed_ref[now, :] = back_mixed
        skip_grad += jnp.sum(back_mixed.astype(f32) * normed_ref[now, :].astype(f32), axis=0, keepdims=True)
        back_state = dot_t(back_mixed, mix_ref[k]).astype(bf16)
        dh_ref[now, :] = back_state
        wide_state = back_state.astype(f32)

        def drive(t, real_lanes, imag_lanes):
            at = slice(t * group, (t + 1) * group)
            return wide_state[at, real_lanes], wide_state[at, imag_lanes]

        shift = 1 if reverse else -1
        scan_block(ends_ref, drive, left, lam, True, shift, first, steps, reverse)
    bias_grad_ref[...] = bias_grad
    skip_grad_ref[...] = skip_grad
    part = stretch_part(ends_ref, power_ref, reverse, seqs)
    for j in range(part_ref.shape[0]):
        part_ref[j] = part
    if k == 1:
        for block in range(BLOCKS):
            copies.wait(block)


def glu_back(k, seqs, seq_devices, info, inputs, arrays, away):
    table = arrays[-1].shape
    states = table[0] * LANES
    width = arrays[-4].shape[1]
    rows = arrays[1 if k == 1 else 0].shape[0]
    outs = [
        near((rows, 2 * width), bf16),
        near((rows, width), bf16),
        near((rows, states), bf16),
        near((1, 2 * width), f32),
        near((1, width), f32),
        near(table, f32),
        moved((seq_devices, seqs, states), f32),
    ]
    if k == 1:
        outs.append(far((rows, width), bf16))
        scratch = [pltpu.VMEM((rows // seqs // CHUNKS, seqs, CHUNKS, width), f32)] + staged([((rows, width), bf16)])
    else:
        outs += [near((rows, width), bf16), near((2, width), f32)]
        scratch = staged([(a.shape, a.dtype) for a in away])
    return call(partial(glu_back_kernel, k, seqs), info, inputs, arrays, away, outs, scratch, "glu_back")


def lift_back_kernel(k, info_ref, parts_ref, *refs):
    reverse = last = k == 0
    (leaps_ref, ends_ref, power_ref, dh_ref, mixed_ref) = refs[:5]
    (stats_ref, weight_ref, skip_ref, lam_ref, scale_ref) = refs[5:10]
    refs = refs[10:]
    if last:
        back_ref, gain_ref = refs[:2]
        small_refs, away, refs = refs[2:8], refs[8:11], refs[11:]
        back_lifted_ref, sums_ref, ahead_ref = refs[:3]
        refs = refs[3:]
        lifted_ref, state_ref, x_ref, sems = refs[-4:]
        copies = Copies(away, refs[-4:-1], sems)
        refs = refs[:-4]
        for block in order(BLOCKS, reverse):
            copies.start(block)
    else:
        lifted_ref, state_ref, x_ref = refs[:3]
        back_lifted_ref, sums_ref, back_normed_ref, lam_grad_ref, scale_grad_ref = refs[3:8]
        refs = refs[8:]
    h_ref, low_ref, acc_ref, lam_acc_ref, scale_acc_ref = refs
    rows, width = x_ref.shape
    group = ends_ref.shape[1]
    seqs = parts_ref.shape[1]
    steps = rows // BLOCKS // group
    states = scale_ref.shape[1]
    where = Where(info_ref, seqs, rows // seqs)
    chunk_starts(h_ref, where.seq, parts_ref, leaps_ref, ends_ref, power_ref, reverse)
    lam_acc_ref[...] = jnp.zeros_like(lam_acc_ref)
    scale_acc_ref[...] = jnp.zeros_like(scale_acc_ref)
    left = where.steps_left()
    lam, scale = lam_ref[k : k + 1, :], scale_ref[k : k + 1, :]
    average, root = stats_ref[0:1, :], stats_ref[1:2, :]
    skip = skip_ref[k : k + 1, :]
    gain_sum = jnp.zeros((1, width), f32)
    shift_sum = jnp.zeros((1, width), f32)
    shift = 1 if reverse else -1
    for block, first, now in blocks_of(rows, group, reverse):
        moving = [left > first + t + shift for t in range(steps)]
        valid = [left > first + t for t in range(steps)]
        if last:
            copies.wait(block)
        dh = dh_ref[now, :].astype(f32)
        lifted = lifted_ref[now, :].astype(f32)
        state = state_ref[now, :].astype(f32)
        for low in range(0, states, LANES):
            real_lanes = slice(low, low + LANES)
            imag_lanes = slice(states + low, states + low + LANES)
            gr, gi = h_ref[low // LANES], h_ref[(states + low) // LANES]
            lr, li = lam[:, real_lanes], -lam[:, imag_lanes]
            part = scale[:, real_lanes]
            sum_r, sum_i = lam_acc_ref[:, real_lanes], lam_acc_ref[:, imag_lanes]
            sum_s = scale_acc_ref[:, real_lanes]
            for t in order(steps, reverse):
                at = slice(t * group, (t + 1) * group)
                hr, hi = state[at, real_lanes], state[at, imag_lanes]
                ur, ui = lifted[at, real_lanes], lifted[at, imag_lanes]
                mr, mi = jnp.where(moving[t], gr, 0.0), jnp.where(moving[t], gi, 0.0)
                sum_r += mr * hr + mi * hi
                sum_i += mi * hr - mr * hi
                nr, ni = cmul(lr, li, gr, gi)
                gr = jnp.where(moving[t], nr, gr) + dh[at, real_lanes]
                gi = jnp.where(moving[t], ni, gi) + dh[at, imag_lanes]
                vr, vi = jnp.where(valid[t], gr, 0.0), jnp.where(valid[t], gi, 0.0)
                sum_s += vr * ur + vi * ui
                low_ref[at, real_lanes] = part * vr
                low_ref[at, imag_lanes] = part * vi
            h_ref[low // LANES] = gr
            h_ref[(states + low) // LANES] = gi
            lam_acc_ref[:, real_lanes] = sum_r
            lam_acc_ref[:, imag_lanes] = sum_i
            scale_acc_ref[:, real_lanes] = sum_s
        back_lifted = low_ref[...].astype(bf16)
        back_lifted_ref[now, :] = back_lifted
        back_normed = dot_t(back_lifted, weight_ref[k]) + skip * mixed_ref[now, :].astype(f32)
        centered = (x_ref[now, :].astype(f32) - average) * root
        gain_sum += jnp.sum(back_normed * centered, axis=0, keepdims=True)
        shift_sum += jnp.sum(back_normed, axis=0, keepdims=True)
        if last:
            ahead_ref[now, :] = (back_ref[now, :].astype(f32) + (root * gain_ref[0:1, :]) * back_normed).astype(bf16)
        else:
            back_normed_ref[now, :] = back_normed.astype(bf16)
    lam_grad = jnp.sum(lam_acc_ref[...], axis=0, keepdims=True)
    scale_grad = jnp.sum(scale_acc_ref[...], axis=0, keepdims=True)
    acc_ref[0:1, :width] = gain_sum
    acc_ref[1:2, :width] = shift_sum
    if last:
        skip0_ref, bias0_ref, skip1_ref, bias1_ref, lam1_ref, scale1_ref = small_refs
        acc_ref[2:3, :width] = skip0_ref[...]
        acc_ref[3:4, :width] = skip1_ref[...]
        acc_ref[4:5, :width] = bias0_ref[:, :width]
        acc_ref[5:6, :width] = bias0_ref[:, width:]
        acc_ref[6:7, :width] = bias1_ref[:, :width]
        acc_ref[7:8, :width] = bias1_ref[:, width:]
        acc_ref[0:1, width:] = lam_grad[:, :states]
        acc_ref[1:2, width:] = lam_grad[:, states:]
        acc_ref[2:3, width:] = lam1_ref[:, :states]
        acc_ref[3:4, width:] = lam1_ref[:, states:]
        acc_ref[4:5, width:] = scale_grad
        acc_ref[5:6, width:] = scale1_ref[...]
        acc_ref[6:8, width:] = jnp.zeros((2, states), f32)
    else:
        lam_grad_ref[...] = lam_grad
        scale_grad_ref[...] = scale_grad
    for j in range(sums_ref.shape[0]):
        sums_ref[j] = acc_ref[...]


def lift_back(k, info, parts, arrays, away, devices):
    table = arrays[2].shape
    rows, states = arrays[3].shape
    width = arrays[4].shape[1]
    scratch = [pltpu.VMEM(table, f32), pltpu.VMEM((rows // BLOCKS, states), f32)]
    if k == 0:
        acc = (8, width + states // 2)
        outs = [near((rows, states), bf16), moved((devices,) + acc, f32), near((rows, width), bf16)]
    else:
        acc = (2, width)
        outs = [near((rows, states), bf16), moved((devices,) + acc, f32), near((rows, width), bf16)]
        outs += [near((1, states), f32), near((1, states // 2), f32)]
    scratch += [
        pltpu.VMEM(acc, f32),
        pltpu.VMEM((table[1], states), f32),
        pltpu.VMEM((table[1], states // 2), f32),
    ]
    if k == 0:
        scratch += staged([(a.shape, a.dtype) for a in away])
    return call(partial(lift_back_kernel, k), info, (parts,), arrays, away, outs, scratch, "lift_back")


def halves_kernel(parts, info_ref, *refs):
    pairs = (len(refs) - 2) // 2
    keep_ref, send_ref = refs[-2:]
    width = keep_ref.shape[1]
    even = info_ref[0] % 2 == 0
    products = [t_dot(refs[2 * n][...], refs[2 * n + 1][...]) for n in range(pairs)]
    first = 0
    for own, other in parts:
        (m, r, rows, c), (n, q, _, d) = own, other
        a = products[m][r : r + rows, c : c + width].astype(bf16)
        b = products[n][q : q + rows, d : d + width].astype(bf16)
        keep_ref[first : first + rows, :] = jnp.where(even, a, b)
        send_ref[first : first + rows, :] = jnp.where(even, b, a)
        first += rows


def halves(info, parts, arrays, rows, width, name):
    outs = [moved((rows, width), bf16)] * 2
    return call(partial(halves_kernel, parts), info, (), arrays, (), outs, [], name)


def split_kernel(shift, slot, info_ref, *refs):
    n = refs[0].shape[0]
    ins, outs = refs[: len(refs) - n], refs[len(refs) - n :]
    place = info_ref[slot] >> shift
    for m in range(n):
        total = ins[0][place ^ m].astype(f32)
        for ref in ins[1:]:
            total += ref[place ^ m].astype(f32)
        outs[m][...] = total.astype(outs[m].dtype)


def split(info, arrays, shift, slot):
    n = arrays[0].shape[0]
    shape = arrays[0].shape[1:]
    outs = [moved(shape, f32)] + [moved(shape, bf16)] * (n - 1)
    return call(partial(split_kernel, shift, slot), info, arrays, (), (), outs, [], "split")


def sum_kernel(info_ref, *refs):
    total = refs[0][...].astype(f32)
    for ref in refs[1:-1]:
        total += ref[...].astype(f32)
    refs[-1][...] = total.astype(bf16)


def join_kernel(shift, slot, info_ref, *refs):
    place = info_ref[slot] >> shift
    for m, ref in enumerate(refs[:-1]):
        refs[-1][place ^ m] = ref[...]


def join(info, arrays, shift, slot):
    outs = [moved((len(arrays),) + arrays[0].shape, bf16)]
    return call(partial(join_kernel, shift, slot), info, arrays, (), (), outs, [], "join")[0]


def trade(x, axis, mask):
    size = lax.axis_size(axis)
    return lax.ppermute(x, axis, [(i, i ^ mask) for i in range(size)])


def sum_along(info, own, sent, batches):
    arrays = [own] + [trade(x, "batch", m + 1) for m, x in enumerate(sent)]
    total = call(sum_kernel, info, arrays, (), (), [moved(own.shape, bf16)], [], "total")[0]
    return join(info, [total] + [trade(total, "batch", m) for m in range(1, batches)], 0, 1)


def all_sum(info, keep, send):
    rows, width = keep.shape
    chips, batches = lax.axis_size("seq") // 2, lax.axis_size("batch")
    shape = (chips, batches, rows // (chips * batches), width)
    own = split(info, [keep.reshape(shape), trade(send, "seq", 1).reshape(shape)], 1, 0)
    own = split(info, [own[0]] + [trade(x, "seq", 2 * m) for m, x in enumerate(own) if m], 0, 1)
    total = sum_along(info, own[0], own[1:], batches)
    total = join(info, [total] + [trade(total, "seq", 2 * m) for m in range(1, chips)], 1, 0).reshape(rows, width)
    return total, trade(total, "seq", 1)


def all_sum_slowly(info, keep, send):
    rows, width = keep.shape
    chips, batches = lax.axis_size("seq") // 2, lax.axis_size("batch")
    groups = [[2 * chip + core for chip in range(chips)] for core in range(2)]
    whole = call(sum_kernel, info, [keep, trade(send, "seq", 1)], (), (), [moved(keep.shape, bf16)], [], "total")[0]
    own = lax.psum_scatter(whole, "seq", axis_index_groups=groups, tiled=True)

    def finish(own, after):
        own, _ = lax.optimization_barrier((own, after))
        own = split(info, [own.reshape(batches, rows // (chips * batches), width)], 0, 1)
        total = sum_along(info, own[0], own[1:], batches).reshape(rows // chips, width)
        total = lax.all_gather(total, "seq", axis_index_groups=groups, tiled=True)
        return total, trade(total, "seq", 1)

    return partial(finish, own)


def results_kernel(k, parts, info_ref, *refs):
    pairs = len(parts)
    halves_refs = refs[: 2 * pairs]
    outs, wide_ref, sems = refs[-5:-2], refs[-2], refs[-1]
    even = info_ref[0] % 2 == 0
    width = wide_ref.shape[2]
    copies = []
    slot = 0
    for n, pieces in enumerate(parts):
        mine_ref, other_ref = halves_refs[2 * n : 2 * n + 2]
        first = 0
        for rows, low, high in pieces:
            mine = mine_ref[first : first + rows, :width].astype(f32)
            other = other_ref[first : first + rows, :width].astype(f32)
            for value, (out, row, column) in (
                (jnp.where(even, mine, other), low),
                (jnp.where(even, other, mine), high),
            ):
                wide_ref[slot, :rows, :] = value
                copy = pltpu.make_async_copy(
                    wide_ref.at[slot, pl.ds(0, rows), :],
                    outs[out].at[k, pl.ds(row, rows), pl.ds(column, width)],
                    sems.at[slot],
                )
                copy.start()
                copies.append(copy)
                slot += 1
            first += rows
    for copy in copies:
        copy.wait()


def results(k, info, parts, pairs, width, into):
    arrays = [half for pair in pairs for half in pair]
    slots = 2 * sum(len(p) for p in parts)
    shapes = [(2, width, 2 * width), (2, width, width), (2, width, width)]
    anywhere = pl.BlockSpec(memory_space=pl.ANY)
    into = list(into)
    return pl.pallas_call(
        partial(results_kernel, k, parts),
        in_specs=[in_smem] + [in_vmem] * len(arrays) + [anywhere] * len(into),
        out_specs=[anywhere] * 3,
        out_shape=[jax.ShapeDtypeStruct(shape, f32) for shape in shapes],
        scratch_shapes=[pltpu.VMEM((slots, width, width), f32), pltpu.SemaphoreType.DMA((slots,))],
        input_output_aliases={1 + len(arrays) + i: i for i in range(len(into))},
        compiler_params=pltpu.CompilerParams(vmem_limit_bytes=VMEM_LIMIT),
        name="results",
    )(info, *arrays, *into)


def leave_kernel(seqs, info_ref, rows_ref, out_ref, wide_ref):
    _, span, width = out_ref.shape
    wide_ref[...] = rows_ref[...].astype(f32).reshape(wide_ref.shape)
    shuffle = shuffle_matrix(span, True)
    for s in range(seqs):
        out_ref[s] = dot(shuffle, wide_ref[:, s].reshape(span, width).astype(bf16)).astype(bf16)


def leave(info, rows, seqs):
    span, width = rows.shape[0] // seqs, rows.shape[1]
    scratch = [pltpu.VMEM((span // CHUNKS, seqs, CHUNKS, width), f32)]
    outs = [moved((seqs, span, width), bf16)]
    return call(partial(leave_kernel, seqs), info, (rows,), (), (), outs, scratch, "leave")[0]


def input_grad_kernel(
    info_ref, sums_ref, tokens_ref, ahead_ref, stats_ref, gain_ref, count_ref, grad_ref, total_ref, wide_ref
):
    seqs, span, width = tokens_ref.shape
    where = Where(info_ref, seqs, span)
    wide_ref[...] = ahead_ref[...].astype(f32).reshape(wide_ref.shape)
    shuffle = shuffle_matrix(span, True)
    sums = jnp.sum(sums_ref[...], axis=0)
    total_ref[...] = sums
    average, root = stats_ref[0:1, :], stats_ref[1:2, :]
    factor = root * gain_ref[0:1, :] / count_ref[0:1, 0:1]
    by_gain = factor * sums[0:1, :width] * root
    fixed = factor * sums[1:2, :width] - by_gain * average
    step = lax.broadcasted_iota(jnp.int32, (span, 1), 0)
    for s in range(seqs):
        valid = (step < where.lefts[s]).astype(f32)
        ahead = dot(shuffle, wide_ref[:, s].reshape(span, width).astype(bf16))
        grad_ref[s] = (ahead - valid * (fixed + by_gain * tokens_ref[s].astype(f32))).astype(bf16)


def input_grads(info, sums, tokens, ahead, stats, gain, count):
    seqs, span, width = tokens.shape
    outs = [moved(tokens.shape, bf16), moved(sums.shape[1:], f32)]
    scratch = [pltpu.VMEM((span // CHUNKS, seqs, CHUNKS, width), f32)]
    return call(
        input_grad_kernel, info, (sums, tokens), (ahead, stats, gain, count), (), outs, scratch, "input_grad"
    )


def rotation_decay(decay_log, phase_log):
    decay_rate = jnp.exp(decay_log)
    magnitude = jnp.exp(-decay_rate)
    phase_angle = jnp.exp(phase_log)
    return (
        magnitude * jnp.cos(phase_angle),
        magnitude * jnp.sin(phase_angle),
        jnp.sqrt(1.0 - jnp.exp(-2.0 * decay_rate)),
    )


def to_all(x, axes):
    return lax.all_to_all(x, axes, split_axis=0, concat_axis=0, tiled=True)


def local(
    tokens,
    lengths,
    cotangent,
    norm_gain,
    norm_shift,
    lift_weight,
    decay_log,
    phase_log,
    skip_gain,
    mix_weight,
    glu_weight,
    glu_bias,
):
    both = ("seq", "batch")
    seq_devices = lax.axis_size("seq")
    devices = seq_devices * lax.axis_size("batch")
    seqs, span, width = tokens.shape
    rows = seqs * span
    states = decay_log.shape[1]
    info = jnp.concatenate(
        [jnp.stack([lax.axis_index("seq"), lax.axis_index("batch")]).astype(jnp.int32), lengths]
    )

    x0, sums = enter(info, tokens, devices)
    sums = to_all(sums, both)
    lam, scale, *tables = power_tables(info, decay_log, phase_log, seqs, seq_devices, span)

    power, leaps = tables[0:2]
    normed0, lifted0, ends, part, stats0, count = lift(
        0, seqs, seq_devices, info, sums, (x0, norm_gain, norm_shift, lift_weight, lam, scale, power)
    )
    weights = (mix_weight, skip_gain, glu_weight, glu_bias, lam, scale)
    x1, sums, state0, activated0, slope0, gate0, gate_slope0, low_x1 = mix(
        0, info, to_all(part, "seq"), (leaps, ends, power, lifted0, normed0, x0, *weights), devices
    )
    sums = to_all(sums, both)

    power, leaps = tables[4:6]
    normed1, lifted1, ends, part, stats1 = lift(
        1, seqs, seq_devices, info, sums, (count, x1, norm_gain, norm_shift, lift_weight, lam, scale, power)
    )
    state1, activated1, slope1, gate1, gate_slope1, masked = mix(
        1, info, to_all(part, "seq"), (leaps, ends, power, lifted1, normed1, x1, *weights), devices
    )

    power, leaps = tables[6:8]
    projected1, mixed1, dh, bias_grad1, skip_grad1, ends, part, back = glu_back(
        1, seqs, seq_devices, info, (),
        (cotangent, normed1, slope1, gate1, gate_slope1, glu_weight, mix_weight, lam, power), (),
    )
    back_lifted1, sums, back_normed, lam_grad1, scale_grad1 = lift_back(
        1, info, to_all(part, "seq"),
        (leaps, ends, power, dh, mixed1, stats1, lift_weight, skip_gain, lam, scale, lifted1, state1, x1), (), devices,
    )
    sums = to_all(sums, both)
    pieces = (((0, 0, width, 0), (1, 0, width, 0)), ((0, 0, width, width), (2, 0, width, 0)))
    keep, send = halves(
        info, pieces, (activated1, projected1, state1, mixed1, normed1, back_lifted1), 2 * width, width, "halves1"
    )
    finish1 = all_sum_slowly(info, keep, send)

    power, leaps = tables[2:4]
    projected0, mixed0, dh, bias_grad0, skip_grad0, ends, part, back, norm_sums1 = glu_back(
        0, seqs, seq_devices, info, (sums,),
        (back_normed, stats1, norm_gain, count, glu_weight, mix_weight, lam, power),
        (low_x1, back, normed0, slope0, gate0, gate_slope0),
    )
    small = (skip_grad0, bias_grad0, skip_grad1, bias_grad1, lam_grad1, scale_grad1)
    back_lifted0, sums, ahead = lift_back(
        0, info, to_all(part, "seq"),
        (leaps, ends, power, dh, mixed0, stats0, lift_weight, skip_gain, lam, scale, back, norm_gain, *small),
        (lifted0, state0, x0), devices,
    )
    sums = to_all(sums, both)
    half = width // 2
    pieces = (
        ((0, 0, width, 0), (0, 0, width, width)),
        ((1, 0, half, 0), (1, half, half, 0)),
        ((2, 0, half, 0), (2, half, half, 0)),
    )
    keep, send = halves(
        info, pieces, (activated0, projected0, state0, mixed0, normed0, back_lifted0), 2 * width, width, "halves0"
    )
    total0 = all_sum(info, keep, send)
    total1 = finish1(keep)
    input_grad, sums = input_grads(info, sums, tokens, ahead, stats0, norm_gain, count)
    produced = leave(info, masked, seqs)

    grads = results(1, info, (((width, (0, 0, 0), (1, 0, 0)), (width, (0, 0, width), (2, 0, 0))),), [total1], width, ())
    parts = ((width, (0, 0, 0), (0, 0, width)), (half, (1, 0, 0), (1, half, 0)), (half, (2, 0, 0), (2, half, 0)))
    grad_glu, grad_mix, grad_lift = results(0, info, (parts,), [total0], width, grads)

    inner, outer = sums[:, :width], sums[:, width:]
    lam_grad = outer[0:4].reshape(2, 2, states)
    grad_decay, grad_phase = jax.vjp(rotation_decay, decay_log, phase_log)[1](
        (lam_grad[:, 0], lam_grad[:, 1], outer[4:6])
    )
    return (
        produced,
        input_grad,
        jnp.stack([inner[0], norm_sums1[0]]),
        jnp.stack([inner[1], norm_sums1[1]]),
        grad_lift,
        grad_decay,
        grad_phase,
        inner[2:4],
        grad_mix,
        grad_glu,
        inner[4:8].reshape(2, 2 * width),
    )


def solution(mesh):
    split = P("batch", "seq", None)
    placed = (split, P("batch"), split) + (P(),) * 9
    return jax.shard_map(
        local,
        mesh=mesh,
        in_specs=placed,
        out_specs=(split, split) + (P(),) * 9,
        check_vma=False,
    )
```

```python
from functools import partial

import jax
import jax.numpy as jnp
from jax import lax
from jax.experimental import pallas as pl
from jax.experimental.pallas import tpu as pltpu
from jax.sharding import PartitionSpec as P

norm_eps = 1e-05
f32 = jnp.float32
bf16 = jnp.bfloat16

CHUNKS = 8
BLOCKS = 4
PARTS = 1
EXTRA = 16
LANES = 128
VMEM_LIMIT = 24 * 1024 * 1024

in_vmem = pl.BlockSpec(memory_space=pltpu.VMEM)
in_smem = pl.BlockSpec(memory_space=pltpu.SMEM)
in_hbm = pl.BlockSpec(memory_space=pltpu.HBM)


def near(shape, dtype):
    return in_vmem, pltpu.VMEM(shape, dtype)


def moved(shape, dtype):
    return in_vmem, jax.ShapeDtypeStruct(shape, dtype)


def copy_parts(source, target, sems):
    size = source.shape[0] // sems.shape[0]
    cuts = [pl.ds(i * size, size) for i in range(sems.shape[0])]
    return [pltpu.make_async_copy(source.at[cut], target.at[cut], sems.at[i]) for i, cut in enumerate(cuts)]


def begin(copies):
    for copy in copies:
        copy.start()


def finished(copies):
    for copy in copies:
        copy.wait()


class Outs(list):
    tick = None


def run(body, info, given, specs, outs, scratch, name, after, aliases=(), us=None):
    cost = None
    if us is not None:
        cost = pl.CostEstimate(flops=int(us * 1.1e9), bytes_accessed=int(us * 3e6), transcendentals=0)
    after = [pltpu.with_memory_space_constraint(t, pltpu.HBM) for t in after]
    n_in, n_out = 1 + len(given), len(outs)

    def ticking(*refs):
        body(*refs[:n_in], *refs[n_in + len(after) : n_in + len(after) + n_out], *refs[n_in + len(after) + n_out + 1 :])

    out = pl.pallas_call(
        ticking,
        in_specs=[in_smem] + specs + [in_hbm] * len(after),
        out_specs=[spec for spec, _ in outs] + [in_hbm],
        out_shape=[shape for _, shape in outs] + [pltpu.HBM((8, LANES), f32)],
        scratch_shapes=scratch,
        input_output_aliases=dict(aliases),
        compiler_params=pltpu.CompilerParams(vmem_limit_bytes=VMEM_LIMIT),
        cost_estimate=cost,
        name=name,
    )(info, *given, *after)
    result = Outs(out[:n_out])
    result.tick = out[n_out]
    return result


def here(x):
    return pltpu.with_memory_space_constraint(x, pltpu.VMEM)


def there(x):
    return pltpu.with_memory_space_constraint(x, pltpu.HBM)


def call(kernel, info, inputs, arrays, away, outs, scratch, name, after=(), fetch=(), spill=(), us=None):
    first = 1 + len(inputs) + len(arrays) + len(away)
    n_copies = len(fetch) + len(spill)
    fetched = [jax.eval_shape(lambda x, at=at: x if at is None else x[at], a) for a, at in fetch]
    outs = list(outs)
    n_outs = len(outs)
    outs += [near(a.shape, a.dtype) for a in fetched] + [(in_hbm, pltpu.HBM(a.shape, a.dtype)) for a in spill]

    def body(*refs):
        ins, rest = refs[: first + n_copies], refs[first + n_copies :]
        sources = list(ins[first:])
        for i, (_, at) in enumerate(fetch):
            if at is not None:
                sources[i] = sources[i].at[at]
        targets = rest[n_outs : n_outs + n_copies]
        rest = rest[:n_outs] + rest[n_outs + n_copies :]
        copies = []
        for i, (x, y) in enumerate(zip(sources, targets)):
            copies += copy_parts(x, y, rest[-1].at[i])
        begin(copies)
        kernel(*ins[:first], *(rest[:-1] if copies else rest))
        finished(copies)

    given = [*inputs, *map(here, arrays), *map(there, away), *(there(a) for a, _ in fetch), *map(here, spill)]
    specs = [in_vmem] * (len(inputs) + len(arrays)) + [in_hbm] * (len(away) + len(fetch)) + [in_vmem] * len(spill)
    scratch = list(scratch) + [pltpu.SemaphoreType.DMA((n_copies, PARTS))] * bool(n_copies)
    return run(body, info, given, specs, outs, scratch, name, after, us=us)


class Pack:
    def __init__(self, *fields):
        self.lanes, self.width = {}, 0
        for name, width in fields:
            self.lanes[name] = slice(self.width, self.width + width)
            self.width += width

    def views(self, ref, *names):
        return [ref.at[:, self.lanes[n]] for n in names]


def kept_pack(width, states):
    return Pack(*((n, width) for n in ("slope", "gate", "gate_slope", "activated")), ("state", states))


def glu_pack(width, states):
    return Pack(("projected", 2 * width), ("mixed", width), ("dh", states), ("back", width))


def lift_pack(width, states):
    return Pack(("lifted", states), ("back_normed", width), ("back", width), ("normed", width))


def wide(mask, width):
    return jnp.concatenate([mask] * (width // LANES), axis=1)


def dot(a, b):
    return lax.dot_general(a, b, (((1,), (0,)), ((), ())), preferred_element_type=f32)


def dot_t(a, b):
    return lax.dot_general(a, b, (((1,), (1,)), ((), ())), preferred_element_type=f32)


def t_dot(a, b):
    return lax.dot_general(a, b, (((0,), (0,)), ((), ())), preferred_element_type=f32)


def cmul(ar, ai, br, bi):
    return ar * br - ai * bi, ar * bi + ai * br


def order(steps, reverse):
    return range(steps - 1, -1, -1) if reverse else range(steps)


def shuffle_matrix(span, back):
    chunk = span // CHUNKS
    place = lax.broadcasted_iota(jnp.int32, (span, span), 0)
    source = lax.broadcasted_iota(jnp.int32, (span, span), 1)
    if back:
        wanted = (place % chunk) * CHUNKS + place // chunk
    else:
        wanted = (place % CHUNKS) * chunk + place // CHUNKS
    return (source == wanted).astype(f32).astype(bf16)


class Where:
    def __init__(self, info_ref, seqs, span):
        self.seq = lax.axis_index("seq")
        self.seqs, self.span = seqs, span
        self.lengths = [info_ref[s] for s in range(seqs)]
        self.lefts = [length - self.seq * span for length in self.lengths]

    def steps_left(self):
        before = (self.span // CHUNKS) * lax.broadcasted_iota(jnp.int32, (CHUNKS, LANES), 0)
        return jnp.concatenate([left - before for left in self.lefts], axis=0)


def valid_rows(left, first, steps):
    return jnp.concatenate([(left > first + t).astype(f32) for t in range(steps)], axis=0)


def shuffle_rows(wide_ref, source_ref):
    steps, seqs, chunks, width = wide_ref.shape
    shuffle = shuffle_matrix(steps * chunks, False)
    for s in range(seqs):
        wide_ref[:, s] = dot(shuffle, source_ref[s]).reshape(steps, chunks, width)


def enter_kernel(info_ref, tokens_ref, sums_ref, here_ref, acc_ref, sems):
    seqs, span, width = tokens_ref.shape
    copies = [copy_parts(tokens_ref.at[s], here_ref.at[s], sems.at[s]) for s in range(seqs)]
    for parts in copies:
        begin(parts)
    where = Where(info_ref, seqs, span)
    step = lax.broadcasted_iota(jnp.int32, (span, 1), 0)
    total = jnp.zeros((1, width), f32)
    squares = jnp.zeros((1, width), f32)
    count = jnp.zeros((1, 1), f32)
    for s in range(seqs):
        valid = (step < where.lefts[s]).astype(f32)
        finished(copies[s])
        x = here_ref[s].astype(f32)
        masked = x * valid
        total += jnp.sum(masked, axis=0, keepdims=True)
        squares += jnp.sum(masked * x, axis=0, keepdims=True)
        count += jnp.sum(valid, axis=0, keepdims=True)
    tail = jnp.broadcast_to(count, (1, LANES))
    acc_ref[0:1, :] = jnp.concatenate([total, tail], axis=1)
    acc_ref[1:2, :] = jnp.concatenate([squares, tail], axis=1)
    for j in range(sums_ref.shape[0]):
        sums_ref[j] = acc_ref[...]


def enter(info, tokens, devices, fetch):
    seqs, _, width = tokens.shape
    outs = [moved((devices, 2, width + LANES), f32), near(tokens.shape, bf16)]
    scratch = [pltpu.VMEM((2, width + LANES), f32), pltpu.SemaphoreType.DMA((seqs, 1))]
    return call(enter_kernel, info, (), (), (tokens,), outs, scratch, "enter", fetch=fetch)


class Powers:
    @staticmethod
    def scratch(seqs, seq_devices, states, leaps):
        tables = [((1, 2 * states), f32), ((1, states), f32), ((2 * states // LANES, seqs * CHUNKS, LANES), f32)]
        if leaps:
            tables.append(((seq_devices * seqs, 2 * states), f32))
        return [pltpu.VMEM(*t) for t in tables]

    def __init__(self, k, back, where, decay_ref, phase_ref, lam_ref, scale_ref, table_ref, leap_ref=None):
        states = scale_ref.shape[1]
        groups, group = states // LANES, table_ref.shape[1]
        seqs, span, limit = where.seqs, where.span, where.span // CHUNKS
        rate = jnp.exp(decay_ref[k : k + 1, :])
        size, angle = jnp.exp(-rate), jnp.exp(phase_ref[k : k + 1, :])
        lam_ref[:, :states] = size * jnp.cos(angle)
        lam_ref[:, states:] = size * jnp.sin(angle) * (-1.0 if back else 1.0)
        scale_ref[...] = jnp.sqrt(1.0 - jnp.exp(-2.0 * rate))
        self.lam, self.scale, self.table, self.leaps = lam_ref, scale_ref, table_ref, leap_ref
        shift = 0 if not back else (-1 if k == 0 else 1)
        chunk_count = jnp.clip(where.steps_left() + shift, 0, limit)
        if leap_ref is not None:
            total = leap_ref.shape[0]
            line = lax.broadcasted_iota(jnp.int32, (total, LANES), 0)
            span_left = jnp.zeros((total, LANES), jnp.int32)
            for s, length in enumerate(where.lengths):
                span_left = jnp.where(line % seqs == s, length - span * (line // seqs), span_left)
            span_count = jnp.clip(span_left + shift, 0, span)
        for low in range(groups):
            real_lanes = slice(low * LANES, (low + 1) * LANES)
            imag_lanes = slice((groups + low) * LANES, (groups + low + 1) * LANES)
            br, bi = lam_ref[:, real_lanes], lam_ref[:, imag_lanes]
            cr = jnp.ones((group, LANES), f32)
            ci = jnp.zeros((group, LANES), f32)
            if leap_ref is not None:
                pr = jnp.ones((total, LANES), f32)
                pi = jnp.zeros((total, LANES), f32)
            for bit in range((limit if leap_ref is None else span).bit_length()):
                if (1 << bit) <= limit:
                    nr, ni = cmul(cr, ci, br, bi)
                    odd = (chunk_count & (1 << bit)) != 0
                    cr, ci = jnp.where(odd, nr, cr), jnp.where(odd, ni, ci)
                if leap_ref is not None:
                    nr, ni = cmul(pr, pi, br, bi)
                    odd = (span_count & (1 << bit)) != 0
                    pr, pi = jnp.where(odd, nr, pr), jnp.where(odd, ni, pi)
                br, bi = cmul(br, bi, br, bi)
            table_ref[low] = cr
            table_ref[groups + low] = ci
            if leap_ref is not None:
                leap_ref[:, real_lanes] = pr
                leap_ref[:, imag_lanes] = pi


def stretch_part(ends_ref, power_ref, reverse, seqs):
    groups = ends_ref.shape[0] // 2
    reals, imags = [], []
    for low in range(groups):
        real = jnp.zeros((seqs, LANES), f32)
        imag = jnp.zeros((seqs, LANES), f32)
        for c in order(CHUNKS, reverse):
            here = pl.ds(c, seqs, stride=CHUNKS)
            real, imag = cmul(power_ref[low, here, :], power_ref[groups + low, here, :], real, imag)
            real += ends_ref[low, here, :]
            imag += ends_ref[groups + low, here, :]
        reals.append(real)
        imags.append(imag)
    return jnp.concatenate(reals + imags, axis=1)


def chunk_starts(start_ref, place, parts_ref, leaps_ref, ends_ref, power_ref, reverse):
    devices, seqs, width = parts_ref.shape
    states = width // 2
    groups = states // LANES
    real = jnp.zeros((seqs, states), f32)
    imag = jnp.zeros((seqs, states), f32)
    for j in order(devices, reverse):
        ahead = (j > place) if reverse else (j < place)
        leap, part = leaps_ref[seqs * j : seqs * (j + 1), :], parts_ref[j]
        next_real, next_imag = cmul(leap[:, :states], leap[:, states:], real, imag)
        real = jnp.where(ahead, next_real + part[:, :states], real)
        imag = jnp.where(ahead, next_imag + part[:, states:], imag)
    for low in range(groups):
        hr = real[:, low * LANES : (low + 1) * LANES]
        hi = imag[:, low * LANES : (low + 1) * LANES]
        for c in order(CHUNKS, reverse):
            here = pl.ds(c, seqs, stride=CHUNKS)
            start_ref[low, here, :] = hr
            start_ref[groups + low, here, :] = hi
            hr, hi = cmul(power_ref[low, here, :], power_ref[groups + low, here, :], hr, hi)
            hr += ends_ref[low, here, :]
            hi += ends_ref[groups + low, here, :]


def scan_block(h_ref, drive, left, lam, shift, first, steps, reverse, out_ref=None):
    groups, group, _ = h_ref.shape
    groups = groups // 2
    masks = [left > first + t + shift for t in range(steps)]
    for low in range(groups):
        real_lanes = slice(low * LANES, (low + 1) * LANES)
        imag_lanes = slice((groups + low) * LANES, (groups + low + 1) * LANES)
        hr, hi = h_ref[low], h_ref[groups + low]
        lr, li = lam[:, real_lanes], lam[:, imag_lanes]
        for t in order(steps, reverse):
            ur, ui = drive(t, real_lanes, imag_lanes)
            nr, ni = cmul(lr, li, hr, hi)
            hr = jnp.where(masks[t], nr, hr) + ur
            hi = jnp.where(masks[t], ni, hi) + ui
            if out_ref is not None:
                out_ref[t * group : (t + 1) * group, real_lanes] = hr
                out_ref[t * group : (t + 1) * group, imag_lanes] = hi
        h_ref[low] = hr
        h_ref[groups + low] = hi


def input_drive(lifted, scale, left, first, steps):
    group = left.shape[0]
    masks = [left > first + t for t in range(steps)]

    def drive(t, real_lanes, imag_lanes):
        here = slice(t * group, (t + 1) * group)
        factor = jnp.where(masks[t], scale[:, real_lanes], 0.0)
        return factor * lifted[here, real_lanes], factor * lifted[here, imag_lanes]

    return drive


def blocks_of(rows, group, reverse):
    size = rows // BLOCKS
    for block in order(BLOCKS, reverse):
        yield block, block * (size // group), slice(block * size, (block + 1) * size)


def lift_kernel(k, seqs, info_ref, sums_ref, gain_ref, shift_ref, decay_ref, phase_ref, *refs):
    reverse = k == 1
    if k == 0:
        x_ref, weight_ref, normed_ref, lifted_ref, ends_ref, part_ref, stats_ref, rows_ref, wide_ref = refs[:9]
        refs = refs[9:]
    else:
        count_ref, x_ref, weight_ref, normed_ref, lifted_ref, ends_ref, part_ref, stats_ref = refs[:8]
        refs = refs[8:]
    rows, width = normed_ref.shape
    group = ends_ref.shape[1]
    size = rows // BLOCKS
    steps = size // group
    where = Where(info_ref, seqs, rows // seqs)
    powers = Powers(k, False, where, decay_ref, phase_ref, *refs)
    if k == 0:
        shuffle_rows(wide_ref, x_ref)
    sums = jnp.sum(sums_ref[...], axis=0)
    if k == 0:
        count = sums[0:1, width : width + 1]
    else:
        count = count_ref[2:3, 0:1]
    average = sums[0:1, :width] / count
    root = lax.rsqrt(sums[1:2, :width] / count - average * average + norm_eps)
    stats_ref[0:1, :] = average
    stats_ref[1:2, :] = root
    stats_ref[2:3, :] = jnp.broadcast_to(count, (1, width))
    gain, shift = gain_ref[k : k + 1, :], shift_ref[k : k + 1, :]
    lam, scale = powers.lam[...], powers.scale[...]
    left = where.steps_left()
    ends_ref[...] = jnp.zeros_like(ends_ref)
    for _, first, now in blocks_of(rows, group, reverse):
        if k == 0:
            x = wide_ref[first : first + steps].reshape(size, width)
            rows_ref[now, :] = x.astype(bf16)
        else:
            x = x_ref[now, :]
        normed = ((x - average) * root * gain + shift).astype(bf16)
        normed_ref[now, :] = normed
        lifted = dot(normed, weight_ref[...]).astype(bf16)
        lifted_ref[now, :] = lifted
        drive = input_drive(lifted.astype(f32), scale, left, first, steps)
        scan_block(ends_ref, drive, left, lam, 0, first, steps, reverse)
    part = stretch_part(ends_ref, powers.table, reverse, seqs)
    for j in range(part_ref.shape[0]):
        part_ref[j] = part


def lift(k, seqs, seq_devices, info, inputs, arrays, rows, fetch):
    gain, decay = inputs[1], inputs[3]
    width, states = gain.shape[1], decay.shape[1]
    outs = [
        near((rows, width), bf16),
        near((rows, 2 * states), bf16),
        near((2 * states // LANES, seqs * CHUNKS, LANES), f32),
        moved((seq_devices, seqs, 2 * states), f32),
        moved((8, width), f32),
    ]
    scratch = []
    if k == 0:
        outs.append(near((rows, width), bf16))
        scratch.append(pltpu.VMEM((rows // seqs // CHUNKS, seqs, CHUNKS, width), f32))
    scratch += Powers.scratch(seqs, seq_devices, states, False)
    return call(partial(lift_kernel, k, seqs), info, inputs, arrays, (), outs, scratch, "lift", fetch=fetch)


def mix_kernel(k, info_ref, parts_ref, skip_ref, bias_ref, decay_ref, phase_ref, *refs):
    reverse = k == 1
    (ends_ref, lifted_ref, normed_ref, x_ref, mix_ref, glu_ref) = refs[:6]
    tables, refs = refs[-4:], refs[6:-4]
    if reverse:
        state_ref, activated_ref, slope_ref, gate_ref, gate_slope_ref, masked_ref, h_ref, states_ref = refs
    else:
        next_ref, sums_ref, kept_out, h_ref, states_ref, acc_ref, kept_ref, sems = refs
        pack = kept_pack(x_ref.shape[1], lifted_ref.shape[1])
        state_ref, activated_ref, slope_ref, gate_ref, gate_slope_ref = pack.views(
            kept_ref, "state", "activated", "slope", "gate", "gate_slope"
        )
        copies = []
    seqs = parts_ref.shape[1]
    rows, width = x_ref.shape
    group = ends_ref.shape[1]
    steps = rows // BLOCKS // group
    where = Where(info_ref, seqs, rows // seqs)
    powers = Powers(k, False, where, decay_ref, phase_ref, *tables)
    chunk_starts(h_ref, where.seq, parts_ref, powers.leaps, ends_ref, powers.table, reverse)
    left = where.steps_left()
    skip, bias = skip_ref[k : k + 1, :], bias_ref[k : k + 1, :]
    lam, scale = powers.lam[...], powers.scale[...]
    total = jnp.zeros((1, width), f32)
    squares = jnp.zeros((1, width), f32)
    for block, first, now in blocks_of(rows, group, reverse):
        drive = input_drive(lifted_ref[now, :].astype(f32), scale, left, first, steps)
        scan_block(h_ref, drive, left, lam, 0, first, steps, reverse, states_ref)
        state = states_ref[...].astype(bf16)
        state_ref[now, :] = state
        mixed = dot(state, mix_ref[...]) + skip * normed_ref[now, :].astype(f32)
        base, cube = 0.7978845608028654, 0.044715
        square = mixed * mixed
        bend = jnp.tanh(mixed * (base + (base * cube) * square))
        half = 0.5 + 0.5 * bend
        activated = (mixed * half).astype(bf16)
        activated_ref[now, :] = activated
        slope_ref[now, :] = (
            half + mixed * (half - half * half) * (2.0 * base + (6.0 * base * cube) * square)
        ).astype(bf16)
        projected = dot(activated, glu_ref[...]) + bias
        gate = 0.5 + 0.5 * jnp.tanh(0.5 * projected[:, width:])
        gated = projected[:, :width] * gate
        gate_ref[now, :] = gate.astype(bf16)
        gate_slope_ref[now, :] = (gated - gated * gate).astype(bf16)
        after = x_ref[now, :].astype(f32) + gated
        masked = after * wide(valid_rows(left, first, steps), width)
        if reverse:
            masked_ref[now, :] = masked.astype(bf16)
        else:
            next_ref[now, :] = after
            total += jnp.sum(masked, axis=0, keepdims=True)
            squares += jnp.sum(masked * after, axis=0, keepdims=True)
            parts = copy_parts(kept_ref.at[now, :], kept_out.at[now, :], sems.at[block])
            begin(parts)
            copies += parts
    if not reverse:
        acc_ref[0:1, :] = total
        acc_ref[1:2, :] = squares
        for j in range(sums_ref.shape[0]):
            sums_ref[j] = acc_ref[...]
        finished(copies)


def mix(k, info, inputs, arrays, devices, fetch, spill=()):
    parts = inputs[0]
    ends, lifted, _, x = arrays[:4]
    rows, width = x.shape
    states = lifted.shape[1]
    seq_devices, seqs, _ = parts.shape
    scratch = [pltpu.VMEM(ends.shape, f32), pltpu.VMEM((rows // BLOCKS, states), f32)]
    if k == 1:
        outs = [near((rows, states), bf16)] + [near((rows, width), bf16)] * 5
    else:
        kept = (rows, kept_pack(width, states).width)
        outs = [near((rows, width), f32), moved((devices, 2, width), f32), (in_hbm, pltpu.HBM(kept, bf16))]
        scratch += [pltpu.VMEM((2, width), f32), pltpu.VMEM(kept, bf16), pltpu.SemaphoreType.DMA((BLOCKS, 1))]
    scratch += Powers.scratch(seqs, seq_devices, states // 2, True)
    return call(
        partial(mix_kernel, k), info, inputs, arrays, (), outs, scratch, "mix", fetch=fetch, spill=spill
    )


def glu_back_kernel(k, seqs, info_ref, decay_ref, phase_ref, *refs):
    reverse = k == 0
    if k == 0:
        sums_ref, stats_ref, gain_ref, shift_ref, lift_pack_ref, kept_ref, normed_in, glu_in, mix_in = refs[:9]
        tables, refs = refs[-3:], refs[9:-3]
    else:
        start_ref, normed_ref, slope_ref, gate_ref, gate_slope_ref, glu_ref, mix_ref = refs[:7]
        tables, refs = refs[-3:], refs[7:-3]
    out_ref, bias_grad_ref, skip_grad_ref, ends_ref, part_ref = refs[:5]
    refs = refs[5:]
    rows, width = out_ref.shape[0], skip_grad_ref.shape[1]
    states = 2 * decay_ref.shape[1]
    names = ("projected", "mixed", "dh", "back")
    projected_ref, mixed_ref, dh_ref, back_ref = glu_pack(width, states).views(out_ref, *names)
    if k == 0:
        total_ref, normed_ref, slopes_ref, glu_ref, mix_ref, sems, weight_sems = refs
        pack = kept_pack(width, states)
        back_normed_ref, start_ref, later_ref = lift_pack(width, states).views(
            lift_pack_ref, "back_normed", "back", "normed"
        )
        slope_ref, gate_ref, gate_slope_ref = pack.views(slopes_ref, "slope", "gate", "gate_slope")
    group = ends_ref.shape[1]
    size = rows // BLOCKS
    steps = size // group
    where = Where(info_ref, seqs, rows // seqs)
    if k == 1:
        (wide_ref,) = refs
        shuffle_rows(wide_ref, start_ref)
    else:
        copies = {}
        for block, _, now in blocks_of(rows, group, reverse):
            lanes = slice(0, 3 * width)
            copies[block] = copy_parts(kept_ref.at[now, lanes], slopes_ref.at[now, :], sems.at[0, block])
            copies[block] += copy_parts(normed_in.at[now, :], normed_ref.at[now, :], sems.at[1, block])
        weights = copy_parts(glu_in.at[k], glu_ref, weight_sems.at[0])
        weights += copy_parts(mix_in.at[k], mix_ref, weight_sems.at[1])
        for n, block in enumerate(order(BLOCKS, reverse)):
            begin(copies[block])
            if n == 0:
                begin(weights)
        sums = jnp.sum(sums_ref[...], axis=0)
        total_ref[...] = sums
        root, count = stats_ref[1:2, :], stats_ref[2:3, 0:1]
        gain, shift = gain_ref[1:2, :], shift_ref[1:2, :]
        by_normed = sums[0:1] / count
        fixed = (gain * sums[1:2] - shift * sums[0:1]) / count
    powers = Powers(k, True, where, decay_ref, phase_ref, *tables)
    left = where.steps_left()
    lam = powers.lam[...]
    ends_ref[...] = jnp.zeros_like(ends_ref)
    bias_grad = jnp.zeros((1, 2 * width), f32)
    skip_grad = jnp.zeros((1, width), f32)
    for block, first, now in blocks_of(rows, group, reverse):
        valid = wide(valid_rows(left, first, steps), width)
        if k == 1:
            back = wide_ref[first : first + steps].reshape(size, width) * valid
        else:
            finished(copies[block])
            back = start_ref[now, :].astype(f32) + root * (
                gain * back_normed_ref[now, :].astype(f32)
                - valid * (fixed + by_normed * later_ref[now, :].astype(f32))
            )
        back_ref[now, :] = back.astype(bf16)
        value_back = (back * gate_ref[now, :].astype(f32)).astype(bf16)
        gate_back = (back * gate_slope_ref[now, :].astype(f32)).astype(bf16)
        back_projected = jnp.concatenate([value_back, gate_back], axis=1)
        projected_ref[now, :] = back_projected
        bias_grad += jnp.sum(back_projected.astype(f32), axis=0, keepdims=True)
        if k == 0 and block == BLOCKS - 1:
            finished(weights)
        back_activated = dot_t(back_projected, glu_ref[...])
        back_mixed = (slope_ref[now, :].astype(f32) * back_activated).astype(bf16)
        mixed_ref[now, :] = back_mixed
        skip_grad += jnp.sum(back_mixed.astype(f32) * normed_ref[now, :].astype(f32), axis=0, keepdims=True)
        back_state = dot_t(back_mixed, mix_ref[...]).astype(bf16)
        dh_ref[now, :] = back_state
        wide_state = back_state.astype(f32)

        def drive(t, real_lanes, imag_lanes):
            at = slice(t * group, (t + 1) * group)
            return wide_state[at, real_lanes], wide_state[at, imag_lanes]

        shift = 1 if reverse else -1
        scan_block(ends_ref, drive, left, lam, shift, first, steps, reverse)
    bias_grad_ref[...] = bias_grad
    skip_grad_ref[...] = skip_grad
    part = stretch_part(ends_ref, powers.table, reverse, seqs)
    for j in range(part_ref.shape[0]):
        part_ref[j] = part


def glu_back(k, seqs, seq_devices, info, inputs, arrays, away, rows, width, after, fetch, spill=()):
    states = inputs[0].shape[1]
    outs = [
        near((rows, glu_pack(width, 2 * states).width), bf16),
        moved((1, 2 * width), f32),
        moved((1, width), f32),
        near((2 * states // LANES, seqs * CHUNKS, LANES), f32),
        moved((seq_devices, seqs, 2 * states), f32),
    ]
    if k == 1:
        scratch = [pltpu.VMEM((rows // seqs // CHUNKS, seqs, CHUNKS, width), f32)]
    else:
        outs += [moved((2, width), f32), near((rows, width), bf16)]
        scratch = [
            pltpu.VMEM((rows, 3 * width), bf16),
            pltpu.VMEM((width, 2 * width), bf16),
            pltpu.VMEM((2 * states, width), bf16),
            pltpu.SemaphoreType.DMA((2, BLOCKS, 1)),
            pltpu.SemaphoreType.DMA((2, 1)),
        ]
    scratch += Powers.scratch(seqs, seq_devices, states, False)
    return call(
        partial(glu_back_kernel, k, seqs), info, inputs, arrays, away, outs, scratch, "glu_back", after, fetch, spill
    )


def lift_back_kernel(
    k, info_ref, parts_ref, stats_ref, skip_ref, decay_ref, phase_ref, gain_ref, shift_ref, *refs
):
    reverse = last = k == 0
    if last:
        small_refs, refs = refs[:2], refs[2:]
    ends_ref, glu_pack_ref = refs[:2]
    states, width = 2 * decay_ref.shape[1], stats_ref.shape[1]
    mixed_ref, dh_ref, back_ref = glu_pack(width, states).views(glu_pack_ref, "mixed", "dh", "back")
    normed_ref, state_ref, weight_ref = refs[2:5]
    tables, refs = refs[-4:], refs[5:-4]
    if last:
        back_lifted_ref, sums_ref, ahead_ref = refs[:3]
        refs = refs[3:]
    else:
        out_ref, sums_ref, lam_grad_ref, scale_grad_ref = refs[:4]
        back_lifted_ref, back_normed_ref, kept_back_ref, kept_normed_ref = lift_pack(width, states).views(
            out_ref, "lifted", "back_normed", "back", "normed"
        )
        kept_back_ref[...] = back_ref[...]
        kept_normed_ref[...] = normed_ref[...]
        refs = refs[4:]
    h_ref, low_ref, acc_ref, lam_acc_ref, scale_acc_ref = refs
    rows, width = normed_ref.shape
    group = ends_ref.shape[1]
    seqs = parts_ref.shape[1]
    steps = rows // BLOCKS // group
    states = decay_ref.shape[1]
    where = Where(info_ref, seqs, rows // seqs)
    powers = Powers(k, True, where, decay_ref, phase_ref, *tables)
    chunk_starts(h_ref, where.seq, parts_ref, powers.leaps, ends_ref, powers.table, reverse)
    lam_acc_ref[...] = jnp.zeros_like(lam_acc_ref)
    scale_acc_ref[...] = jnp.zeros_like(scale_acc_ref)
    left = where.steps_left()
    lam, scale = powers.lam[...], powers.scale[...]
    root, gain, shift_row = stats_ref[1:2, :], gain_ref[k : k + 1, :], shift_ref[k : k + 1, :]
    skip = skip_ref[k : k + 1, :]
    gain_sum = jnp.zeros((1, width), f32)
    shift_sum = jnp.zeros((1, width), f32)
    shift = 1 if reverse else -1
    for _, first, now in blocks_of(rows, group, reverse):
        moving = [left > first + t + shift for t in range(steps)]
        valid = [left > first + t for t in range(steps)]
        dh = dh_ref[now, :].astype(f32)
        normed = normed_ref[now, :]
        lifted = dot(normed, weight_ref[...]).astype(bf16).astype(f32)
        state = state_ref[now, :].astype(f32)
        for low in range(0, states, LANES):
            real_lanes = slice(low, low + LANES)
            imag_lanes = slice(states + low, states + low + LANES)
            gr, gi = h_ref[low // LANES], h_ref[(states + low) // LANES]
            lr, li = lam[:, real_lanes], lam[:, imag_lanes]
            part = scale[:, real_lanes]
            sum_r, sum_i = lam_acc_ref[:, real_lanes], lam_acc_ref[:, imag_lanes]
            sum_s = scale_acc_ref[:, real_lanes]
            for t in order(steps, reverse):
                at = slice(t * group, (t + 1) * group)
                hr, hi = state[at, real_lanes], state[at, imag_lanes]
                ur, ui = lifted[at, real_lanes], lifted[at, imag_lanes]
                mr, mi = jnp.where(moving[t], gr, 0.0), jnp.where(moving[t], gi, 0.0)
                sum_r += mr * hr + mi * hi
                sum_i += mi * hr - mr * hi
                nr, ni = cmul(lr, li, gr, gi)
                gr = jnp.where(moving[t], nr, gr) + dh[at, real_lanes]
                gi = jnp.where(moving[t], ni, gi) + dh[at, imag_lanes]
                vr, vi = jnp.where(valid[t], gr, 0.0), jnp.where(valid[t], gi, 0.0)
                sum_s += vr * ur + vi * ui
                low_ref[at, real_lanes] = part * vr
                low_ref[at, imag_lanes] = part * vi
            h_ref[low // LANES] = gr
            h_ref[(states + low) // LANES] = gi
            lam_acc_ref[:, real_lanes] = sum_r
            lam_acc_ref[:, imag_lanes] = sum_i
            scale_acc_ref[:, real_lanes] = sum_s
        back_lifted = low_ref[...].astype(bf16)
        back_lifted_ref[now, :] = back_lifted
        back_normed = dot_t(back_lifted, weight_ref[...]) + skip * mixed_ref[now, :].astype(f32)
        gain_sum += jnp.sum(back_normed * normed.astype(f32), axis=0, keepdims=True)
        shift_sum += jnp.sum(back_normed, axis=0, keepdims=True)
        if last:
            ahead_ref[now, :] = (back_ref[now, :].astype(f32) + (root * gain) * back_normed).astype(bf16)
        else:
            back_normed_ref[now, :] = back_normed.astype(bf16)
    lam_grad = jnp.sum(lam_acc_ref[...], axis=0, keepdims=True)
    scale_grad = jnp.sum(scale_acc_ref[...], axis=0, keepdims=True)
    acc_ref[0:1, :] = (gain_sum - shift_row * shift_sum) / gain
    acc_ref[1:2, :] = shift_sum
    devices = sums_ref.shape[0]
    if last:
        skip_grad_ref, bias_grad_ref = small_refs
        acc_ref[2:3, :] = skip_grad_ref[...]
        acc_ref[3:4, :] = bias_grad_ref[:, :width]
        acc_ref[4:5, :] = bias_grad_ref[:, width:]
        acc_ref[5:6, :states] = lam_grad[:, :states]
        acc_ref[5:6, states : 2 * states] = lam_grad[:, states:]
        acc_ref[6:7, :states] = scale_grad
        acc_ref[6:7, states:] = jnp.zeros((1, width - states), f32)
        acc_ref[7:8, :] = jnp.zeros((1, width), f32)
    else:
        lam_grad_ref[...] = lam_grad
        scale_grad_ref[...] = scale_grad
    for j in range(devices):
        sums_ref[j] = acc_ref[...]


def lift_back(k, info, inputs, arrays, devices, after=(), fetch=()):
    parts, stats, decay = inputs[0], inputs[1], inputs[3]
    ends, packed = arrays[:2]
    rows, width, states = packed.shape[0], stats.shape[1], 2 * decay.shape[1]
    seq_devices, seqs, _ = parts.shape
    table = ends.shape
    acc = (8, width) if k == 0 else (2, width)
    if k == 0:
        outs = [near((rows, states), bf16), moved((devices,) + acc, f32), moved((rows, width), bf16)]
    else:
        outs = [near((rows, lift_pack(width, states).width), bf16), moved((devices, 2, width), f32)]
        outs += [moved((1, states), f32), moved((1, states // 2), f32)]
    scratch = [
        pltpu.VMEM(table, f32),
        pltpu.VMEM((rows // BLOCKS, states), f32),
        pltpu.VMEM(acc, f32),
        pltpu.VMEM((table[1], states), f32),
        pltpu.VMEM((table[1], states // 2), f32),
    ]
    scratch += Powers.scratch(seqs, seq_devices, states // 2, True)
    return call(partial(lift_back_kernel, k), info, inputs, arrays, (), outs, scratch, "lift_back", after, fetch)


def halves_kernel(parts, pairs, small, info_ref, *refs):
    keep_ref, send_ref = refs[-2:]
    width = keep_ref.shape[1]
    even = lax.axis_index("seq") % 2 == 0
    if small:
        small_refs, refs = refs[:4], refs[4:]
    products = [t_dot(*(refs[n][:, lanes] for n, lanes in pair)) for pair in pairs]
    first = 0
    for n, rows, (r, c), (q, d) in parts:
        a = products[n][r : r + rows, c : c + width].astype(bf16)
        b = products[n][q : q + rows, d : d + width].astype(bf16)
        keep_ref[first : first + rows, :] = jnp.where(even, a, b)
        send_ref[first : first + rows, :] = jnp.where(even, b, a)
        first += rows
    if small:
        skip_ref, bias_ref, lam_ref, scale_ref = small_refs
        extra = keep_ref.shape[0] - first
        low = jnp.concatenate([skip_ref[...], bias_ref[:, :width], bias_ref[:, width:]], axis=0)
        scale = jnp.concatenate([scale_ref[...], jnp.zeros((1, width - scale_ref.shape[1]), f32)], axis=1)
        high = jnp.concatenate([lam_ref[...], scale, jnp.zeros((1, width), f32)], axis=0)
        low, high = (jnp.concatenate([x, jnp.zeros((extra - 3, width), f32)], axis=0).astype(bf16) for x in (low, high))
        keep_ref[first:, :] = jnp.where(even, low, high)
        send_ref[first:, :] = jnp.where(even, high, low)


def halves(info, parts, pairs, small, arrays, width, name, after=()):
    rows = sum(p[1] for p in parts)
    if small:
        rows += EXTRA * (lax.axis_size("seq") // 2)
    outs = [moved((rows, width), bf16)] * 2
    return call(partial(halves_kernel, parts, pairs, bool(small)), info, small, arrays, (), outs, [], name, after)


def place_of(axis):
    return lax.axis_index("batch") if axis == "batch" else lax.axis_index("seq") // 2


def total_of(refs, rows):
    total = refs[0][rows, :].astype(f32)
    for ref in refs[1:]:
        total += ref[rows, :].astype(f32)
    return total


def split_kernel(chips, sets, xor, info_ref, *refs):
    n_in = 2 * len(sets)
    outs = refs[n_in:]
    place = place_of("seq")
    for m in range(chips):
        chip = place ^ m if xor else m
        low = 0
        for n, parts in enumerate(sets):
            first = 0
            for rows in parts:
                share = rows // chips
                start = first + chip * share
                if xor:
                    start = pl.multiple_of(start, 16)
                total = total_of(refs[2 * n : 2 * n + 2], pl.ds(start, share))
                if xor:
                    outs[m][low : low + share, :] = total.astype(outs[m].dtype)
                else:
                    base = m * (outs[0].shape[0] // chips) + low
                    outs[0][base : base + share, :] = total.astype(outs[0].dtype)
                first, low = first + rows, low + share


def split(info, sets, arrays, xor, after=()):
    chips = lax.axis_size("seq") // 2
    width = arrays[0].shape[1]
    rows = sum(map(sum, sets))
    outs = [moved((rows, width), bf16)]
    if xor:
        outs = [moved((rows // chips, width), f32)] + [moved((rows // chips, width), bf16)] * (chips - 1)
    return call(partial(split_kernel, chips, sets, xor), info, arrays, (), (), outs, [], "split", after, us=0.8)


def cut_kernel(extra, info_ref, *refs):
    low_ref, refs = refs[-1], refs[:-1]
    batches, share, width = low_ref.shape
    arrays, outs = refs[:-batches], refs[-batches:]
    place = place_of("batch")
    rows = batches * share
    low_ref[...] = total_of(arrays, slice(0, rows)).reshape(batches, share, width)
    under = total_of(arrays, slice(rows, rows + extra)) if extra else None
    for m in range(batches):
        outs[m][:share, :] = low_ref[place ^ m].astype(outs[m].dtype)
        if extra:
            outs[m][share:, :] = under.astype(outs[m].dtype)


def cut(info, arrays, extra, after=()):
    batches = lax.axis_size("batch")
    rows, width = arrays[0].shape
    share = (rows - extra) // batches
    outs = [moved((share + extra, width), f32)] + [moved((share + extra, width), bf16)] * (batches - 1)
    scratch = [pltpu.VMEM((batches, share, width), f32)]
    return call(partial(cut_kernel, extra), info, arrays, (), (), outs, scratch, "cut", after, us=1.2)


def sum_kernel(info_ref, *refs):
    total = refs[0][...].astype(f32)
    for ref in refs[1:-1]:
        total += ref[...].astype(f32)
    refs[-1][...] = total.astype(bf16)


def sum_of(info, arrays, after=()):
    return call(sum_kernel, info, arrays, (), (), [moved(arrays[0].shape, bf16)], [], "total", after, us=0.6)


def join_kernel(info_ref, *refs):
    pieces, out_ref, low_ref = refs[:-2], refs[-2], refs[-1]
    batches, share, width = low_ref.shape
    place = place_of("batch")
    for m, ref in enumerate(pieces):
        low_ref[place ^ m] = ref[:share, :].astype(f32)
    rows = batches * share
    out_ref[:rows, :] = low_ref[...].reshape(rows, width).astype(bf16)
    if out_ref.shape[0] > rows:
        out_ref[rows:, :] = pieces[0][share:, :]


def join(info, arrays, extra, after=()):
    batches = len(arrays)
    rows, width = arrays[0].shape
    share = rows - extra
    outs = [moved((batches * share + extra, width), bf16)]
    scratch = [pltpu.VMEM((batches, share, width), f32)]
    return call(join_kernel, info, arrays, (), (), outs, scratch, "join", after, us=0.6)


def trade(x, axis, mask):
    size = lax.axis_size(axis)
    return lax.ppermute(x, axis, [(i, i ^ mask) for i in range(size)])


def sent(arrays, axis, masks):
    return [arrays[0]] + [trade(x, axis, m) for x, m in zip(arrays[1:], masks)]


def to_others(x, axis, masks):
    return [x] + [trade(x, axis, m) for m in masks]


def gate_kernel(*refs):
    pass


def gate(info, arrays, after):
    outs = [(in_hbm, pltpu.HBM(x.shape, x.dtype)) for x in arrays]
    aliases = {1 + i: i for i in range(len(arrays))}
    return run(gate_kernel, info, list(map(there, arrays)), [in_hbm] * len(arrays), outs, [], "gate", after, aliases, 0.5)


def small_grads(sums, norm1, low, high, decay_log, phase_log, refs):
    gain_ref, shift_ref, decay_grad_ref, phase_grad_ref, skip_grad_ref, bias_grad_ref = refs
    blocks, states = decay_log.shape
    width = sums.shape[1]
    rows = (
        [sums[n : n + 1] for n in range(2, 7)],
        [low[0:1], low[1:2], low[2:3], high[0:1], high[1:2]],
    )
    norms = ([sums[0:1], sums[1:2]], [norm1[0:1], norm1[1:2]])
    for k in range(blocks):
        gain_ref[k : k + 1, :], shift_ref[k : k + 1, :] = norms[k]
        skip, bias_low, bias_high, lam, scale = rows[k]
        skip_grad_ref[k : k + 1, :] = skip
        bias_grad_ref[k : k + 1, :width] = bias_low
        bias_grad_ref[k : k + 1, width:] = bias_high
        rate, angle = jnp.exp(decay_log[k : k + 1]), jnp.exp(phase_log[k : k + 1])
        size, fade = jnp.exp(-rate), jnp.exp(-2.0 * rate)
        lam_real, lam_imag = size * jnp.cos(angle), size * jnp.sin(angle)
        real, imag = lam[:, :states], lam[:, states : 2 * states]
        by_rate = scale[:, :states] * fade * lax.rsqrt(1.0 - fade) - (real * lam_real + imag * lam_imag)
        decay_grad_ref[k : k + 1, :] = rate * by_rate
        phase_grad_ref[k : k + 1, :] = angle * (imag * lam_real - real * lam_imag)


def results_kernel(chips, info_ref, sums_ref, norm1_ref, decay_ref, phase_ref, *refs):
    pieces, refs = refs[: 4 * chips], refs[4 * chips :]
    glu_ref, mix_ref, lift_ref, *small_refs = refs[:9]
    low_ref, under_ref, wide_ref, in_sems, sems = refs[9:]
    place = place_of("seq")
    core = lax.axis_index("seq") % 2
    _, rows, width = wide_ref.shape
    half, quarter = rows // 2, rows // 4
    arriving = []
    for n, piece in enumerate(pieces):
        parts = [pltpu.make_async_copy(piece.at[pl.ds(0, rows), :], low_ref.at[n], in_sems.at[n, 0])]
        if n >= 2 * chips:
            under = piece.at[pl.ds(rows, EXTRA), :]
            parts.append(pltpu.make_async_copy(under, under_ref.at[n - 2 * chips], in_sems.at[n, 1]))
        begin(parts)
        arriving.append(parts)
    copies = []
    extras = [jnp.zeros((EXTRA, width), f32)] * 2
    for n in range(4 * chips):
        finished(arriving[n])
        k, n_in = divmod(n, 2 * chips)
        chip, side = place ^ (n_in % chips), core if n_in < chips else 1 - core
        if k == 1:
            extra = under_ref[n_in].astype(f32)
            extras[n_in // chips] = jnp.where(chip == 0, extra, extras[n_in // chips])
        column = pl.multiple_of(side * width, width)
        row = pl.multiple_of(chip * half, 8)
        low = pl.multiple_of(side * (quarter * chips) + chip * quarter, 8)
        wide_ref[n] = low_ref[n].astype(f32)
        for i, (first, size, target) in enumerate(
            (
                (0, half, glu_ref.at[k, pl.ds(row, half), pl.ds(column, width)]),
                (half, quarter, mix_ref.at[k, pl.ds(low, quarter), :]),
                (half + quarter, quarter, lift_ref.at[k, pl.ds(low, quarter), :]),
            )
        ):
            copies.append(pltpu.make_async_copy(wide_ref.at[n, pl.ds(first, size), :], target, sems.at[n, i]))
            copies[-1].start()
    even = core == 0
    small_grads(
        jnp.sum(sums_ref[...], axis=0),
        norm1_ref[...],
        jnp.where(even, extras[0], extras[1]),
        jnp.where(even, extras[1], extras[0]),
        decay_ref[...],
        phase_ref[...],
        small_refs,
    )
    finished(copies)


def results(info, sums, norm1, decay_log, phase_log, pieces, after=()):
    rows, width = pieces[0].shape
    count = len(pieces)
    anywhere = pl.BlockSpec(memory_space=pl.ANY)
    shapes = [(2, width, 2 * width), (2, width, width), (2, width, width)]
    outs = [(anywhere, jax.ShapeDtypeStruct(shape, f32)) for shape in shapes]
    blocks, states = decay_log.shape
    outs += [moved((blocks, n), f32) for n in (width, width, states, states, width, 2 * width)]
    scratch = [
        pltpu.VMEM((count, rows, width), bf16),
        pltpu.VMEM((count // 2, EXTRA, width), bf16),
        pltpu.VMEM((count, rows, width), f32),
        pltpu.SemaphoreType.DMA((count, 2)),
        pltpu.SemaphoreType.DMA((count, 3)),
    ]
    inputs = (sums, norm1, decay_log, phase_log)
    kernel = partial(results_kernel, count // 4)
    return call(kernel, info, inputs, (), pieces, outs, scratch, "results", after, us=7.0)


def leave_kernel(seqs, info_ref, rows_ref, out_ref, wide_ref):
    _, span, width = out_ref.shape
    wide_ref[...] = rows_ref[...].astype(f32).reshape(wide_ref.shape)
    shuffle = shuffle_matrix(span, True)
    for s in range(seqs):
        out_ref[s] = dot(shuffle, wide_ref[:, s].reshape(span, width).astype(bf16)).astype(bf16)


def leave(info, rows, seqs, after=()):
    span, width = rows.shape[0] // seqs, rows.shape[1]
    scratch = [pltpu.VMEM((span // CHUNKS, seqs, CHUNKS, width), f32)]
    outs = [moved((seqs, span, width), bf16)]
    return call(partial(leave_kernel, seqs), info, (rows,), (), (), outs, scratch, "leave", after)


def input_grad_kernel(
    info_ref, sums_ref, tokens_ref, ahead_ref, stats_ref, gain_ref, grad_ref, wide_ref
):
    seqs, span, width = tokens_ref.shape
    where = Where(info_ref, seqs, span)
    wide_ref[...] = ahead_ref[...].astype(f32).reshape(wide_ref.shape)
    shuffle = shuffle_matrix(span, True)
    average, root = stats_ref[0:1, :], stats_ref[1:2, :]
    factor = root * gain_ref[0:1, :] / stats_ref[2:3, 0:1]
    sums = jnp.sum(sums_ref[...], axis=0)
    by_gain = factor * sums[0:1] * root
    fixed = factor * sums[1:2] - by_gain * average
    step = lax.broadcasted_iota(jnp.int32, (span, 1), 0)
    for s in range(seqs):
        valid = (step < where.lefts[s]).astype(f32)
        ahead = dot(shuffle, wide_ref[:, s].reshape(span, width).astype(bf16))
        grad_ref[s] = (ahead - valid * (fixed + by_gain * tokens_ref[s].astype(f32))).astype(bf16)


def input_grads(info, sums, tokens, ahead, stats, gain, after=()):
    seqs, span, width = tokens.shape
    outs = [moved(tokens.shape, bf16)]
    scratch = [pltpu.VMEM((span // CHUNKS, seqs, CHUNKS, width), f32)]
    return call(
        input_grad_kernel, info, (sums, tokens, ahead, stats, gain), (), (), outs, scratch, "input_grad", after, us=2.0
    )


def to_all(x, axes):
    return lax.all_to_all(x, axes, split_axis=0, concat_axis=0, tiled=True)


def local(
    tokens,
    lengths,
    cotangent,
    norm_gain,
    norm_shift,
    lift_weight,
    decay_log,
    phase_log,
    skip_gain,
    mix_weight,
    glu_weight,
    glu_bias,
):
    both = ("seq", "batch")
    seq_devices, batches = lax.axis_size("seq"), lax.axis_size("batch")
    devices, chips = seq_devices * batches, seq_devices // 2
    seqs, span, width = tokens.shape
    rows = seqs * span
    info = lengths
    turns = (decay_log, phase_log)
    norms_in = (norm_gain, norm_shift)
    states = decay_log.shape[1]
    half = width // 2

    sums, tokens_here, lift_w = enter(info, tokens, devices, [(lift_weight, 0)])
    sums = to_all(sums, both)
    normed, lifted, ends, part, stats0, x, mix_w, glu_w = lift(
        0, seqs, seq_devices, info, (sums, *norms_in, *turns), (tokens_here, lift_w), rows,
        [(mix_weight, 0), (glu_weight, 0)],
    )
    x1, sums, kept, lift_w, normed0 = mix(
        0, info, (to_all(part, "seq"), skip_gain, glu_bias, *turns), (ends, lifted, normed, x, mix_w, glu_w),
        devices, [(lift_weight, 1)], (normed,),
    )
    sums = to_all(sums, both)

    normed1, lifted1, ends, part, stats1, mix_w, glu_w = lift(
        1, seqs, seq_devices, info, (sums, *norms_in, *turns, stats0), (x1, lift_w), rows,
        [(mix_weight, 1), (glu_weight, 1)],
    )
    state1, activated1, slope1, gate1, gate_slope1, masked, cot = mix(
        1, info, (to_all(part, "seq"), skip_gain, glu_bias, *turns), (ends, lifted1, normed1, x1, mix_w, glu_w),
        devices, [(cotangent, None)],
    )

    glu_packed, bias_grad1, skip_grad1, ends, part, lift_w, masked = glu_back(
        1, seqs, seq_devices, info, turns, (cot, normed1, slope1, gate1, gate_slope1, glu_w, mix_w), (), rows, width,
        (), [(lift_weight, 1)], [masked],
    )
    lift_packed, sums, lam_grad1, scale_grad1 = lift_back(
        1, info, (to_all(part, "seq"), stats1, skip_gain, *turns, *norms_in),
        (ends, glu_packed, normed1, state1, lift_w), devices,
    )
    glu_part, mix_part, lift_part = (0, width, (0, 0), (0, width)), (1, half, (0, 0), (half, 0)), (2, half, (0, 0), (half, 0))
    glu_lanes, lift_lanes = glu_pack(width, 2 * states).lanes, lift_pack(width, 2 * states).lanes
    kept_lanes, every = kept_pack(width, 2 * states).lanes, slice(None)
    out = halves(
        info,
        (glu_part, mix_part, lift_part),
        (
            ((0, every), (1, glu_lanes["projected"])),
            ((2, every), (1, glu_lanes["mixed"])),
            ((3, every), (4, lift_lanes["lifted"])),
        ),
        (skip_grad1, bias_grad1, lam_grad1, scale_grad1),
        (activated1, glu_packed, state1, normed1, lift_packed),
        width,
        "halves1",
    )
    keep1, send = out
    got1 = trade(send, "seq", 1)
    (produced,) = out = leave(info, masked, seqs, (out.tick,))
    shares = (width, half, half)
    z, xy = range(1, batches), range(2, seq_devices, 2)
    extra = EXTRA * chips
    out = split(info, ((*shares, extra),), [keep1, got1], True, (out.tick,))
    (sums,) = gate(info, [sums], (out.tick,))
    pieces1 = sent(out, "seq", xy)
    sums = to_all(sums, both)

    state_lanes = (slice(None), kept_lanes["state"])
    pieces1 = there1 = gate(info, pieces1, ())
    out = glu_back(
        0, seqs, seq_devices, info, (*turns, sums, stats1, *norms_in), (lift_packed,),
        (kept, normed0, glu_weight, mix_weight), rows, width, (there1.tick,),
        [(kept, state_lanes), (lift_weight, 0)],
    )
    glu_packed, bias_grad0, skip_grad0, ends, part, norm_sums1, normed, state, lift_w = out
    small = (skip_grad0, bias_grad0)
    activated_lanes = (slice(None), kept_lanes["activated"])
    back_lifted0, sums, ahead, activated = out = lift_back(
        0, info, (to_all(part, "seq"), stats0, skip_gain, *turns, *norms_in, *small),
        (ends, glu_packed, normed, state, lift_w), devices, (), [(kept, activated_lanes)],
    )

    keep0, send = out = halves(
        info,
        (glu_part, mix_part, lift_part),
        (
            ((0, every), (1, glu_lanes["projected"])),
            ((2, every), (1, glu_lanes["mixed"])),
            ((3, every), (4, every)),
        ),
        (),
        (activated, glu_packed, state, normed, back_lifted0),
        width,
        "halves0",
    )
    got0 = trade(send, "seq", 1)
    (sums,) = gate(info, [sums], (out.tick,))
    sums = to_all(sums, both)
    out1 = cut(info, pieces1, EXTRA, (out.tick,))
    out0 = split(info, (shares,), [keep0, got0], True, (out1.tick,))
    out0 = cut(info, sent(out0, "seq", xy), 0, (out0.tick,))
    sum1 = sum_of(info, sent(out1, "batch", z), (out0.tick,))
    sum0 = sum_of(info, sent(out0, "batch", z), (sum1.tick,))
    (own1,) = out = join(info, to_others(sum1[0], "batch", z), EXTRA, (sum0.tick,))
    (own0,) = out = join(info, to_others(sum0[0], "batch", z), 0, (out.tick,))
    total = to_others(own0, "seq", xy) + to_others(own1, "seq", xy)
    (input_grad,) = out = input_grads(info, sums, tokens, ahead, stats0, norm_gain, (out.tick,))
    total = gate(info, total, (out.tick,))
    other = [trade(x, "seq", 1) for x in total]
    total = total[:chips] + other[:chips] + total[chips:] + other[chips:]
    grad_glu, grad_mix, grad_lift, grad_gain, grad_shift, grad_decay, grad_phase, grad_skip, grad_bias = results(
        info, sums, norm_sums1, *turns, total
    )
    return (
        produced,
        input_grad,
        grad_gain,
        grad_shift,
        grad_lift,
        grad_decay,
        grad_phase,
        grad_skip,
        grad_mix,
        grad_glu,
        grad_bias,
    )


def solution(mesh):
    split = P("batch", "seq", None)
    placed = (split, P("batch"), split) + (P(),) * 9
    return jax.shard_map(
        local,
        mesh=mesh,
        in_specs=placed,
        out_specs=(split, split) + (P(),) * 9,
        check_vma=False,
    )
```

```python
from functools import partial

import jax
import jax.numpy as jnp
from jax import lax
from jax.experimental import pallas as pl
from jax.experimental.pallas import tpu as pltpu
from jax.sharding import PartitionSpec as P

norm_eps = 1e-05
f32 = jnp.float32
bf16 = jnp.bfloat16

CHUNKS = 8
BLOCKS = 4
PARTS = 1
EXTRA = 16
LANES = 128
VMEM_LIMIT = 32 * 1024 * 1024

in_vmem = pl.BlockSpec(memory_space=pltpu.VMEM)
in_smem = pl.BlockSpec(memory_space=pltpu.SMEM)
in_hbm = pl.BlockSpec(memory_space=pltpu.HBM)


def near(shape, dtype):
    return in_vmem, pltpu.VMEM(shape, dtype)


def moved(shape, dtype):
    return in_vmem, jax.ShapeDtypeStruct(shape, dtype)


def copy_parts(source, target, sems):
    size = source.shape[0] // sems.shape[0]
    cuts = [pl.ds(i * size, size) for i in range(sems.shape[0])]
    return [pltpu.make_async_copy(source.at[cut], target.at[cut], sems.at[i]) for i, cut in enumerate(cuts)]


def begin(copies):
    for copy in copies:
        copy.start()


def finished(copies):
    for copy in copies:
        copy.wait()


class Outs(list):
    tick = None


def run(body, info, given, specs, outs, scratch, name, after, aliases=(), us=None):
    cost = None
    if us is not None:
        cost = pl.CostEstimate(flops=int(us * 1.1e9), bytes_accessed=int(us * 3e6), transcendentals=0)
    after = [pltpu.with_memory_space_constraint(t, pltpu.HBM) for t in after]
    n_in, n_out = 1 + len(given), len(outs)

    def ticking(*refs):
        body(*refs[:n_in], *refs[n_in + len(after) : n_in + len(after) + n_out], *refs[n_in + len(after) + n_out + 1 :])

    out = pl.pallas_call(
        ticking,
        in_specs=[in_smem] + specs + [in_hbm] * len(after),
        out_specs=[spec for spec, _ in outs] + [in_hbm],
        out_shape=[shape for _, shape in outs] + [pltpu.HBM((8, LANES), f32)],
        scratch_shapes=scratch,
        input_output_aliases=dict(aliases),
        compiler_params=pltpu.CompilerParams(vmem_limit_bytes=VMEM_LIMIT),
        cost_estimate=cost,
        name=name,
    )(info, *given, *after)
    result = Outs(out[:n_out])
    result.tick = out[n_out]
    return result


def here(x):
    return pltpu.with_memory_space_constraint(x, pltpu.VMEM)


def there(x):
    return pltpu.with_memory_space_constraint(x, pltpu.HBM)


def call(kernel, info, inputs, arrays, away, outs, scratch, name, after=(), fetch=(), spill=(), us=None):
    first = 1 + len(inputs) + len(arrays) + len(away)
    n_copies = len(fetch) + len(spill)
    fetched = [jax.eval_shape(lambda x, at=at: x if at is None else x[at], a) for a, at in fetch]
    outs = list(outs)
    n_outs = len(outs)
    outs += [near(a.shape, a.dtype) for a in fetched] + [(in_hbm, pltpu.HBM(a.shape, a.dtype)) for a in spill]

    def body(*refs):
        ins, rest = refs[: first + n_copies], refs[first + n_copies :]
        sources = list(ins[first:])
        for i, (_, at) in enumerate(fetch):
            if at is not None:
                sources[i] = sources[i].at[at]
        targets = rest[n_outs : n_outs + n_copies]
        rest = rest[:n_outs] + rest[n_outs + n_copies :]
        copies = []
        for i, (x, y) in enumerate(zip(sources, targets)):
            copies += copy_parts(x, y, rest[-1].at[i])
        begin(copies)
        kernel(*ins[:first], *(rest[:-1] if copies else rest))
        finished(copies)

    given = [*inputs, *map(here, arrays), *map(there, away), *(there(a) for a, _ in fetch), *map(here, spill)]
    specs = [in_vmem] * (len(inputs) + len(arrays)) + [in_hbm] * (len(away) + len(fetch)) + [in_vmem] * len(spill)
    scratch = list(scratch) + [pltpu.SemaphoreType.DMA((n_copies, PARTS))] * bool(n_copies)
    return run(body, info, given, specs, outs, scratch, name, after, us=us)


class Pack:
    def __init__(self, *fields):
        self.lanes, self.width = {}, 0
        for name, width in fields:
            self.lanes[name] = slice(self.width, self.width + width)
            self.width += width

    def views(self, ref, *names):
        return [ref.at[:, self.lanes[n]] for n in names]


def kept_pack(width, states):
    return Pack(*((n, width) for n in ("slope", "gate", "gate_slope", "activated")), ("state", states))


def glu_pack(width, states):
    return Pack(("projected", 2 * width), ("mixed", width), ("dh", states), ("back", width))


def lift_pack(width, states):
    return Pack(("lifted", states), ("back_normed", width), ("back", width), ("normed", width))


def wide(mask, width):
    return jnp.concatenate([mask] * (width // LANES), axis=1)


def dot(a, b):
    return lax.dot_general(a, b, (((1,), (0,)), ((), ())), preferred_element_type=f32)


def dot_t(a, b):
    return lax.dot_general(a, b, (((1,), (1,)), ((), ())), preferred_element_type=f32)


def t_dot(a, b):
    return lax.dot_general(a, b, (((0,), (0,)), ((), ())), preferred_element_type=f32)


def cmul(ar, ai, br, bi):
    return ar * br - ai * bi, ar * bi + ai * br


def order(steps, reverse):
    return range(steps - 1, -1, -1) if reverse else range(steps)


def shuffle_matrix(span, back):
    chunk = span // CHUNKS
    place = lax.broadcasted_iota(jnp.int32, (span, span), 0)
    source = lax.broadcasted_iota(jnp.int32, (span, span), 1)
    if back:
        wanted = (place % chunk) * CHUNKS + place // chunk
    else:
        wanted = (place % CHUNKS) * chunk + place // CHUNKS
    return (source == wanted).astype(f32).astype(bf16)


class Where:
    def __init__(self, info_ref, seqs, span):
        self.seq = lax.axis_index("seq")
        self.seqs, self.span = seqs, span
        self.lengths = [info_ref[s] for s in range(seqs)]
        self.lefts = [length - self.seq * span for length in self.lengths]

    def steps_left(self):
        before = (self.span // CHUNKS) * lax.broadcasted_iota(jnp.int32, (CHUNKS, LANES), 0)
        return jnp.concatenate([left - before for left in self.lefts], axis=0)


def valid_rows(left, first, steps):
    return jnp.concatenate([(left > first + t).astype(f32) for t in range(steps)], axis=0)


def shuffle_rows(wide_ref, source_ref):
    steps, seqs, chunks, width = wide_ref.shape
    shuffle = shuffle_matrix(steps * chunks, False)
    for s in range(seqs):
        wide_ref[:, s] = dot(shuffle, source_ref[s]).reshape(steps, chunks, width)


def enter_kernel(info_ref, tokens_ref, sums_ref, here_ref, acc_ref, sems):
    seqs, span, width = tokens_ref.shape
    copies = [copy_parts(tokens_ref.at[s], here_ref.at[s], sems.at[s]) for s in range(seqs)]
    for parts in copies:
        begin(parts)
    where = Where(info_ref, seqs, span)
    step = lax.broadcasted_iota(jnp.int32, (span, 1), 0)
    total = jnp.zeros((1, width), f32)
    squares = jnp.zeros((1, width), f32)
    count = jnp.zeros((1, 1), f32)
    for s in range(seqs):
        valid = (step < where.lefts[s]).astype(f32)
        finished(copies[s])
        x = here_ref[s].astype(f32)
        masked = x * valid
        total += jnp.sum(masked, axis=0, keepdims=True)
        squares += jnp.sum(masked * x, axis=0, keepdims=True)
        count += jnp.sum(valid, axis=0, keepdims=True)
    tail = jnp.broadcast_to(count, (1, LANES))
    acc_ref[0:1, :] = jnp.concatenate([total, tail], axis=1)
    acc_ref[1:2, :] = jnp.concatenate([squares, tail], axis=1)
    for j in range(sums_ref.shape[0]):
        sums_ref[j] = acc_ref[...]


def enter(info, tokens, devices, fetch):
    seqs, _, width = tokens.shape
    outs = [moved((devices, 2, width + LANES), f32), near(tokens.shape, bf16)]
    scratch = [pltpu.VMEM((2, width + LANES), f32), pltpu.SemaphoreType.DMA((seqs, 1))]
    return call(enter_kernel, info, (), (), (tokens,), outs, scratch, "enter", fetch=fetch)


class Powers:
    @staticmethod
    def scratch(seqs, seq_devices, states, leaps):
        tables = [((1, 2 * states), f32), ((1, states), f32), ((2 * states // LANES, seqs * CHUNKS, LANES), f32)]
        if leaps:
            tables.append(((seq_devices * seqs, 2 * states), f32))
        return [pltpu.VMEM(*t) for t in tables]

    def __init__(self, k, back, where, decay_ref, phase_ref, lam_ref, scale_ref, table_ref, leap_ref=None):
        states = scale_ref.shape[1]
        groups, group = states // LANES, table_ref.shape[1]
        seqs, span, limit = where.seqs, where.span, where.span // CHUNKS
        rate = jnp.exp(decay_ref[k : k + 1, :])
        size, angle = jnp.exp(-rate), jnp.exp(phase_ref[k : k + 1, :])
        lam_ref[:, :states] = size * jnp.cos(angle)
        lam_ref[:, states:] = size * jnp.sin(angle) * (-1.0 if back else 1.0)
        scale_ref[...] = jnp.sqrt(1.0 - jnp.exp(-2.0 * rate))
        self.lam, self.scale, self.table, self.leaps = lam_ref, scale_ref, table_ref, leap_ref
        shift = 0 if not back else (-1 if k == 0 else 1)
        chunk_count = jnp.clip(where.steps_left() + shift, 0, limit)
        if leap_ref is not None:
            total = leap_ref.shape[0]
            line = lax.broadcasted_iota(jnp.int32, (total, LANES), 0)
            span_left = jnp.zeros((total, LANES), jnp.int32)
            for s, length in enumerate(where.lengths):
                span_left = jnp.where(line % seqs == s, length - span * (line // seqs), span_left)
            span_count = jnp.clip(span_left + shift, 0, span)
        for low in range(groups):
            real_lanes = slice(low * LANES, (low + 1) * LANES)
            imag_lanes = slice((groups + low) * LANES, (groups + low + 1) * LANES)
            br, bi = lam_ref[:, real_lanes], lam_ref[:, imag_lanes]
            cr = jnp.ones((group, LANES), f32)
            ci = jnp.zeros((group, LANES), f32)
            if leap_ref is not None:
                pr = jnp.ones((total, LANES), f32)
                pi = jnp.zeros((total, LANES), f32)
            for bit in range((limit if leap_ref is None else span).bit_length()):
                if (1 << bit) <= limit:
                    nr, ni = cmul(cr, ci, br, bi)
                    odd = (chunk_count & (1 << bit)) != 0
                    cr, ci = jnp.where(odd, nr, cr), jnp.where(odd, ni, ci)
                if leap_ref is not None:
                    nr, ni = cmul(pr, pi, br, bi)
                    odd = (span_count & (1 << bit)) != 0
                    pr, pi = jnp.where(odd, nr, pr), jnp.where(odd, ni, pi)
                br, bi = cmul(br, bi, br, bi)
            table_ref[low] = cr
            table_ref[groups + low] = ci
            if leap_ref is not None:
                leap_ref[:, real_lanes] = pr
                leap_ref[:, imag_lanes] = pi


def stretch_part(ends_ref, power_ref, reverse, seqs):
    groups = ends_ref.shape[0] // 2
    reals, imags = [], []
    for low in range(groups):
        real = jnp.zeros((seqs, LANES), f32)
        imag = jnp.zeros((seqs, LANES), f32)
        for c in order(CHUNKS, reverse):
            here = pl.ds(c, seqs, stride=CHUNKS)
            real, imag = cmul(power_ref[low, here, :], power_ref[groups + low, here, :], real, imag)
            real += ends_ref[low, here, :]
            imag += ends_ref[groups + low, here, :]
        reals.append(real)
        imags.append(imag)
    return jnp.concatenate(reals + imags, axis=1)


def chunk_starts(start_ref, place, parts_ref, leaps_ref, ends_ref, power_ref, reverse):
    devices, seqs, width = parts_ref.shape
    states = width // 2
    groups = states // LANES
    real = jnp.zeros((seqs, states), f32)
    imag = jnp.zeros((seqs, states), f32)
    for j in order(devices, reverse):
        ahead = (j > place) if reverse else (j < place)
        leap, part = leaps_ref[seqs * j : seqs * (j + 1), :], parts_ref[j]
        next_real, next_imag = cmul(leap[:, :states], leap[:, states:], real, imag)
        real = jnp.where(ahead, next_real + part[:, :states], real)
        imag = jnp.where(ahead, next_imag + part[:, states:], imag)
    for low in range(groups):
        hr = real[:, low * LANES : (low + 1) * LANES]
        hi = imag[:, low * LANES : (low + 1) * LANES]
        for c in order(CHUNKS, reverse):
            here = pl.ds(c, seqs, stride=CHUNKS)
            start_ref[low, here, :] = hr
            start_ref[groups + low, here, :] = hi
            hr, hi = cmul(power_ref[low, here, :], power_ref[groups + low, here, :], hr, hi)
            hr += ends_ref[low, here, :]
            hi += ends_ref[groups + low, here, :]


def scan_block(h_ref, drive, left, lam, shift, first, steps, reverse, out_ref=None):
    groups, group, _ = h_ref.shape
    groups = groups // 2
    masks = [left > first + t + shift for t in range(steps)]
    for low in range(groups):
        real_lanes = slice(low * LANES, (low + 1) * LANES)
        imag_lanes = slice((groups + low) * LANES, (groups + low + 1) * LANES)
        hr, hi = h_ref[low], h_ref[groups + low]
        lr, li = lam[:, real_lanes], lam[:, imag_lanes]
        for t in order(steps, reverse):
            ur, ui = drive(t, real_lanes, imag_lanes)
            nr, ni = cmul(lr, li, hr, hi)
            hr = jnp.where(masks[t], nr, hr) + ur
            hi = jnp.where(masks[t], ni, hi) + ui
            if out_ref is not None:
                out_ref[t * group : (t + 1) * group, real_lanes] = hr
                out_ref[t * group : (t + 1) * group, imag_lanes] = hi
        h_ref[low] = hr
        h_ref[groups + low] = hi


def input_drive(lifted, scale, left, first, steps):
    group = left.shape[0]
    masks = [left > first + t for t in range(steps)]

    def drive(t, real_lanes, imag_lanes):
        here = slice(t * group, (t + 1) * group)
        factor = jnp.where(masks[t], scale[:, real_lanes], 0.0)
        return factor * lifted[here, real_lanes], factor * lifted[here, imag_lanes]

    return drive


def blocks_of(rows, group, reverse):
    size = rows // BLOCKS
    for block in order(BLOCKS, reverse):
        yield block, block * (size // group), slice(block * size, (block + 1) * size)


def lift_kernel(k, seqs, info_ref, sums_ref, gain_ref, shift_ref, decay_ref, phase_ref, *refs):
    reverse = k == 1
    if k == 0:
        x_ref, weight_ref, normed_ref, lifted_ref, ends_ref, part_ref, stats_ref, rows_ref, wide_ref = refs[:9]
        refs = refs[9:]
    else:
        count_ref, x_ref, weight_ref, normed_ref, lifted_ref, ends_ref, part_ref, stats_ref = refs[:8]
        refs = refs[8:]
    rows, width = normed_ref.shape
    group = ends_ref.shape[1]
    size = rows // BLOCKS
    steps = size // group
    where = Where(info_ref, seqs, rows // seqs)
    powers = Powers(k, False, where, decay_ref, phase_ref, *refs)
    if k == 0:
        shuffle_rows(wide_ref, x_ref)
    sums = jnp.sum(sums_ref[...], axis=0)
    if k == 0:
        count = sums[0:1, width : width + 1]
    else:
        count = count_ref[2:3, 0:1]
    average = sums[0:1, :width] / count
    root = lax.rsqrt(sums[1:2, :width] / count - average * average + norm_eps)
    stats_ref[0:1, :] = average
    stats_ref[1:2, :] = root
    stats_ref[2:3, :] = jnp.broadcast_to(count, (1, width))
    gain, shift = gain_ref[k : k + 1, :], shift_ref[k : k + 1, :]
    lam, scale = powers.lam[...], powers.scale[...]
    left = where.steps_left()
    ends_ref[...] = jnp.zeros_like(ends_ref)
    for _, first, now in blocks_of(rows, group, reverse):
        if k == 0:
            x = wide_ref[first : first + steps].reshape(size, width)
            rows_ref[now, :] = x.astype(bf16)
        else:
            x = x_ref[now, :]
        normed = ((x - average) * root * gain + shift).astype(bf16)
        normed_ref[now, :] = normed
        lifted = dot(normed, weight_ref[...]).astype(bf16)
        lifted_ref[now, :] = lifted
        drive = input_drive(lifted.astype(f32), scale, left, first, steps)
        scan_block(ends_ref, drive, left, lam, 0, first, steps, reverse)
    part = stretch_part(ends_ref, powers.table, reverse, seqs)
    for j in range(part_ref.shape[0]):
        part_ref[j] = part


def lift(k, seqs, seq_devices, info, inputs, arrays, rows, fetch):
    gain, decay = inputs[1], inputs[3]
    width, states = gain.shape[1], decay.shape[1]
    outs = [
        near((rows, width), bf16),
        near((rows, 2 * states), bf16),
        near((2 * states // LANES, seqs * CHUNKS, LANES), f32),
        moved((seq_devices, seqs, 2 * states), f32),
        moved((8, width), f32),
    ]
    scratch = []
    if k == 0:
        outs.append(near((rows, width), bf16))
        scratch.append(pltpu.VMEM((rows // seqs // CHUNKS, seqs, CHUNKS, width), f32))
    scratch += Powers.scratch(seqs, seq_devices, states, False)
    return call(partial(lift_kernel, k, seqs), info, inputs, arrays, (), outs, scratch, "lift", fetch=fetch)


def mix_kernel(k, info_ref, parts_ref, skip_ref, bias_ref, decay_ref, phase_ref, *refs):
    reverse = k == 1
    (ends_ref, lifted_ref, normed_ref, x_ref, mix_ref, glu_ref) = refs[:6]
    tables, refs = refs[-4:], refs[6:-4]
    if reverse:
        state_ref, activated_ref, slope_ref, gate_ref, gate_slope_ref, masked_ref, h_ref, states_ref = refs
    else:
        next_ref, sums_ref, kept_out, h_ref, states_ref, acc_ref, kept_ref, sems = refs
        pack = kept_pack(x_ref.shape[1], lifted_ref.shape[1])
        state_ref, activated_ref, slope_ref, gate_ref, gate_slope_ref = pack.views(
            kept_ref, "state", "activated", "slope", "gate", "gate_slope"
        )
        copies = []
    seqs = parts_ref.shape[1]
    rows, width = x_ref.shape
    group = ends_ref.shape[1]
    steps = rows // BLOCKS // group
    where = Where(info_ref, seqs, rows // seqs)
    powers = Powers(k, False, where, decay_ref, phase_ref, *tables)
    chunk_starts(h_ref, where.seq, parts_ref, powers.leaps, ends_ref, powers.table, reverse)
    left = where.steps_left()
    skip, bias = skip_ref[k : k + 1, :], bias_ref[k : k + 1, :]
    lam, scale = powers.lam[...], powers.scale[...]
    total = jnp.zeros((1, width), f32)
    squares = jnp.zeros((1, width), f32)
    for block, first, now in blocks_of(rows, group, reverse):
        drive = input_drive(lifted_ref[now, :].astype(f32), scale, left, first, steps)
        scan_block(h_ref, drive, left, lam, 0, first, steps, reverse, states_ref)
        state = states_ref[...].astype(bf16)
        state_ref[now, :] = state
        mixed = dot(state, mix_ref[...]) + skip * normed_ref[now, :].astype(f32)
        base, cube = 0.7978845608028654, 0.044715
        square = mixed * mixed
        bend = jnp.tanh(mixed * (base + (base * cube) * square))
        half = 0.5 + 0.5 * bend
        activated = (mixed * half).astype(bf16)
        activated_ref[now, :] = activated
        slope_ref[now, :] = (
            half + mixed * (half - half * half) * (2.0 * base + (6.0 * base * cube) * square)
        ).astype(bf16)
        projected = dot(activated, glu_ref[...]) + bias
        gate = 0.5 + 0.5 * jnp.tanh(0.5 * projected[:, width:])
        gated = projected[:, :width] * gate
        gate_ref[now, :] = gate.astype(bf16)
        gate_slope_ref[now, :] = (gated - gated * gate).astype(bf16)
        after = x_ref[now, :].astype(f32) + gated
        masked = after * wide(valid_rows(left, first, steps), width)
        if reverse:
            masked_ref[now, :] = masked.astype(bf16)
        else:
            next_ref[now, :] = after
            total += jnp.sum(masked, axis=0, keepdims=True)
            squares += jnp.sum(masked * after, axis=0, keepdims=True)
            parts = copy_parts(kept_ref.at[now, :], kept_out.at[now, :], sems.at[block])
            begin(parts)
            copies += parts
    if not reverse:
        acc_ref[0:1, :] = total
        acc_ref[1:2, :] = squares
        for j in range(sums_ref.shape[0]):
            sums_ref[j] = acc_ref[...]
        finished(copies)


def mix(k, info, inputs, arrays, devices, fetch, spill=()):
    parts = inputs[0]
    ends, lifted, _, x = arrays[:4]
    rows, width = x.shape
    states = lifted.shape[1]
    seq_devices, seqs, _ = parts.shape
    scratch = [pltpu.VMEM(ends.shape, f32), pltpu.VMEM((rows // BLOCKS, states), f32)]
    if k == 1:
        outs = [near((rows, states), bf16)] + [near((rows, width), bf16)] * 5
    else:
        kept = (rows, kept_pack(width, states).width)
        outs = [near((rows, width), f32), moved((devices, 2, width), f32), (in_hbm, pltpu.HBM(kept, bf16))]
        scratch += [pltpu.VMEM((2, width), f32), pltpu.VMEM(kept, bf16), pltpu.SemaphoreType.DMA((BLOCKS, 1))]
    scratch += Powers.scratch(seqs, seq_devices, states // 2, True)
    return call(
        partial(mix_kernel, k), info, inputs, arrays, (), outs, scratch, "mix", fetch=fetch, spill=spill
    )


def glu_back_kernel(k, seqs, info_ref, decay_ref, phase_ref, *refs):
    reverse = k == 0
    if k == 0:
        sums_ref, stats_ref, gain_ref, shift_ref, lift_pack_ref, kept_ref, normed_in, glu_in, mix_in = refs[:9]
        tables, refs = refs[-3:], refs[9:-3]
    else:
        start_ref, normed_ref, slope_ref, gate_ref, gate_slope_ref, glu_ref, mix_ref = refs[:7]
        tables, refs = refs[-3:], refs[7:-3]
    out_ref, bias_grad_ref, skip_grad_ref, ends_ref, part_ref = refs[:5]
    refs = refs[5:]
    rows, width = out_ref.shape[0], skip_grad_ref.shape[1]
    states = 2 * decay_ref.shape[1]
    names = ("projected", "mixed", "dh", "back")
    projected_ref, mixed_ref, dh_ref, back_ref = glu_pack(width, states).views(out_ref, *names)
    if k == 0:
        total_ref, normed_ref, slopes_ref, glu_ref, mix_ref, sems, weight_sems = refs
        pack = kept_pack(width, states)
        back_normed_ref, start_ref, later_ref = lift_pack(width, states).views(
            lift_pack_ref, "back_normed", "back", "normed"
        )
        slope_ref, gate_ref, gate_slope_ref = pack.views(slopes_ref, "slope", "gate", "gate_slope")
    group = ends_ref.shape[1]
    size = rows // BLOCKS
    steps = size // group
    where = Where(info_ref, seqs, rows // seqs)
    if k == 1:
        (wide_ref,) = refs
        shuffle_rows(wide_ref, start_ref)
    else:
        copies = {}
        for block, _, now in blocks_of(rows, group, reverse):
            lanes = slice(0, 3 * width)
            copies[block] = copy_parts(kept_ref.at[now, lanes], slopes_ref.at[now, :], sems.at[0, block])
            copies[block] += copy_parts(normed_in.at[now, :], normed_ref.at[now, :], sems.at[1, block])
        weights = copy_parts(glu_in.at[k], glu_ref, weight_sems.at[0])
        weights += copy_parts(mix_in.at[k], mix_ref, weight_sems.at[1])
        for n, block in enumerate(order(BLOCKS, reverse)):
            begin(copies[block])
            if n == 0:
                begin(weights)
        sums = jnp.sum(sums_ref[...], axis=0)
        total_ref[...] = sums
        root, count = stats_ref[1:2, :], stats_ref[2:3, 0:1]
        gain, shift = gain_ref[1:2, :], shift_ref[1:2, :]
        by_normed = sums[0:1] / count
        fixed = (gain * sums[1:2] - shift * sums[0:1]) / count
    powers = Powers(k, True, where, decay_ref, phase_ref, *tables)
    left = where.steps_left()
    lam = powers.lam[...]
    ends_ref[...] = jnp.zeros_like(ends_ref)
    bias_grad = jnp.zeros((1, 2 * width), f32)
    skip_grad = jnp.zeros((1, width), f32)
    for block, first, now in blocks_of(rows, group, reverse):
        valid = wide(valid_rows(left, first, steps), width)
        if k == 1:
            back = wide_ref[first : first + steps].reshape(size, width) * valid
        else:
            finished(copies[block])
            back = start_ref[now, :].astype(f32) + root * (
                gain * back_normed_ref[now, :].astype(f32)
                - valid * (fixed + by_normed * later_ref[now, :].astype(f32))
            )
        back_ref[now, :] = back.astype(bf16)
        value_back = (back * gate_ref[now, :].astype(f32)).astype(bf16)
        gate_back = (back * gate_slope_ref[now, :].astype(f32)).astype(bf16)
        back_projected = jnp.concatenate([value_back, gate_back], axis=1)
        projected_ref[now, :] = back_projected
        bias_grad += jnp.sum(back_projected.astype(f32), axis=0, keepdims=True)
        if k == 0 and block == BLOCKS - 1:
            finished(weights)
        back_activated = dot_t(back_projected, glu_ref[...])
        back_mixed = (slope_ref[now, :].astype(f32) * back_activated).astype(bf16)
        mixed_ref[now, :] = back_mixed
        skip_grad += jnp.sum(back_mixed.astype(f32) * normed_ref[now, :].astype(f32), axis=0, keepdims=True)
        back_state = dot_t(back_mixed, mix_ref[...]).astype(bf16)
        dh_ref[now, :] = back_state
        wide_state = back_state.astype(f32)

        def drive(t, real_lanes, imag_lanes):
            at = slice(t * group, (t + 1) * group)
            return wide_state[at, real_lanes], wide_state[at, imag_lanes]

        shift = 1 if reverse else -1
        scan_block(ends_ref, drive, left, lam, shift, first, steps, reverse)
    bias_grad_ref[...] = bias_grad
    skip_grad_ref[...] = skip_grad
    part = stretch_part(ends_ref, powers.table, reverse, seqs)
    for j in range(part_ref.shape[0]):
        part_ref[j] = part


def glu_back(k, seqs, seq_devices, info, inputs, arrays, away, rows, width, after, fetch, spill=()):
    states = inputs[0].shape[1]
    outs = [
        near((rows, glu_pack(width, 2 * states).width), bf16),
        moved((1, 2 * width), f32),
        moved((1, width), f32),
        near((2 * states // LANES, seqs * CHUNKS, LANES), f32),
        moved((seq_devices, seqs, 2 * states), f32),
    ]
    if k == 1:
        scratch = [pltpu.VMEM((rows // seqs // CHUNKS, seqs, CHUNKS, width), f32)]
    else:
        outs += [moved((2, width), f32), near((rows, width), bf16)]
        scratch = [
            pltpu.VMEM((rows, 3 * width), bf16),
            pltpu.VMEM((width, 2 * width), bf16),
            pltpu.VMEM((2 * states, width), bf16),
            pltpu.SemaphoreType.DMA((2, BLOCKS, 1)),
            pltpu.SemaphoreType.DMA((2, 1)),
        ]
    scratch += Powers.scratch(seqs, seq_devices, states, False)
    return call(
        partial(glu_back_kernel, k, seqs), info, inputs, arrays, away, outs, scratch, "glu_back", after, fetch, spill
    )


def lift_back_kernel(
    k, info_ref, parts_ref, stats_ref, skip_ref, decay_ref, phase_ref, gain_ref, shift_ref, *refs
):
    reverse = last = k == 0
    ends_ref, glu_pack_ref = refs[:2]
    states, width = 2 * decay_ref.shape[1], stats_ref.shape[1]
    mixed_ref, dh_ref, back_ref = glu_pack(width, states).views(glu_pack_ref, "mixed", "dh", "back")
    normed_ref, state_ref, weight_ref = refs[2:5]
    tables, refs = refs[-4:], refs[5:-4]
    if last:
        back_lifted_ref, sums_ref, lam_grad_ref, scale_grad_ref, ahead_ref = refs[:5]
        refs = refs[5:]
    else:
        out_ref, sums_ref, lam_grad_ref, scale_grad_ref = refs[:4]
        back_lifted_ref, back_normed_ref, kept_back_ref, kept_normed_ref = lift_pack(width, states).views(
            out_ref, "lifted", "back_normed", "back", "normed"
        )
        kept_back_ref[...] = back_ref[...]
        kept_normed_ref[...] = normed_ref[...]
        refs = refs[4:]
    h_ref, low_ref, acc_ref, lam_acc_ref, scale_acc_ref = refs
    rows, width = normed_ref.shape
    group = ends_ref.shape[1]
    seqs = parts_ref.shape[1]
    steps = rows // BLOCKS // group
    states = decay_ref.shape[1]
    where = Where(info_ref, seqs, rows // seqs)
    powers = Powers(k, True, where, decay_ref, phase_ref, *tables)
    chunk_starts(h_ref, where.seq, parts_ref, powers.leaps, ends_ref, powers.table, reverse)
    lam_acc_ref[...] = jnp.zeros_like(lam_acc_ref)
    scale_acc_ref[...] = jnp.zeros_like(scale_acc_ref)
    left = where.steps_left()
    lam, scale = powers.lam[...], powers.scale[...]
    root, gain, shift_row = stats_ref[1:2, :], gain_ref[k : k + 1, :], shift_ref[k : k + 1, :]
    skip = skip_ref[k : k + 1, :]
    gain_sum = jnp.zeros((1, width), f32)
    shift_sum = jnp.zeros((1, width), f32)
    shift = 1 if reverse else -1
    for _, first, now in blocks_of(rows, group, reverse):
        moving = [left > first + t + shift for t in range(steps)]
        valid = [left > first + t for t in range(steps)]
        dh = dh_ref[now, :].astype(f32)
        normed = normed_ref[now, :]
        lifted = dot(normed, weight_ref[...]).astype(bf16).astype(f32)
        state = state_ref[now, :].astype(f32)
        for low in range(0, states, LANES):
            real_lanes = slice(low, low + LANES)
            imag_lanes = slice(states + low, states + low + LANES)
            gr, gi = h_ref[low // LANES], h_ref[(states + low) // LANES]
            lr, li = lam[:, real_lanes], lam[:, imag_lanes]
            part = scale[:, real_lanes]
            sum_r, sum_i = lam_acc_ref[:, real_lanes], lam_acc_ref[:, imag_lanes]
            sum_s = scale_acc_ref[:, real_lanes]
            for t in order(steps, reverse):
                at = slice(t * group, (t + 1) * group)
                hr, hi = state[at, real_lanes], state[at, imag_lanes]
                ur, ui = lifted[at, real_lanes], lifted[at, imag_lanes]
                mr, mi = jnp.where(moving[t], gr, 0.0), jnp.where(moving[t], gi, 0.0)
                sum_r += mr * hr + mi * hi
                sum_i += mi * hr - mr * hi
                nr, ni = cmul(lr, li, gr, gi)
                gr = jnp.where(moving[t], nr, gr) + dh[at, real_lanes]
                gi = jnp.where(moving[t], ni, gi) + dh[at, imag_lanes]
                vr, vi = jnp.where(valid[t], gr, 0.0), jnp.where(valid[t], gi, 0.0)
                sum_s += vr * ur + vi * ui
                low_ref[at, real_lanes] = part * vr
                low_ref[at, imag_lanes] = part * vi
            h_ref[low // LANES] = gr
            h_ref[(states + low) // LANES] = gi
            lam_acc_ref[:, real_lanes] = sum_r
            lam_acc_ref[:, imag_lanes] = sum_i
            scale_acc_ref[:, real_lanes] = sum_s
        back_lifted = low_ref[...].astype(bf16)
        back_lifted_ref[now, :] = back_lifted
        back_normed = dot_t(back_lifted, weight_ref[...]) + skip * mixed_ref[now, :].astype(f32)
        gain_sum += jnp.sum(back_normed * normed.astype(f32), axis=0, keepdims=True)
        shift_sum += jnp.sum(back_normed, axis=0, keepdims=True)
        if last:
            ahead_ref[now, :] = (back_ref[now, :].astype(f32) + (root * gain) * back_normed).astype(bf16)
        else:
            back_normed_ref[now, :] = back_normed.astype(bf16)
    lam_grad = jnp.sum(lam_acc_ref[...], axis=0, keepdims=True)
    scale_grad = jnp.sum(scale_acc_ref[...], axis=0, keepdims=True)
    acc_ref[0:1, :] = (gain_sum - shift_row * shift_sum) / gain
    acc_ref[1:2, :] = shift_sum
    lam_grad_ref[...] = lam_grad
    scale_grad_ref[...] = scale_grad
    for j in range(sums_ref.shape[0]):
        sums_ref[j] = acc_ref[...]


def lift_back(k, info, inputs, arrays, devices, after=(), fetch=()):
    parts, stats, decay = inputs[0], inputs[1], inputs[3]
    ends, packed = arrays[:2]
    rows, width, states = packed.shape[0], stats.shape[1], 2 * decay.shape[1]
    seq_devices, seqs, _ = parts.shape
    table = ends.shape
    acc = (2, width)
    outs = [near((rows, states if k == 0 else lift_pack(width, states).width), bf16), moved((devices,) + acc, f32)]
    outs += [moved((1, states), f32), moved((1, states // 2), f32)]
    if k == 0:
        outs.append(moved((rows, width), bf16))
    scratch = [
        pltpu.VMEM(table, f32),
        pltpu.VMEM((rows // BLOCKS, states), f32),
        pltpu.VMEM(acc, f32),
        pltpu.VMEM((table[1], states), f32),
        pltpu.VMEM((table[1], states // 2), f32),
    ]
    scratch += Powers.scratch(seqs, seq_devices, states // 2, True)
    return call(partial(lift_back_kernel, k), info, inputs, arrays, (), outs, scratch, "lift_back", after, fetch)


def two_parts(rows):
    high = rows.astype(bf16).astype(f32)
    return jnp.concatenate([high, rows - high], axis=0)


def one_part(rows):
    half = rows.shape[0] // 2
    return rows[:half] + rows[half:]


def halves_kernel(parts, pairs, small, info_ref, *refs):
    keep_ref, send_ref = refs[-2:]
    width = keep_ref.shape[1]
    even = lax.axis_index("seq") % 2 == 0
    if small:
        small_refs, refs = refs[:4], refs[4:]
    products = [t_dot(*(refs[n][:, lanes] for n, lanes in pair)) for pair in pairs]
    first = 0
    for n, rows, (r, c), (q, d) in parts:
        a = products[n][r : r + rows, c : c + width].astype(bf16)
        b = products[n][q : q + rows, d : d + width].astype(bf16)
        keep_ref[first : first + rows, :] = jnp.where(even, a, b)
        send_ref[first : first + rows, :] = jnp.where(even, b, a)
        first += rows
    if small:
        skip_ref, bias_ref, lam_ref, scale_ref = small_refs
        extra = keep_ref.shape[0] - first
        low = jnp.concatenate([skip_ref[...], bias_ref[:, :width], bias_ref[:, width:]], axis=0)
        scale = jnp.concatenate([scale_ref[...], jnp.zeros((1, width - scale_ref.shape[1]), f32)], axis=1)
        high = jnp.concatenate([lam_ref[...], scale, jnp.zeros((1, width), f32)], axis=0)
        rest = [jnp.zeros((EXTRA // 2 - 3, width), f32)], [jnp.zeros((extra - EXTRA, width), f32)]
        low, high = (two_parts(jnp.concatenate([x, *rest[0]], axis=0)) for x in (low, high))
        low, high = (jnp.concatenate([x, *rest[1]], axis=0).astype(bf16) for x in (low, high))
        keep_ref[first:, :] = jnp.where(even, low, high)
        send_ref[first:, :] = jnp.where(even, high, low)


def halves(info, parts, pairs, small, arrays, width, name, after=()):
    rows = sum(p[1] for p in parts)
    if small:
        rows += EXTRA * (lax.axis_size("seq") // 2)
    outs = [moved((rows, width), bf16)] * 2
    return call(partial(halves_kernel, parts, pairs, bool(small)), info, small, arrays, (), outs, [], name, after)


def place_of(axis):
    return lax.axis_index("batch") if axis == "batch" else lax.axis_index("seq") // 2


def total_of(refs, rows):
    total = refs[0][rows, :].astype(f32)
    for ref in refs[1:]:
        total += ref[rows, :].astype(f32)
    return total


def split_kernel(chips, sets, xor, info_ref, *refs):
    n_in = 2 * len(sets)
    outs = refs[n_in:]
    place = place_of("seq")
    for m in range(chips):
        chip = place ^ m if xor else m
        low = 0
        for n, parts in enumerate(sets):
            first = 0
            for rows in parts:
                share = rows // chips
                start = first + chip * share
                if xor:
                    start = pl.multiple_of(start, 16)
                total = total_of(refs[2 * n : 2 * n + 2], pl.ds(start, share))
                if share == EXTRA:
                    total = two_parts(one_part(total))
                if xor:
                    outs[m][low : low + share, :] = total.astype(outs[m].dtype)
                else:
                    base = m * (outs[0].shape[0] // chips) + low
                    outs[0][base : base + share, :] = total.astype(outs[0].dtype)
                first, low = first + rows, low + share


def split(info, sets, arrays, xor, after=()):
    chips = lax.axis_size("seq") // 2
    width = arrays[0].shape[1]
    rows = sum(map(sum, sets))
    outs = [moved((rows, width), bf16)]
    if xor:
        outs = [moved((rows // chips, width), f32)] + [moved((rows // chips, width), bf16)] * (chips - 1)
    return call(partial(split_kernel, chips, sets, xor), info, arrays, (), (), outs, [], "split", after, us=0.8)


def cut_kernel(extra, info_ref, *refs):
    low_ref, refs = refs[-1], refs[:-1]
    batches, share, width = low_ref.shape
    arrays, outs = refs[:-batches], refs[-batches:]
    place = place_of("batch")
    rows = batches * share
    low_ref[...] = total_of(arrays, slice(0, rows)).reshape(batches, share, width)
    under = two_parts(one_part(total_of(arrays, slice(rows, rows + extra))))
    for m in range(batches):
        outs[m][:share, :] = low_ref[place ^ m].astype(outs[m].dtype)
        outs[m][share:, :] = under.astype(outs[m].dtype)


def cut(info, arrays, extra, after=()):
    batches = lax.axis_size("batch")
    rows, width = arrays[0].shape
    share = (rows - extra) // batches
    outs = [moved((share + extra, width), f32)] + [moved((share + extra, width), bf16)] * (batches - 1)
    scratch = [pltpu.VMEM((batches, share, width), f32)]
    return call(partial(cut_kernel, extra), info, arrays, (), (), outs, scratch, "cut", after, us=1.2)


def sum_kernel(info_ref, *refs):
    total = refs[0][...].astype(f32)
    for ref in refs[1:-1]:
        total += ref[...].astype(f32)
    rows = total.shape[0] - EXTRA
    refs[-1][:rows, :] = total[:rows].astype(bf16)
    refs[-1][rows:, :] = two_parts(one_part(total[rows:])).astype(bf16)


def sum_of(info, arrays, after=()):
    return call(sum_kernel, info, arrays, (), (), [moved(arrays[0].shape, bf16)], [], "total", after, us=0.6)


def join_kernel(info_ref, *refs):
    pieces, out_ref, low_ref = refs[:-2], refs[-2], refs[-1]
    batches, share, width = low_ref.shape
    place = place_of("batch")
    for m, ref in enumerate(pieces):
        low_ref[place ^ m] = ref[:share, :].astype(f32)
    rows = batches * share
    out_ref[:rows, :] = low_ref[...].reshape(rows, width).astype(bf16)
    out_ref[rows:, :] = pieces[0][share:, :]


def join(info, arrays, extra, after=()):
    batches = len(arrays)
    rows, width = arrays[0].shape
    share = rows - extra
    outs = [moved((batches * share + extra, width), bf16)]
    scratch = [pltpu.VMEM((batches, share, width), f32)]
    return call(join_kernel, info, arrays, (), (), outs, scratch, "join", after, us=0.6)


def trade(x, axis, mask):
    size = lax.axis_size(axis)
    return lax.ppermute(x, axis, [(i, i ^ mask) for i in range(size)])


def sent(arrays, axis, masks):
    return [arrays[0]] + [trade(x, axis, m) for x, m in zip(arrays[1:], masks)]


def to_others(x, axis, masks):
    return [x] + [trade(x, axis, m) for m in masks]


def gate_kernel(*refs):
    pass


def gate(info, arrays, after):
    anywhere = pl.BlockSpec(memory_space=pl.ANY)
    outs = [(anywhere, jax.ShapeDtypeStruct(x.shape, x.dtype)) for x in arrays]
    aliases = {1 + i: i for i in range(len(arrays))}
    return run(gate_kernel, info, list(arrays), [anywhere] * len(arrays), outs, [], "gate", after, aliases)


def small_grads(norms, rows, decay_log, phase_log, refs):
    gain_ref, shift_ref, decay_grad_ref, phase_grad_ref, skip_grad_ref, bias_grad_ref = refs
    blocks, states = decay_log.shape
    width = norms[0].shape[1]
    for k in range(blocks):
        gain_ref[k : k + 1, :], shift_ref[k : k + 1, :] = norms[k][0:1], norms[k][1:2]
        low, high = rows[k]
        skip, bias_low, bias_high, lam, scale = low[0:1], low[1:2], low[2:3], high[0:1], high[1:2]
        skip_grad_ref[k : k + 1, :] = skip
        bias_grad_ref[k : k + 1, :width] = bias_low
        bias_grad_ref[k : k + 1, width:] = bias_high
        rate, angle = jnp.exp(decay_log[k : k + 1]), jnp.exp(phase_log[k : k + 1])
        size, fade = jnp.exp(-rate), jnp.exp(-2.0 * rate)
        lam_real, lam_imag = size * jnp.cos(angle), size * jnp.sin(angle)
        real, imag = lam[:, :states], lam[:, states : 2 * states]
        by_rate = scale[:, :states] * fade * lax.rsqrt(1.0 - fade) - (real * lam_real + imag * lam_imag)
        decay_grad_ref[k : k + 1, :] = rate * by_rate
        phase_grad_ref[k : k + 1, :] = angle * (imag * lam_real - real * lam_imag)


def input_grad(where, sums, stats_ref, gain_ref, tokens_ref, wide_ref, grad_ref):
    seqs, span, width = tokens_ref.shape
    shuffle = shuffle_matrix(span, True)
    average, root = stats_ref[0:1, :], stats_ref[1:2, :]
    factor = root * gain_ref[0:1, :] / stats_ref[2:3, 0:1]
    by_gain = factor * sums[0:1] * root
    fixed = factor * sums[1:2] - by_gain * average
    step = lax.broadcasted_iota(jnp.int32, (span, 1), 0)
    for s in range(seqs):
        valid = (step < where.lefts[s]).astype(f32)
        ahead = dot(shuffle, wide_ref[:, s].reshape(span, width).astype(bf16))
        grad_ref[s] = (ahead - valid * (fixed + by_gain * tokens_ref[s].astype(f32))).astype(bf16)


def results_kernel(chips, info_ref, sums_ref, norm1_ref, decay_ref, phase_ref, stats_ref, gain_ref, *refs):
    (tokens_in, ahead_in), pieces, refs = refs[:2], refs[2 : 2 + 4 * chips], refs[2 + 4 * chips :]
    glu_ref, mix_ref, lift_ref, grad_out, *small_refs = refs[:10]
    low_ref, under_ref, wide_ref, tokens_ref, ahead_ref, rows_ref, grad_ref, in_sems, sems, own_sems = refs[10:]
    own = [
        pltpu.make_async_copy(ahead_in, ahead_ref, own_sems.at[0]),
        pltpu.make_async_copy(tokens_in, tokens_ref, own_sems.at[1]),
    ]
    place = place_of("seq")
    core = lax.axis_index("seq") % 2
    _, rows, width = wide_ref.shape
    half, quarter = rows // 2, rows // 4
    arriving = []
    for n, piece in enumerate(pieces):
        parts = [pltpu.make_async_copy(piece.at[pl.ds(0, rows), :], low_ref.at[n], in_sems.at[n, 0])]
        parts.append(pltpu.make_async_copy(piece.at[pl.ds(rows, EXTRA), :], under_ref.at[n], in_sems.at[n, 1]))
        begin(parts)
        arriving.append(parts)
    begin(own)
    copies = []
    extras = [[jnp.zeros((EXTRA // 2, width), f32)] * 2 for _ in range(2)]
    for n in range(4 * chips):
        finished(arriving[n])
        k, n_in = divmod(n, 2 * chips)
        chip, side = place ^ (n_in % chips), core if n_in < chips else 1 - core
        extra = one_part(under_ref[n].astype(f32))
        extras[k][n_in // chips] = jnp.where(chip == 0, extra, extras[k][n_in // chips])
        column = pl.multiple_of(side * width, width)
        row = pl.multiple_of(chip * half, 8)
        low = pl.multiple_of(side * (quarter * chips) + chip * quarter, 8)
        wide_ref[n] = low_ref[n].astype(f32)
        for i, (first, size, target) in enumerate(
            (
                (0, half, glu_ref.at[k, pl.ds(row, half), pl.ds(column, width)]),
                (half, quarter, mix_ref.at[k, pl.ds(low, quarter), :]),
                (half + quarter, quarter, lift_ref.at[k, pl.ds(low, quarter), :]),
            )
        ):
            copies.append(pltpu.make_async_copy(wide_ref.at[n, pl.ds(first, size), :], target, sems.at[n, i]))
            copies[-1].start()
    even = core == 0
    sums = sums_ref[...]
    finished(own)
    rows_ref[...] = ahead_ref[...].astype(f32).reshape(rows_ref.shape)
    seqs, span, _ = tokens_ref.shape
    input_grad(Where(info_ref, seqs, span), sums, stats_ref, gain_ref, tokens_ref, rows_ref, grad_ref)
    copies.append(pltpu.make_async_copy(grad_ref, grad_out, own_sems.at[2]))
    copies[-1].start()
    small_grads(
        (sums, norm1_ref[...]),
        [(jnp.where(even, mine, other), jnp.where(even, other, mine)) for mine, other in extras],
        decay_ref[...],
        phase_ref[...],
        small_refs,
    )
    finished(copies)


def results(info, sums, norm1, decay_log, phase_log, stats, gain, tokens, ahead, pieces, after=()):
    seqs, span, _ = tokens.shape
    rows, width = pieces[0].shape
    rows -= EXTRA
    count = len(pieces)
    anywhere = pl.BlockSpec(memory_space=pl.ANY)
    shapes = [(2, width, 2 * width), (2, width, width), (2, width, width)]
    outs = [(anywhere, jax.ShapeDtypeStruct(shape, f32)) for shape in shapes]
    outs.append((anywhere, jax.ShapeDtypeStruct(tokens.shape, bf16)))
    blocks, states = decay_log.shape
    outs += [moved((blocks, n), f32) for n in (width, width, states, states, width, 2 * width)]
    scratch = [
        pltpu.VMEM((count, rows, width), bf16),
        pltpu.VMEM((count, EXTRA, width), bf16),
        pltpu.VMEM((count, rows, width), f32),
        pltpu.VMEM(tokens.shape, bf16),
        pltpu.VMEM(ahead.shape, bf16),
        pltpu.VMEM((span // CHUNKS, seqs, CHUNKS, width), f32),
        pltpu.VMEM(tokens.shape, bf16),
        pltpu.SemaphoreType.DMA((count, 2)),
        pltpu.SemaphoreType.DMA((count, 3)),
        pltpu.SemaphoreType.DMA((3,)),
    ]
    inputs = [sums, norm1, decay_log, phase_log, stats, gain]
    given = [*inputs, *map(there, (tokens, ahead)), *pieces]
    specs = [in_vmem] * len(inputs) + [in_hbm] * 2 + [anywhere] * count
    return run(partial(results_kernel, count // 4), info, given, specs, outs, scratch, "results", after, us=7.0)


def norms_kernel(info_ref, sums_ref, total_ref):
    total_ref[...] = jnp.sum(sums_ref[...], axis=0)


def norms(info, sums, after=()):
    outs = [moved(sums.shape[1:], f32)]
    return call(norms_kernel, info, (sums,), (), (), outs, [], "norms", after, us=0.6)


def leave_kernel(seqs, info_ref, rows_ref, out_ref, wide_ref):
    _, span, width = out_ref.shape
    wide_ref[...] = rows_ref[...].astype(f32).reshape(wide_ref.shape)
    shuffle = shuffle_matrix(span, True)
    for s in range(seqs):
        out_ref[s] = dot(shuffle, wide_ref[:, s].reshape(span, width).astype(bf16)).astype(bf16)


def leave(info, rows, seqs, after=()):
    span, width = rows.shape[0] // seqs, rows.shape[1]
    scratch = [pltpu.VMEM((span // CHUNKS, seqs, CHUNKS, width), f32)]
    outs = [moved((seqs, span, width), bf16)]
    return call(partial(leave_kernel, seqs), info, (rows,), (), (), outs, scratch, "leave", after)


def to_all(x, axes):
    return lax.all_to_all(x, axes, split_axis=0, concat_axis=0, tiled=True)


def local(
    tokens,
    lengths,
    cotangent,
    norm_gain,
    norm_shift,
    lift_weight,
    decay_log,
    phase_log,
    skip_gain,
    mix_weight,
    glu_weight,
    glu_bias,
):
    both = ("seq", "batch")
    seq_devices, batches = lax.axis_size("seq"), lax.axis_size("batch")
    devices, chips = seq_devices * batches, seq_devices // 2
    seqs, span, width = tokens.shape
    rows = seqs * span
    info = lengths
    turns = (decay_log, phase_log)
    norms_in = (norm_gain, norm_shift)
    states = decay_log.shape[1]
    half = width // 2

    sums, tokens_here, lift_w = enter(info, tokens, devices, [(lift_weight, 0)])
    sums = to_all(sums, both)
    normed, lifted, ends, part, stats0, x, mix_w, glu_w = lift(
        0, seqs, seq_devices, info, (sums, *norms_in, *turns), (tokens_here, lift_w), rows,
        [(mix_weight, 0), (glu_weight, 0)],
    )
    x1, sums, kept, lift_w, normed0 = mix(
        0, info, (to_all(part, "seq"), skip_gain, glu_bias, *turns), (ends, lifted, normed, x, mix_w, glu_w),
        devices, [(lift_weight, 1)], (normed,),
    )
    sums = to_all(sums, both)

    normed1, lifted1, ends, part, stats1, mix_w, glu_w = lift(
        1, seqs, seq_devices, info, (sums, *norms_in, *turns, stats0), (x1, lift_w), rows,
        [(mix_weight, 1), (glu_weight, 1)],
    )
    state1, activated1, slope1, gate1, gate_slope1, masked, cot = mix(
        1, info, (to_all(part, "seq"), skip_gain, glu_bias, *turns), (ends, lifted1, normed1, x1, mix_w, glu_w),
        devices, [(cotangent, None)],
    )

    glu_packed, bias_grad1, skip_grad1, ends, part, lift_w, masked = glu_back(
        1, seqs, seq_devices, info, turns, (cot, normed1, slope1, gate1, gate_slope1, glu_w, mix_w), (), rows, width,
        (), [(lift_weight, 1)], [masked],
    )
    lift_packed, sums, lam_grad1, scale_grad1 = lift_back(
        1, info, (to_all(part, "seq"), stats1, skip_gain, *turns, *norms_in),
        (ends, glu_packed, normed1, state1, lift_w), devices,
    )
    glu_part, mix_part, lift_part = (0, width, (0, 0), (0, width)), (1, half, (0, 0), (half, 0)), (2, half, (0, 0), (half, 0))
    glu_lanes, lift_lanes = glu_pack(width, 2 * states).lanes, lift_pack(width, 2 * states).lanes
    kept_lanes, every = kept_pack(width, 2 * states).lanes, slice(None)
    out = halves(
        info,
        (glu_part, mix_part, lift_part),
        (
            ((0, every), (1, glu_lanes["projected"])),
            ((2, every), (1, glu_lanes["mixed"])),
            ((3, every), (4, lift_lanes["lifted"])),
        ),
        (skip_grad1, bias_grad1, lam_grad1, scale_grad1),
        (activated1, glu_packed, state1, normed1, lift_packed),
        width,
        "halves1",
    )
    keep1, send = out
    got1 = trade(send, "seq", 1)
    (produced,) = out = leave(info, masked, seqs, (out.tick,))
    shares = (width, half, half)
    z, xy = range(1, batches), range(2, seq_devices, 2)
    extra = EXTRA * chips
    out = split(info, ((*shares, extra),), [keep1, got1], True, (out.tick,))
    pieces1 = sent(out, "seq", xy)
    sums = to_all(sums, both)

    state_lanes = (slice(None), kept_lanes["state"])
    out = glu_back(
        0, seqs, seq_devices, info, (*turns, sums, stats1, *norms_in), (lift_packed,),
        (kept, normed0, glu_weight, mix_weight), rows, width, (),
        [(kept, state_lanes), (lift_weight, 0)],
    )
    glu_packed, bias_grad0, skip_grad0, ends, part, norm_sums1, normed, state, lift_w = out
    activated_lanes = (slice(None), kept_lanes["activated"])
    parts, *pieces1 = gate(info, [to_all(part, "seq"), *pieces1], ())
    back_lifted0, sums, lam_grad0, scale_grad0, ahead, activated = out = lift_back(
        0, info, (parts, stats0, skip_gain, *turns, *norms_in),
        (ends, glu_packed, normed, state, lift_w), devices, (), [(kept, activated_lanes)],
    )

    keep0, send = out = halves(
        info,
        (glu_part, mix_part, lift_part),
        (
            ((0, every), (1, glu_lanes["projected"])),
            ((2, every), (1, glu_lanes["mixed"])),
            ((3, every), (4, every)),
        ),
        (skip_grad0, bias_grad0, lam_grad0, scale_grad0),
        (activated, glu_packed, state, normed, back_lifted0),
        width,
        "halves0",
    )
    got0 = trade(send, "seq", 1)
    out1 = cut(info, pieces1, EXTRA, (out.tick,))
    out0 = split(info, ((*shares, extra),), [keep0, got0], True, (out1.tick,))
    (sums,) = gate(info, [sums], (out0.tick,))
    sums = to_all(sums, both)
    sum1 = sum_of(info, sent(out1, "batch", z), (out0.tick,))
    (own1,) = out = join(info, to_others(sum1[0], "batch", z), EXTRA, (sum1.tick,))
    out0 = cut(info, sent(out0, "seq", xy), EXTRA, (out.tick,))
    (sums,) = out = norms(info, sums, (out0.tick,))
    sum0 = sum_of(info, sent(out0, "batch", z), (out.tick,))
    (own0,) = join(info, to_others(sum0[0], "batch", z), EXTRA)
    pieces = []
    for own in (own0, own1):
        total = to_others(own, "seq", xy)
        pieces += total + [trade(x, "seq", 1) for x in total]
    out = results(info, sums, norm_sums1, *turns, stats0, norm_gain, tokens, ahead, pieces)
    grad_glu, grad_mix, grad_lift, tokens_grad, grad_gain, grad_shift, grad_decay, grad_phase, grad_skip, grad_bias = out
    return (
        produced,
        tokens_grad,
        grad_gain,
        grad_shift,
        grad_lift,
        grad_decay,
        grad_phase,
        grad_skip,
        grad_mix,
        grad_glu,
        grad_bias,
    )


def solution(mesh):
    split = P("batch", "seq", None)
    placed = (split, P("batch"), split) + (P(),) * 9
    return jax.shard_map(
        local,
        mesh=mesh,
        in_specs=placed,
        out_specs=(split, split) + (P(),) * 9,
        check_vma=False,
    )
```

```python
from functools import partial

import jax
import jax.numpy as jnp
from jax import lax
from jax.experimental import pallas as pl
from jax.experimental.pallas import tpu as pltpu
from jax.sharding import PartitionSpec as P

norm_eps = 1e-05
f32 = jnp.float32
bf16 = jnp.bfloat16

CHUNKS = 8
BLOCKS = 4
BACK_BLOCKS = 2
PARTS = 1
EXTRA = 16
LANES = 128
VMEM_LIMIT = 32 * 1024 * 1024

in_vmem = pl.BlockSpec(memory_space=pltpu.VMEM)
in_smem = pl.BlockSpec(memory_space=pltpu.SMEM)
in_hbm = pl.BlockSpec(memory_space=pltpu.HBM)


def near(shape, dtype):
    return in_vmem, pltpu.VMEM(shape, dtype)


def moved(shape, dtype):
    return in_vmem, jax.ShapeDtypeStruct(shape, dtype)


def copy_parts(source, target, sems):
    size = source.shape[0] // sems.shape[0]
    cuts = [pl.ds(i * size, size) for i in range(sems.shape[0])]
    return [pltpu.make_async_copy(source.at[cut], target.at[cut], sems.at[i]) for i, cut in enumerate(cuts)]


def begin(copies):
    for copy in copies:
        copy.start()


def finished(copies):
    for copy in copies:
        copy.wait()


class Outs(list):
    tick = None


def run(body, info, given, specs, outs, scratch, name, after, aliases=(), us=None):
    cost = None
    if us is not None:
        cost = pl.CostEstimate(flops=int(us * 1.1e9), bytes_accessed=int(us * 3e6), transcendentals=0)
    after = [pltpu.with_memory_space_constraint(t, pltpu.HBM) for t in after]
    n_in, n_out = 1 + len(given), len(outs)

    def ticking(*refs):
        body(*refs[:n_in], *refs[n_in + len(after) : n_in + len(after) + n_out], *refs[n_in + len(after) + n_out + 1 :])

    out = pl.pallas_call(
        ticking,
        in_specs=[in_smem] + specs + [in_hbm] * len(after),
        out_specs=[spec for spec, _ in outs] + [in_hbm],
        out_shape=[shape for _, shape in outs] + [pltpu.HBM((8, LANES), f32)],
        scratch_shapes=scratch,
        input_output_aliases=dict(aliases),
        compiler_params=pltpu.CompilerParams(vmem_limit_bytes=VMEM_LIMIT),
        cost_estimate=cost,
        name=name,
    )(info, *given, *after)
    result = Outs(out[:n_out])
    result.tick = out[n_out]
    return result


def here(x):
    return pltpu.with_memory_space_constraint(x, pltpu.VMEM)


def there(x):
    return pltpu.with_memory_space_constraint(x, pltpu.HBM)


def call(kernel, info, inputs, arrays, away, outs, scratch, name, after=(), fetch=(), spill=(), us=None):
    first = 1 + len(inputs) + len(arrays) + len(away)
    n_copies = len(fetch) + len(spill)
    fetched = [jax.eval_shape(lambda x, at=at: x if at is None else x[at], a) for a, at in fetch]
    outs = list(outs)
    n_outs = len(outs)
    outs += [near(a.shape, a.dtype) for a in fetched] + [(in_hbm, pltpu.HBM(a.shape, a.dtype)) for a in spill]

    def body(*refs):
        ins, rest = refs[: first + n_copies], refs[first + n_copies :]
        sources = list(ins[first:])
        for i, (_, at) in enumerate(fetch):
            if at is not None:
                sources[i] = sources[i].at[at]
        targets = rest[n_outs : n_outs + n_copies]
        rest = rest[:n_outs] + rest[n_outs + n_copies :]
        copies = []
        for i, (x, y) in enumerate(zip(sources, targets)):
            copies += copy_parts(x, y, rest[-1].at[i])
        begin(copies)
        kernel(*ins[:first], *(rest[:-1] if copies else rest))
        finished(copies)

    given = [*inputs, *map(here, arrays), *map(there, away), *(there(a) for a, _ in fetch), *map(here, spill)]
    specs = [in_vmem] * (len(inputs) + len(arrays)) + [in_hbm] * (len(away) + len(fetch)) + [in_vmem] * len(spill)
    scratch = list(scratch) + [pltpu.SemaphoreType.DMA((n_copies, PARTS))] * bool(n_copies)
    return run(body, info, given, specs, outs, scratch, name, after, us=us)


class Pack:
    def __init__(self, *fields):
        self.lanes, self.width = {}, 0
        for name, width in fields:
            self.lanes[name] = slice(self.width, self.width + width)
            self.width += width

    def views(self, ref, *names):
        return [ref.at[:, self.lanes[n]] for n in names]


def kept_pack(width, states):
    return Pack(*((n, width) for n in ("slope", "gate", "gate_slope", "activated")), ("state", states))


def glu_pack(width, states):
    return Pack(("projected", 2 * width), ("mixed", width), ("dh", states), ("back", width))


def lift_pack(width, states):
    return Pack(("lifted", states), ("back_normed", width), ("back", width), ("normed", width))


def wide(mask, width):
    return jnp.concatenate([mask] * (width // LANES), axis=1)


def dot(a, b):
    return lax.dot_general(a, b, (((1,), (0,)), ((), ())), preferred_element_type=f32)


def dot_t(a, b):
    return lax.dot_general(a, b, (((1,), (1,)), ((), ())), preferred_element_type=f32)


def t_dot(a, b):
    return lax.dot_general(a, b, (((0,), (0,)), ((), ())), preferred_element_type=f32)


def cmul(ar, ai, br, bi):
    return ar * br - ai * bi, ar * bi + ai * br


def order(steps, reverse):
    return range(steps - 1, -1, -1) if reverse else range(steps)


def shuffle_matrix(span, back):
    chunk = span // CHUNKS
    place = lax.broadcasted_iota(jnp.int32, (span, span), 0)
    source = lax.broadcasted_iota(jnp.int32, (span, span), 1)
    if back:
        wanted = (place % chunk) * CHUNKS + place // chunk
    else:
        wanted = (place % CHUNKS) * chunk + place // CHUNKS
    return (source == wanted).astype(f32).astype(bf16)


class Where:
    def __init__(self, info_ref, seqs, span):
        self.seq = lax.axis_index("seq")
        self.seqs, self.span = seqs, span
        self.lengths = [info_ref[s] for s in range(seqs)]
        self.lefts = [length - self.seq * span for length in self.lengths]

    def steps_left(self):
        before = (self.span // CHUNKS) * lax.broadcasted_iota(jnp.int32, (CHUNKS, LANES), 0)
        return jnp.concatenate([left - before for left in self.lefts], axis=0)


def valid_rows(left, first, steps):
    return jnp.concatenate([(left > first + t).astype(f32) for t in range(steps)], axis=0)


def shuffle_rows(wide_ref, source_ref):
    steps, seqs, chunks, width = wide_ref.shape
    shuffle = shuffle_matrix(steps * chunks, False)
    for s in range(seqs):
        wide_ref[:, s] = dot(shuffle, source_ref[s]).reshape(steps, chunks, width)


def enter_kernel(info_ref, tokens_ref, sums_ref, here_ref, acc_ref, sems):
    seqs, span, width = tokens_ref.shape
    copies = [copy_parts(tokens_ref.at[s], here_ref.at[s], sems.at[s]) for s in range(seqs)]
    for parts in copies:
        begin(parts)
    where = Where(info_ref, seqs, span)
    step = lax.broadcasted_iota(jnp.int32, (span, 1), 0)
    total = jnp.zeros((1, width), f32)
    squares = jnp.zeros((1, width), f32)
    count = jnp.zeros((1, 1), f32)
    for s in range(seqs):
        valid = (step < where.lefts[s]).astype(f32)
        finished(copies[s])
        x = here_ref[s].astype(f32)
        masked = x * valid
        total += jnp.sum(masked, axis=0, keepdims=True)
        squares += jnp.sum(masked * x, axis=0, keepdims=True)
        count += jnp.sum(valid, axis=0, keepdims=True)
    tail = jnp.broadcast_to(count, (1, LANES))
    acc_ref[0:1, :] = jnp.concatenate([total, tail], axis=1)
    acc_ref[1:2, :] = jnp.concatenate([squares, tail], axis=1)
    for j in range(sums_ref.shape[0]):
        sums_ref[j] = acc_ref[...]


def enter(info, tokens, devices, fetch):
    seqs, _, width = tokens.shape
    outs = [moved((devices, 2, width + LANES), f32), near(tokens.shape, bf16)]
    scratch = [pltpu.VMEM((2, width + LANES), f32), pltpu.SemaphoreType.DMA((seqs, 1))]
    return call(enter_kernel, info, (), (), (tokens,), outs, scratch, "enter", fetch=fetch)


class Powers:
    @staticmethod
    def scratch(seqs, seq_devices, states, leaps):
        tables = [((1, 2 * states), f32), ((1, states), f32), ((2 * states // LANES, seqs * CHUNKS, LANES), f32)]
        if leaps:
            tables.append(((seq_devices * seqs, 2 * states), f32))
        return [pltpu.VMEM(*t) for t in tables]

    def __init__(self, k, back, where, decay_ref, phase_ref, lam_ref, scale_ref, table_ref, leap_ref=None):
        states = scale_ref.shape[1]
        groups, group = states // LANES, table_ref.shape[1]
        seqs, span, limit = where.seqs, where.span, where.span // CHUNKS
        rate = jnp.exp(decay_ref[k : k + 1, :])
        size, angle = jnp.exp(-rate), jnp.exp(phase_ref[k : k + 1, :])
        lam_ref[:, :states] = size * jnp.cos(angle)
        lam_ref[:, states:] = size * jnp.sin(angle) * (-1.0 if back else 1.0)
        scale_ref[...] = jnp.sqrt(1.0 - jnp.exp(-2.0 * rate))
        self.lam, self.scale, self.table, self.leaps = lam_ref, scale_ref, table_ref, leap_ref
        shift = 0 if not back else (-1 if k == 0 else 1)
        chunk_count = jnp.clip(where.steps_left() + shift, 0, limit)
        if leap_ref is not None:
            total = leap_ref.shape[0]
            line = lax.broadcasted_iota(jnp.int32, (total, LANES), 0)
            span_left = jnp.zeros((total, LANES), jnp.int32)
            for s, length in enumerate(where.lengths):
                span_left = jnp.where(line % seqs == s, length - span * (line // seqs), span_left)
            span_count = jnp.clip(span_left + shift, 0, span)
        for low in range(groups):
            real_lanes = slice(low * LANES, (low + 1) * LANES)
            imag_lanes = slice((groups + low) * LANES, (groups + low + 1) * LANES)
            br, bi = lam_ref[:, real_lanes], lam_ref[:, imag_lanes]
            cr = jnp.ones((group, LANES), f32)
            ci = jnp.zeros((group, LANES), f32)
            if leap_ref is not None:
                pr = jnp.ones((total, LANES), f32)
                pi = jnp.zeros((total, LANES), f32)
            for bit in range((limit if leap_ref is None else span).bit_length()):
                if (1 << bit) <= limit:
                    nr, ni = cmul(cr, ci, br, bi)
                    odd = (chunk_count & (1 << bit)) != 0
                    cr, ci = jnp.where(odd, nr, cr), jnp.where(odd, ni, ci)
                if leap_ref is not None:
                    nr, ni = cmul(pr, pi, br, bi)
                    odd = (span_count & (1 << bit)) != 0
                    pr, pi = jnp.where(odd, nr, pr), jnp.where(odd, ni, pi)
                br, bi = cmul(br, bi, br, bi)
            table_ref[low] = cr
            table_ref[groups + low] = ci
            if leap_ref is not None:
                leap_ref[:, real_lanes] = pr
                leap_ref[:, imag_lanes] = pi


def stretch_part(ends_ref, power_ref, reverse, seqs):
    groups = ends_ref.shape[0] // 2
    reals, imags = [], []
    for low in range(groups):
        real = jnp.zeros((seqs, LANES), f32)
        imag = jnp.zeros((seqs, LANES), f32)
        for c in order(CHUNKS, reverse):
            here = pl.ds(c, seqs, stride=CHUNKS)
            real, imag = cmul(power_ref[low, here, :], power_ref[groups + low, here, :], real, imag)
            real += ends_ref[low, here, :]
            imag += ends_ref[groups + low, here, :]
        reals.append(real)
        imags.append(imag)
    return jnp.concatenate(reals + imags, axis=1)


def chunk_starts(start_ref, place, parts_ref, leaps_ref, ends_ref, power_ref, reverse):
    devices, seqs, width = parts_ref.shape
    states = width // 2
    groups = states // LANES
    real = jnp.zeros((seqs, states), f32)
    imag = jnp.zeros((seqs, states), f32)
    for j in order(devices, reverse):
        ahead = (j > place) if reverse else (j < place)
        leap, part = leaps_ref[seqs * j : seqs * (j + 1), :], parts_ref[j]
        next_real, next_imag = cmul(leap[:, :states], leap[:, states:], real, imag)
        real = jnp.where(ahead, next_real + part[:, :states], real)
        imag = jnp.where(ahead, next_imag + part[:, states:], imag)
    for low in range(groups):
        hr = real[:, low * LANES : (low + 1) * LANES]
        hi = imag[:, low * LANES : (low + 1) * LANES]
        for c in order(CHUNKS, reverse):
            here = pl.ds(c, seqs, stride=CHUNKS)
            start_ref[low, here, :] = hr
            start_ref[groups + low, here, :] = hi
            hr, hi = cmul(power_ref[low, here, :], power_ref[groups + low, here, :], hr, hi)
            hr += ends_ref[low, here, :]
            hi += ends_ref[groups + low, here, :]


def scan_block(h_ref, drive, left, lam, shift, first, steps, reverse, out_ref=None):
    groups, group, _ = h_ref.shape
    groups = groups // 2
    masks = [left > first + t + shift for t in range(steps)]
    for low in range(groups):
        real_lanes = slice(low * LANES, (low + 1) * LANES)
        imag_lanes = slice((groups + low) * LANES, (groups + low + 1) * LANES)
        hr, hi = h_ref[low], h_ref[groups + low]
        lr, li = lam[:, real_lanes], lam[:, imag_lanes]
        for t in order(steps, reverse):
            ur, ui = drive(t, real_lanes, imag_lanes)
            nr, ni = cmul(lr, li, hr, hi)
            hr = jnp.where(masks[t], nr, hr) + ur
            hi = jnp.where(masks[t], ni, hi) + ui
            if out_ref is not None:
                out_ref[t * group : (t + 1) * group, real_lanes] = hr
                out_ref[t * group : (t + 1) * group, imag_lanes] = hi
        h_ref[low] = hr
        h_ref[groups + low] = hi


def input_drive(lifted, scale, left, first, steps):
    group = left.shape[0]
    masks = [left > first + t for t in range(steps)]

    def drive(t, real_lanes, imag_lanes):
        here = slice(t * group, (t + 1) * group)
        factor = jnp.where(masks[t], scale[:, real_lanes], 0.0)
        return factor * lifted[here, real_lanes], factor * lifted[here, imag_lanes]

    return drive


def blocks_of(rows, group, reverse, blocks=BLOCKS):
    size = rows // blocks
    for block in order(blocks, reverse):
        yield block, block * (size // group), slice(block * size, (block + 1) * size)


def lift_kernel(k, seqs, info_ref, sums_ref, gain_ref, shift_ref, decay_ref, phase_ref, *refs):
    reverse = k == 1
    if k == 0:
        x_ref, weight_ref, normed_ref, lifted_ref, ends_ref, part_ref, stats_ref, rows_ref, wide_ref = refs[:9]
        refs = refs[9:]
    else:
        count_ref, x_ref, weight_ref, normed_ref, lifted_ref, ends_ref, part_ref, stats_ref = refs[:8]
        refs = refs[8:]
    rows, width = normed_ref.shape
    group = ends_ref.shape[1]
    size = rows // BLOCKS
    steps = size // group
    where = Where(info_ref, seqs, rows // seqs)
    powers = Powers(k, False, where, decay_ref, phase_ref, *refs)
    if k == 0:
        shuffle_rows(wide_ref, x_ref)
    sums = jnp.sum(sums_ref[...], axis=0)
    if k == 0:
        count = sums[0:1, width : width + 1]
    else:
        count = count_ref[2:3, 0:1]
    average = sums[0:1, :width] / count
    root = lax.rsqrt(sums[1:2, :width] / count - average * average + norm_eps)
    stats_ref[0:1, :] = average
    stats_ref[1:2, :] = root
    stats_ref[2:3, :] = jnp.broadcast_to(count, (1, width))
    gain, shift = gain_ref[k : k + 1, :], shift_ref[k : k + 1, :]
    lam, scale = powers.lam[...], powers.scale[...]
    left = where.steps_left()
    ends_ref[...] = jnp.zeros_like(ends_ref)
    for _, first, now in blocks_of(rows, group, reverse):
        if k == 0:
            x = wide_ref[first : first + steps].reshape(size, width)
            rows_ref[now, :] = x.astype(bf16)
        else:
            x = x_ref[now, :]
        normed = ((x - average) * root * gain + shift).astype(bf16)
        normed_ref[now, :] = normed
        lifted = dot(normed, weight_ref[...]).astype(bf16)
        lifted_ref[now, :] = lifted
        drive = input_drive(lifted.astype(f32), scale, left, first, steps)
        scan_block(ends_ref, drive, left, lam, 0, first, steps, reverse)
    part = stretch_part(ends_ref, powers.table, reverse, seqs)
    for j in range(part_ref.shape[0]):
        part_ref[j] = part


def lift(k, seqs, seq_devices, info, inputs, arrays, rows, fetch):
    gain, decay = inputs[1], inputs[3]
    width, states = gain.shape[1], decay.shape[1]
    outs = [
        near((rows, width), bf16),
        near((rows, 2 * states), bf16),
        near((2 * states // LANES, seqs * CHUNKS, LANES), f32),
        moved((seq_devices, seqs, 2 * states), f32),
        moved((8, width), f32),
    ]
    scratch = []
    if k == 0:
        outs.append(near((rows, width), bf16))
        scratch.append(pltpu.VMEM((rows // seqs // CHUNKS, seqs, CHUNKS, width), f32))
    scratch += Powers.scratch(seqs, seq_devices, states, False)
    return call(partial(lift_kernel, k, seqs), info, inputs, arrays, (), outs, scratch, "lift", fetch=fetch)


def mix_kernel(k, info_ref, parts_ref, skip_ref, bias_ref, decay_ref, phase_ref, *refs):
    reverse = k == 1
    (ends_ref, lifted_ref, normed_ref, x_ref, mix_ref, glu_ref) = refs[:6]
    tables, refs = refs[-4:], refs[6:-4]
    if reverse:
        state_ref, activated_ref, slope_ref, gate_ref, gate_slope_ref, masked_ref, h_ref, states_ref = refs
    else:
        next_ref, sums_ref, kept_out, h_ref, states_ref, acc_ref, kept_ref, sems = refs
        pack = kept_pack(x_ref.shape[1], lifted_ref.shape[1])
        state_ref, activated_ref, slope_ref, gate_ref, gate_slope_ref = pack.views(
            kept_ref, "state", "activated", "slope", "gate", "gate_slope"
        )
        copies = []
    seqs = parts_ref.shape[1]
    rows, width = x_ref.shape
    group = ends_ref.shape[1]
    steps = rows // BLOCKS // group
    where = Where(info_ref, seqs, rows // seqs)
    powers = Powers(k, False, where, decay_ref, phase_ref, *tables)
    chunk_starts(h_ref, where.seq, parts_ref, powers.leaps, ends_ref, powers.table, reverse)
    left = where.steps_left()
    skip, bias = skip_ref[k : k + 1, :], bias_ref[k : k + 1, :]
    lam, scale = powers.lam[...], powers.scale[...]
    total = jnp.zeros((1, width), f32)
    squares = jnp.zeros((1, width), f32)
    for block, first, now in blocks_of(rows, group, reverse):
        drive = input_drive(lifted_ref[now, :].astype(f32), scale, left, first, steps)
        scan_block(h_ref, drive, left, lam, 0, first, steps, reverse, states_ref)
        state = states_ref[...].astype(bf16)
        state_ref[now, :] = state
        mixed = dot(state, mix_ref[...]) + skip * normed_ref[now, :].astype(f32)
        base, cube = 0.7978845608028654, 0.044715
        square = mixed * mixed
        bend = jnp.tanh(mixed * (base + (base * cube) * square))
        half = 0.5 + 0.5 * bend
        activated = (mixed * half).astype(bf16)
        activated_ref[now, :] = activated
        slope_ref[now, :] = (
            half + mixed * (half - half * half) * (2.0 * base + (6.0 * base * cube) * square)
        ).astype(bf16)
        projected = dot(activated, glu_ref[...]) + bias
        gate = 0.5 + 0.5 * jnp.tanh(0.5 * projected[:, width:])
        gated = projected[:, :width] * gate
        gate_ref[now, :] = gate.astype(bf16)
        gate_slope_ref[now, :] = (gated - gated * gate).astype(bf16)
        after = x_ref[now, :].astype(f32) + gated
        masked = after * wide(valid_rows(left, first, steps), width)
        if reverse:
            masked_ref[now, :] = masked.astype(bf16)
        else:
            next_ref[now, :] = after
            total += jnp.sum(masked, axis=0, keepdims=True)
            squares += jnp.sum(masked * after, axis=0, keepdims=True)
            parts = copy_parts(kept_ref.at[now, :], kept_out.at[now, :], sems.at[block])
            begin(parts)
            copies += parts
    if not reverse:
        acc_ref[0:1, :] = total
        acc_ref[1:2, :] = squares
        for j in range(sums_ref.shape[0]):
            sums_ref[j] = acc_ref[...]
        finished(copies)


def mix(k, info, inputs, arrays, devices, fetch, spill=()):
    parts = inputs[0]
    ends, lifted, _, x = arrays[:4]
    rows, width = x.shape
    states = lifted.shape[1]
    seq_devices, seqs, _ = parts.shape
    scratch = [pltpu.VMEM(ends.shape, f32), pltpu.VMEM((rows // BLOCKS, states), f32)]
    if k == 1:
        outs = [near((rows, states), bf16)] + [near((rows, width), bf16)] * 5
    else:
        kept = (rows, kept_pack(width, states).width)
        outs = [near((rows, width), f32), moved((devices, 2, width), f32), (in_hbm, pltpu.HBM(kept, bf16))]
        scratch += [pltpu.VMEM((2, width), f32), pltpu.VMEM(kept, bf16), pltpu.SemaphoreType.DMA((BLOCKS, 1))]
    scratch += Powers.scratch(seqs, seq_devices, states // 2, True)
    return call(
        partial(mix_kernel, k), info, inputs, arrays, (), outs, scratch, "mix", fetch=fetch, spill=spill
    )


def glu_back_kernel(k, seqs, info_ref, decay_ref, phase_ref, *refs):
    reverse = k == 0
    if k == 0:
        sums_ref, stats_ref, gain_ref, shift_ref, lift_pack_ref, kept_ref, normed_in, glu_in, mix_in = refs[:9]
        tables, refs = refs[-3:], refs[9:-3]
    else:
        start_ref, normed_ref, slope_ref, gate_ref, gate_slope_ref, glu_ref, mix_ref = refs[:7]
        tables, refs = refs[-3:], refs[7:-3]
    out_ref, bias_grad_ref, skip_grad_ref, ends_ref, part_ref = refs[:5]
    refs = refs[5:]
    rows, width = out_ref.shape[0], skip_grad_ref.shape[1]
    states = 2 * decay_ref.shape[1]
    names = ("projected", "mixed", "dh", "back")
    projected_ref, mixed_ref, dh_ref, back_ref = glu_pack(width, states).views(out_ref, *names)
    if k == 0:
        total_ref, normed_ref, slopes_ref, glu_ref, mix_ref, sems, weight_sems = refs
        pack = kept_pack(width, states)
        back_normed_ref, start_ref, later_ref = lift_pack(width, states).views(
            lift_pack_ref, "back_normed", "back", "normed"
        )
        slope_ref, gate_ref, gate_slope_ref = pack.views(slopes_ref, "slope", "gate", "gate_slope")
    group = ends_ref.shape[1]
    size = rows // BACK_BLOCKS
    steps = size // group
    where = Where(info_ref, seqs, rows // seqs)
    if k == 1:
        (wide_ref,) = refs
        shuffle_rows(wide_ref, start_ref)
    else:
        copies = {}
        for block, _, now in blocks_of(rows, group, reverse, BACK_BLOCKS):
            lanes = slice(0, 3 * width)
            copies[block] = copy_parts(kept_ref.at[now, lanes], slopes_ref.at[now, :], sems.at[0, block])
            copies[block] += copy_parts(normed_in.at[now, :], normed_ref.at[now, :], sems.at[1, block])
        weights = copy_parts(glu_in.at[k], glu_ref, weight_sems.at[0])
        weights += copy_parts(mix_in.at[k], mix_ref, weight_sems.at[1])
        for n, block in enumerate(order(BACK_BLOCKS, reverse)):
            begin(copies[block])
            if n == 0:
                begin(weights)
        sums = jnp.sum(sums_ref[...], axis=0)
        total_ref[...] = sums
        root, count = stats_ref[1:2, :], stats_ref[2:3, 0:1]
        gain, shift = gain_ref[1:2, :], shift_ref[1:2, :]
        by_normed = sums[0:1] / count
        fixed = (gain * sums[1:2] - shift * sums[0:1]) / count
    powers = Powers(k, True, where, decay_ref, phase_ref, *tables)
    left = where.steps_left()
    lam = powers.lam[...]
    ends_ref[...] = jnp.zeros_like(ends_ref)
    bias_grad = jnp.zeros((1, 2 * width), f32)
    skip_grad = jnp.zeros((1, width), f32)
    for block, first, now in blocks_of(rows, group, reverse, BACK_BLOCKS):
        valid = wide(valid_rows(left, first, steps), width)
        if k == 1:
            back = wide_ref[first : first + steps].reshape(size, width) * valid
        else:
            finished(copies[block])
            back = start_ref[now, :].astype(f32) + root * (
                gain * back_normed_ref[now, :].astype(f32)
                - valid * (fixed + by_normed * later_ref[now, :].astype(f32))
            )
        back_ref[now, :] = back.astype(bf16)
        value_back = (back * gate_ref[now, :].astype(f32)).astype(bf16)
        gate_back = (back * gate_slope_ref[now, :].astype(f32)).astype(bf16)
        back_projected = jnp.concatenate([value_back, gate_back], axis=1)
        projected_ref[now, :] = back_projected
        bias_grad += jnp.sum(back_projected.astype(f32), axis=0, keepdims=True)
        if k == 0 and block == BACK_BLOCKS - 1:
            finished(weights)
        back_activated = dot_t(back_projected, glu_ref[...])
        back_mixed = (slope_ref[now, :].astype(f32) * back_activated).astype(bf16)
        mixed_ref[now, :] = back_mixed
        skip_grad += jnp.sum(back_mixed.astype(f32) * normed_ref[now, :].astype(f32), axis=0, keepdims=True)
        back_state = dot_t(back_mixed, mix_ref[...]).astype(bf16)
        dh_ref[now, :] = back_state
        wide_state = back_state.astype(f32)

        def drive(t, real_lanes, imag_lanes):
            at = slice(t * group, (t + 1) * group)
            return wide_state[at, real_lanes], wide_state[at, imag_lanes]

        shift = 1 if reverse else -1
        scan_block(ends_ref, drive, left, lam, shift, first, steps, reverse)
    bias_grad_ref[...] = bias_grad
    skip_grad_ref[...] = skip_grad
    part = stretch_part(ends_ref, powers.table, reverse, seqs)
    for j in range(part_ref.shape[0]):
        part_ref[j] = part


def glu_back(k, seqs, seq_devices, info, inputs, arrays, away, rows, width, after, fetch, spill=()):
    states = inputs[0].shape[1]
    outs = [
        near((rows, glu_pack(width, 2 * states).width), bf16),
        moved((1, 2 * width), f32),
        moved((1, width), f32),
        near((2 * states // LANES, seqs * CHUNKS, LANES), f32),
        moved((seq_devices, seqs, 2 * states), f32),
    ]
    if k == 1:
        scratch = [pltpu.VMEM((rows // seqs // CHUNKS, seqs, CHUNKS, width), f32)]
    else:
        outs += [moved((2, width), f32), near((rows, width), bf16)]
        scratch = [
            pltpu.VMEM((rows, 3 * width), bf16),
            pltpu.VMEM((width, 2 * width), bf16),
            pltpu.VMEM((2 * states, width), bf16),
            pltpu.SemaphoreType.DMA((2, BACK_BLOCKS, 1)),
            pltpu.SemaphoreType.DMA((2, 1)),
        ]
    scratch += Powers.scratch(seqs, seq_devices, states, False)
    return call(
        partial(glu_back_kernel, k, seqs), info, inputs, arrays, away, outs, scratch, "glu_back", after, fetch, spill
    )


def lift_back_kernel(
    k, info_ref, parts_ref, stats_ref, skip_ref, decay_ref, phase_ref, gain_ref, shift_ref, *refs
):
    reverse = last = k == 0
    ends_ref, glu_pack_ref = refs[:2]
    states, width = 2 * decay_ref.shape[1], stats_ref.shape[1]
    mixed_ref, dh_ref, back_ref = glu_pack(width, states).views(glu_pack_ref, "mixed", "dh", "back")
    normed_ref, state_ref, weight_ref = refs[2:5]
    tables, refs = refs[-4:], refs[5:-4]
    if last:
        back_lifted_ref, sums_ref, lam_grad_ref, scale_grad_ref, ahead_ref = refs[:5]
        refs = refs[5:]
    else:
        out_ref, sums_ref, lam_grad_ref, scale_grad_ref = refs[:4]
        back_lifted_ref, back_normed_ref, kept_back_ref, kept_normed_ref = lift_pack(width, states).views(
            out_ref, "lifted", "back_normed", "back", "normed"
        )
        kept_back_ref[...] = back_ref[...]
        kept_normed_ref[...] = normed_ref[...]
        refs = refs[4:]
    h_ref, low_ref, acc_ref, lam_acc_ref, scale_acc_ref = refs
    rows, width = normed_ref.shape
    group = ends_ref.shape[1]
    seqs = parts_ref.shape[1]
    steps = rows // BACK_BLOCKS // group
    states = decay_ref.shape[1]
    where = Where(info_ref, seqs, rows // seqs)
    powers = Powers(k, True, where, decay_ref, phase_ref, *tables)
    chunk_starts(h_ref, where.seq, parts_ref, powers.leaps, ends_ref, powers.table, reverse)
    lam_acc_ref[...] = jnp.zeros_like(lam_acc_ref)
    scale_acc_ref[...] = jnp.zeros_like(scale_acc_ref)
    left = where.steps_left()
    lam, scale = powers.lam[...], powers.scale[...]
    root, gain, shift_row = stats_ref[1:2, :], gain_ref[k : k + 1, :], shift_ref[k : k + 1, :]
    skip = skip_ref[k : k + 1, :]
    gain_sum = jnp.zeros((1, width), f32)
    shift_sum = jnp.zeros((1, width), f32)
    shift = 1 if reverse else -1
    for _, first, now in blocks_of(rows, group, reverse, BACK_BLOCKS):
        moving = [left > first + t + shift for t in range(steps)]
        valid = [left > first + t for t in range(steps)]
        dh = dh_ref[now, :].astype(f32)
        normed = normed_ref[now, :]
        lifted = dot(normed, weight_ref[...]).astype(bf16).astype(f32)
        state = state_ref[now, :].astype(f32)
        for low in range(0, states, LANES):
            real_lanes = slice(low, low + LANES)
            imag_lanes = slice(states + low, states + low + LANES)
            gr, gi = h_ref[low // LANES], h_ref[(states + low) // LANES]
            lr, li = lam[:, real_lanes], lam[:, imag_lanes]
            part = scale[:, real_lanes]
            sum_r, sum_i = lam_acc_ref[:, real_lanes], lam_acc_ref[:, imag_lanes]
            sum_s = scale_acc_ref[:, real_lanes]
            for t in order(steps, reverse):
                at = slice(t * group, (t + 1) * group)
                hr, hi = state[at, real_lanes], state[at, imag_lanes]
                ur, ui = lifted[at, real_lanes], lifted[at, imag_lanes]
                mr, mi = jnp.where(moving[t], gr, 0.0), jnp.where(moving[t], gi, 0.0)
                sum_r += mr * hr + mi * hi
                sum_i += mi * hr - mr * hi
                nr, ni = cmul(lr, li, gr, gi)
                gr = jnp.where(moving[t], nr, gr) + dh[at, real_lanes]
                gi = jnp.where(moving[t], ni, gi) + dh[at, imag_lanes]
                vr, vi = jnp.where(valid[t], gr, 0.0), jnp.where(valid[t], gi, 0.0)
                sum_s += vr * ur + vi * ui
                low_ref[at, real_lanes] = part * vr
                low_ref[at, imag_lanes] = part * vi
            h_ref[low // LANES] = gr
            h_ref[(states + low) // LANES] = gi
            lam_acc_ref[:, real_lanes] = sum_r
            lam_acc_ref[:, imag_lanes] = sum_i
            scale_acc_ref[:, real_lanes] = sum_s
        back_lifted = low_ref[...].astype(bf16)
        back_lifted_ref[now, :] = back_lifted
        back_normed = dot_t(back_lifted, weight_ref[...]) + skip * mixed_ref[now, :].astype(f32)
        gain_sum += jnp.sum(back_normed * normed.astype(f32), axis=0, keepdims=True)
        shift_sum += jnp.sum(back_normed, axis=0, keepdims=True)
        if last:
            ahead_ref[now, :] = (back_ref[now, :].astype(f32) + (root * gain) * back_normed).astype(bf16)
        else:
            back_normed_ref[now, :] = back_normed.astype(bf16)
    lam_grad = jnp.sum(lam_acc_ref[...], axis=0, keepdims=True)
    scale_grad = jnp.sum(scale_acc_ref[...], axis=0, keepdims=True)
    acc_ref[0:1, :] = (gain_sum - shift_row * shift_sum) / gain
    acc_ref[1:2, :] = shift_sum
    lam_grad_ref[...] = lam_grad
    scale_grad_ref[...] = scale_grad
    for j in range(sums_ref.shape[0]):
        sums_ref[j] = acc_ref[...]


def lift_back(k, info, inputs, arrays, devices, after=(), fetch=()):
    parts, stats, decay = inputs[0], inputs[1], inputs[3]
    ends, packed = arrays[:2]
    rows, width, states = packed.shape[0], stats.shape[1], 2 * decay.shape[1]
    seq_devices, seqs, _ = parts.shape
    table = ends.shape
    acc = (2, width)
    outs = [near((rows, states if k == 0 else lift_pack(width, states).width), bf16), moved((devices,) + acc, f32)]
    outs += [moved((1, states), f32), moved((1, states // 2), f32)]
    if k == 0:
        outs.append(moved((rows, width), bf16))
    scratch = [
        pltpu.VMEM(table, f32),
        pltpu.VMEM((rows // BACK_BLOCKS, states), f32),
        pltpu.VMEM(acc, f32),
        pltpu.VMEM((table[1], states), f32),
        pltpu.VMEM((table[1], states // 2), f32),
    ]
    scratch += Powers.scratch(seqs, seq_devices, states // 2, True)
    return call(partial(lift_back_kernel, k), info, inputs, arrays, (), outs, scratch, "lift_back", after, fetch)


def two_parts(rows):
    high = rows.astype(bf16).astype(f32)
    return jnp.concatenate([high, rows - high], axis=0)


def one_part(rows):
    half = rows.shape[0] // 2
    return rows[:half] + rows[half:]


def halves_kernel(parts, pairs, small, info_ref, *refs):
    keep_ref, send_ref = refs[-2:]
    width = keep_ref.shape[1]
    even = lax.axis_index("seq") % 2 == 0
    if small:
        small_refs, refs = refs[:4], refs[4:]
    products = [t_dot(*(refs[n][:, lanes] for n, lanes in pair)) for pair in pairs]
    first = 0
    for n, rows, (r, c), (q, d) in parts:
        a = products[n][r : r + rows, c : c + width].astype(bf16)
        b = products[n][q : q + rows, d : d + width].astype(bf16)
        keep_ref[first : first + rows, :] = jnp.where(even, a, b)
        send_ref[first : first + rows, :] = jnp.where(even, b, a)
        first += rows
    if small:
        skip_ref, bias_ref, lam_ref, scale_ref = small_refs
        extra = keep_ref.shape[0] - first
        low = jnp.concatenate([skip_ref[...], bias_ref[:, :width], bias_ref[:, width:]], axis=0)
        scale = jnp.concatenate([scale_ref[...], jnp.zeros((1, width - scale_ref.shape[1]), f32)], axis=1)
        high = jnp.concatenate([lam_ref[...], scale, jnp.zeros((1, width), f32)], axis=0)
        rest = [jnp.zeros((EXTRA // 2 - 3, width), f32)], [jnp.zeros((extra - EXTRA, width), f32)]
        low, high = (two_parts(jnp.concatenate([x, *rest[0]], axis=0)) for x in (low, high))
        low, high = (jnp.concatenate([x, *rest[1]], axis=0).astype(bf16) for x in (low, high))
        keep_ref[first:, :] = jnp.where(even, low, high)
        send_ref[first:, :] = jnp.where(even, high, low)


def halves(info, parts, pairs, small, arrays, width, name, after=()):
    rows = sum(p[1] for p in parts)
    if small:
        rows += EXTRA * (lax.axis_size("seq") // 2)
    outs = [moved((rows, width), bf16)] * 2
    return call(partial(halves_kernel, parts, pairs, bool(small)), info, small, arrays, (), outs, [], name, after)


def place_of(axis):
    return lax.axis_index("batch") if axis == "batch" else lax.axis_index("seq") // 2


def total_of(refs, rows):
    total = refs[0][rows, :].astype(f32)
    for ref in refs[1:]:
        total += ref[rows, :].astype(f32)
    return total


def split_kernel(chips, sets, xor, info_ref, *refs):
    n_in = 2 * len(sets)
    outs = refs[n_in:]
    place = place_of("seq")
    for m in range(chips):
        chip = place ^ m if xor else m
        low = 0
        for n, parts in enumerate(sets):
            first = 0
            for rows in parts:
                share = rows // chips
                start = first + chip * share
                if xor:
                    start = pl.multiple_of(start, 16)
                total = total_of(refs[2 * n : 2 * n + 2], pl.ds(start, share))
                if share == EXTRA:
                    total = two_parts(one_part(total))
                if xor:
                    outs[m][low : low + share, :] = total.astype(outs[m].dtype)
                else:
                    base = m * (outs[0].shape[0] // chips) + low
                    outs[0][base : base + share, :] = total.astype(outs[0].dtype)
                first, low = first + rows, low + share


def split(info, sets, arrays, xor, after=()):
    chips = lax.axis_size("seq") // 2
    width = arrays[0].shape[1]
    rows = sum(map(sum, sets))
    outs = [moved((rows, width), bf16)]
    if xor:
        outs = [moved((rows // chips, width), f32)] + [moved((rows // chips, width), bf16)] * (chips - 1)
    return call(partial(split_kernel, chips, sets, xor), info, arrays, (), (), outs, [], "split", after, us=0.8)


def cut_kernel(extra, info_ref, *refs):
    low_ref, refs = refs[-1], refs[:-1]
    batches, share, width = low_ref.shape
    arrays, outs = refs[:-batches], refs[-batches:]
    place = place_of("batch")
    rows = batches * share
    low_ref[...] = total_of(arrays, slice(0, rows)).reshape(batches, share, width)
    under = two_parts(one_part(total_of(arrays, slice(rows, rows + extra))))
    for m in range(batches):
        outs[m][:share, :] = low_ref[place ^ m].astype(outs[m].dtype)
        outs[m][share:, :] = under.astype(outs[m].dtype)


def cut(info, arrays, extra, after=()):
    batches = lax.axis_size("batch")
    rows, width = arrays[0].shape
    share = (rows - extra) // batches
    outs = [moved((share + extra, width), f32)] + [moved((share + extra, width), bf16)] * (batches - 1)
    scratch = [pltpu.VMEM((batches, share, width), f32)]
    return call(partial(cut_kernel, extra), info, arrays, (), (), outs, scratch, "cut", after, us=1.2)


def sum_kernel(info_ref, *refs):
    total = refs[0][...].astype(f32)
    for ref in refs[1:-1]:
        total += ref[...].astype(f32)
    rows = total.shape[0] - EXTRA
    refs[-1][:rows, :] = total[:rows].astype(bf16)
    refs[-1][rows:, :] = two_parts(one_part(total[rows:])).astype(bf16)


def sum_of(info, arrays, after=()):
    return call(sum_kernel, info, arrays, (), (), [moved(arrays[0].shape, bf16)], [], "total", after, us=0.6)


def join_kernel(info_ref, *refs):
    pieces, out_ref, low_ref = refs[:-2], refs[-2], refs[-1]
    batches, share, width = low_ref.shape
    place = place_of("batch")
    for m, ref in enumerate(pieces):
        low_ref[place ^ m] = ref[:share, :].astype(f32)
    rows = batches * share
    out_ref[:rows, :] = low_ref[...].reshape(rows, width).astype(bf16)
    out_ref[rows:, :] = pieces[0][share:, :]


def join(info, arrays, extra, after=()):
    batches = len(arrays)
    rows, width = arrays[0].shape
    share = rows - extra
    outs = [moved((batches * share + extra, width), bf16)]
    scratch = [pltpu.VMEM((batches, share, width), f32)]
    return call(join_kernel, info, arrays, (), (), outs, scratch, "join", after, us=0.6)


def trade(x, axis, mask):
    size = lax.axis_size(axis)
    return lax.ppermute(x, axis, [(i, i ^ mask) for i in range(size)])


def sent(arrays, axis, masks):
    return [arrays[0]] + [trade(x, axis, m) for x, m in zip(arrays[1:], masks)]


def to_others(x, axis, masks):
    return [x] + [trade(x, axis, m) for m in masks]


def gate_kernel(*refs):
    pass


def gate(info, arrays, after):
    anywhere = pl.BlockSpec(memory_space=pl.ANY)
    outs = [(anywhere, jax.ShapeDtypeStruct(x.shape, x.dtype)) for x in arrays]
    aliases = {1 + i: i for i in range(len(arrays))}
    return run(gate_kernel, info, list(arrays), [anywhere] * len(arrays), outs, [], "gate", after, aliases)


def small_grads(norms, rows, decay_log, phase_log, refs):
    gain_ref, shift_ref, decay_grad_ref, phase_grad_ref, skip_grad_ref, bias_grad_ref = refs
    blocks, states = decay_log.shape
    width = norms[0].shape[1]
    for k in range(blocks):
        gain_ref[k : k + 1, :], shift_ref[k : k + 1, :] = norms[k][0:1], norms[k][1:2]
        low, high = rows[k]
        skip, bias_low, bias_high, lam, scale = low[0:1], low[1:2], low[2:3], high[0:1], high[1:2]
        skip_grad_ref[k : k + 1, :] = skip
        bias_grad_ref[k : k + 1, :width] = bias_low
        bias_grad_ref[k : k + 1, width:] = bias_high
        rate, angle = jnp.exp(decay_log[k : k + 1]), jnp.exp(phase_log[k : k + 1])
        size, fade = jnp.exp(-rate), jnp.exp(-2.0 * rate)
        lam_real, lam_imag = size * jnp.cos(angle), size * jnp.sin(angle)
        real, imag = lam[:, :states], lam[:, states : 2 * states]
        by_rate = scale[:, :states] * fade * lax.rsqrt(1.0 - fade) - (real * lam_real + imag * lam_imag)
        decay_grad_ref[k : k + 1, :] = rate * by_rate
        phase_grad_ref[k : k + 1, :] = angle * (imag * lam_real - real * lam_imag)


def input_grad(where, sums, stats_ref, gain_ref, tokens_ref, wide_ref, grad_ref):
    seqs, span, width = tokens_ref.shape
    shuffle = shuffle_matrix(span, True)
    average, root = stats_ref[0:1, :], stats_ref[1:2, :]
    factor = root * gain_ref[0:1, :] / stats_ref[2:3, 0:1]
    by_gain = factor * sums[0:1] * root
    fixed = factor * sums[1:2] - by_gain * average
    step = lax.broadcasted_iota(jnp.int32, (span, 1), 0)
    for s in range(seqs):
        valid = (step < where.lefts[s]).astype(f32)
        ahead = dot(shuffle, wide_ref[:, s].reshape(span, width).astype(bf16))
        grad_ref[s] = (ahead - valid * (fixed + by_gain * tokens_ref[s].astype(f32))).astype(bf16)


def results_kernel(chips, info_ref, sums_ref, norm1_ref, decay_ref, phase_ref, stats_ref, gain_ref, *refs):
    (tokens_in, ahead_in), pieces, refs = refs[:2], refs[2 : 2 + 4 * chips], refs[2 + 4 * chips :]
    glu_ref, mix_ref, lift_ref, grad_out, *small_refs = refs[:10]
    low_ref, under_ref, wide_ref, tokens_ref, ahead_ref, rows_ref, grad_ref, in_sems, sems, own_sems = refs[10:]
    own = [
        pltpu.make_async_copy(ahead_in, ahead_ref, own_sems.at[0]),
        pltpu.make_async_copy(tokens_in, tokens_ref, own_sems.at[1]),
    ]
    place = place_of("seq")
    core = lax.axis_index("seq") % 2
    _, rows, width = wide_ref.shape
    half, quarter = rows // 2, rows // 4
    arriving = []
    for n, piece in enumerate(pieces):
        parts = [pltpu.make_async_copy(piece.at[pl.ds(0, rows), :], low_ref.at[n], in_sems.at[n, 0])]
        parts.append(pltpu.make_async_copy(piece.at[pl.ds(rows, EXTRA), :], under_ref.at[n], in_sems.at[n, 1]))
        begin(parts)
        arriving.append(parts)
    begin(own)
    copies = []
    extras = [[jnp.zeros((EXTRA // 2, width), f32)] * 2 for _ in range(2)]
    for n in range(4 * chips):
        finished(arriving[n])
        k, n_in = divmod(n, 2 * chips)
        chip, side = place ^ (n_in % chips), core if n_in < chips else 1 - core
        extra = one_part(under_ref[n].astype(f32))
        extras[k][n_in // chips] = jnp.where(chip == 0, extra, extras[k][n_in // chips])
        column = pl.multiple_of(side * width, width)
        row = pl.multiple_of(chip * half, 8)
        low = pl.multiple_of(side * (quarter * chips) + chip * quarter, 8)
        wide_ref[n] = low_ref[n].astype(f32)
        for i, (first, size, target) in enumerate(
            (
                (0, half, glu_ref.at[k, pl.ds(row, half), pl.ds(column, width)]),
                (half, quarter, mix_ref.at[k, pl.ds(low, quarter), :]),
                (half + quarter, quarter, lift_ref.at[k, pl.ds(low, quarter), :]),
            )
        ):
            copies.append(pltpu.make_async_copy(wide_ref.at[n, pl.ds(first, size), :], target, sems.at[n, i]))
            copies[-1].start()
    even = core == 0
    sums = sums_ref[...]
    finished(own)
    rows_ref[...] = ahead_ref[...].astype(f32).reshape(rows_ref.shape)
    seqs, span, _ = tokens_ref.shape
    input_grad(Where(info_ref, seqs, span), sums, stats_ref, gain_ref, tokens_ref, rows_ref, grad_ref)
    copies.append(pltpu.make_async_copy(grad_ref, grad_out, own_sems.at[2]))
    copies[-1].start()
    small_grads(
        (sums, norm1_ref[...]),
        [(jnp.where(even, mine, other), jnp.where(even, other, mine)) for mine, other in extras],
        decay_ref[...],
        phase_ref[...],
        small_refs,
    )
    finished(copies)


def results(info, sums, norm1, decay_log, phase_log, stats, gain, tokens, ahead, pieces, after=()):
    seqs, span, _ = tokens.shape
    rows, width = pieces[0].shape
    rows -= EXTRA
    count = len(pieces)
    anywhere = pl.BlockSpec(memory_space=pl.ANY)
    shapes = [(2, width, 2 * width), (2, width, width), (2, width, width)]
    outs = [(anywhere, jax.ShapeDtypeStruct(shape, f32)) for shape in shapes]
    outs.append((anywhere, jax.ShapeDtypeStruct(tokens.shape, bf16)))
    blocks, states = decay_log.shape
    outs += [moved((blocks, n), f32) for n in (width, width, states, states, width, 2 * width)]
    scratch = [
        pltpu.VMEM((count, rows, width), bf16),
        pltpu.VMEM((count, EXTRA, width), bf16),
        pltpu.VMEM((count, rows, width), f32),
        pltpu.VMEM(tokens.shape, bf16),
        pltpu.VMEM(ahead.shape, bf16),
        pltpu.VMEM((span // CHUNKS, seqs, CHUNKS, width), f32),
        pltpu.VMEM(tokens.shape, bf16),
        pltpu.SemaphoreType.DMA((count, 2)),
        pltpu.SemaphoreType.DMA((count, 3)),
        pltpu.SemaphoreType.DMA((3,)),
    ]
    inputs = [sums, norm1, decay_log, phase_log, stats, gain]
    given = [*inputs, *map(there, (tokens, ahead)), *pieces]
    specs = [in_vmem] * len(inputs) + [in_hbm] * 2 + [anywhere] * count
    return run(partial(results_kernel, count // 4), info, given, specs, outs, scratch, "results", after, us=7.0)


def norms_kernel(info_ref, sums_ref, total_ref):
    total_ref[...] = jnp.sum(sums_ref[...], axis=0)


def norms(info, sums, after=()):
    outs = [moved(sums.shape[1:], f32)]
    return call(norms_kernel, info, (sums,), (), (), outs, [], "norms", after, us=0.6)


def leave_kernel(seqs, info_ref, rows_ref, out_ref, wide_ref):
    _, span, width = out_ref.shape
    wide_ref[...] = rows_ref[...].astype(f32).reshape(wide_ref.shape)
    shuffle = shuffle_matrix(span, True)
    for s in range(seqs):
        out_ref[s] = dot(shuffle, wide_ref[:, s].reshape(span, width).astype(bf16)).astype(bf16)


def leave(info, rows, seqs, after=()):
    span, width = rows.shape[0] // seqs, rows.shape[1]
    scratch = [pltpu.VMEM((span // CHUNKS, seqs, CHUNKS, width), f32)]
    outs = [moved((seqs, span, width), bf16)]
    return call(partial(leave_kernel, seqs), info, (rows,), (), (), outs, scratch, "leave", after)


def to_all(x, axes):
    return lax.all_to_all(x, axes, split_axis=0, concat_axis=0, tiled=True)


def local(
    tokens,
    lengths,
    cotangent,
    norm_gain,
    norm_shift,
    lift_weight,
    decay_log,
    phase_log,
    skip_gain,
    mix_weight,
    glu_weight,
    glu_bias,
):
    both = ("seq", "batch")
    seq_devices, batches = lax.axis_size("seq"), lax.axis_size("batch")
    devices, chips = seq_devices * batches, seq_devices // 2
    seqs, span, width = tokens.shape
    rows = seqs * span
    info = lengths
    turns = (decay_log, phase_log)
    norms_in = (norm_gain, norm_shift)
    states = decay_log.shape[1]
    half = width // 2

    sums, tokens_here, lift_w = enter(info, tokens, devices, [(lift_weight, 0)])
    sums = to_all(sums, both)
    normed, lifted, ends, part, stats0, x, mix_w, glu_w = lift(
        0, seqs, seq_devices, info, (sums, *norms_in, *turns), (tokens_here, lift_w), rows,
        [(mix_weight, 0), (glu_weight, 0)],
    )
    x1, sums, kept, lift_w, normed0 = mix(
        0, info, (to_all(part, "seq"), skip_gain, glu_bias, *turns), (ends, lifted, normed, x, mix_w, glu_w),
        devices, [(lift_weight, 1)], (normed,),
    )
    sums = to_all(sums, both)

    normed1, lifted1, ends, part, stats1, mix_w, glu_w = lift(
        1, seqs, seq_devices, info, (sums, *norms_in, *turns, stats0), (x1, lift_w), rows,
        [(mix_weight, 1), (glu_weight, 1)],
    )
    state1, activated1, slope1, gate1, gate_slope1, masked, cot = mix(
        1, info, (to_all(part, "seq"), skip_gain, glu_bias, *turns), (ends, lifted1, normed1, x1, mix_w, glu_w),
        devices, [(cotangent, None)],
    )

    glu_packed, bias_grad1, skip_grad1, ends, part, lift_w, masked = glu_back(
        1, seqs, seq_devices, info, turns, (cot, normed1, slope1, gate1, gate_slope1, glu_w, mix_w), (), rows, width,
        (), [(lift_weight, 1)], [masked],
    )
    lift_packed, sums, lam_grad1, scale_grad1 = lift_back(
        1, info, (to_all(part, "seq"), stats1, skip_gain, *turns, *norms_in),
        (ends, glu_packed, normed1, state1, lift_w), devices,
    )
    glu_part, mix_part, lift_part = (0, width, (0, 0), (0, width)), (1, half, (0, 0), (half, 0)), (2, half, (0, 0), (half, 0))
    glu_lanes, lift_lanes = glu_pack(width, 2 * states).lanes, lift_pack(width, 2 * states).lanes
    kept_lanes, every = kept_pack(width, 2 * states).lanes, slice(None)
    out = halves(
        info,
        (glu_part, mix_part, lift_part),
        (
            ((0, every), (1, glu_lanes["projected"])),
            ((2, every), (1, glu_lanes["mixed"])),
            ((3, every), (4, lift_lanes["lifted"])),
        ),
        (skip_grad1, bias_grad1, lam_grad1, scale_grad1),
        (activated1, glu_packed, state1, normed1, lift_packed),
        width,
        "halves1",
    )
    keep1, send = out
    got1 = trade(send, "seq", 1)
    (produced,) = out = leave(info, masked, seqs, (out.tick,))
    shares = (width, half, half)
    z, xy = range(1, batches), range(2, seq_devices, 2)
    extra = EXTRA * chips
    out = split(info, ((*shares, extra),), [keep1, got1], True, (out.tick,))
    pieces1 = sent(out, "seq", xy)
    sums = to_all(sums, both)

    state_lanes = (slice(None), kept_lanes["state"])
    out = glu_back(
        0, seqs, seq_devices, info, (*turns, sums, stats1, *norms_in), (lift_packed,),
        (kept, normed0, glu_weight, mix_weight), rows, width, (),
        [(kept, state_lanes), (lift_weight, 0)],
    )
    glu_packed, bias_grad0, skip_grad0, ends, part, norm_sums1, normed, state, lift_w = out
    activated_lanes = (slice(None), kept_lanes["activated"])
    parts, *pieces1 = gate(info, [to_all(part, "seq"), *pieces1], ())
    back_lifted0, sums, lam_grad0, scale_grad0, ahead, activated = out = lift_back(
        0, info, (parts, stats0, skip_gain, *turns, *norms_in),
        (ends, glu_packed, normed, state, lift_w), devices, (), [(kept, activated_lanes)],
    )

    keep0, send = out = halves(
        info,
        (glu_part, mix_part, lift_part),
        (
            ((0, every), (1, glu_lanes["projected"])),
            ((2, every), (1, glu_lanes["mixed"])),
            ((3, every), (4, every)),
        ),
        (skip_grad0, bias_grad0, lam_grad0, scale_grad0),
        (activated, glu_packed, state, normed, back_lifted0),
        width,
        "halves0",
    )
    got0 = trade(send, "seq", 1)
    out1 = cut(info, pieces1, EXTRA, (out.tick,))
    out0 = split(info, ((*shares, extra),), [keep0, got0], True, (out1.tick,))
    sum1 = sum_of(info, sent(out1, "batch", z), (out0.tick,))
    (sums,) = gate(info, [sums], (sum1.tick,))
    sums = to_all(sums, both)
    (own1,) = out = join(info, to_others(sum1[0], "batch", z), EXTRA, (sum1.tick,))
    out0 = cut(info, sent(out0, "seq", xy), EXTRA, (out.tick,))
    sum0 = sum_of(info, sent(out0, "batch", z))
    (own0,) = out = join(info, to_others(sum0[0], "batch", z), EXTRA)
    (sums,) = norms(info, sums, (out.tick,))
    pieces = []
    for own in (own0, own1):
        total = to_others(own, "seq", xy)
        pieces += total + [trade(x, "seq", 1) for x in total]
    out = results(info, sums, norm_sums1, *turns, stats0, norm_gain, tokens, ahead, pieces)
    grad_glu, grad_mix, grad_lift, tokens_grad, grad_gain, grad_shift, grad_decay, grad_phase, grad_skip, grad_bias = out
    return (
        produced,
        tokens_grad,
        grad_gain,
        grad_shift,
        grad_lift,
        grad_decay,
        grad_phase,
        grad_skip,
        grad_mix,
        grad_glu,
        grad_bias,
    )


def solution(mesh):
    split = P("batch", "seq", None)
    placed = (split, P("batch"), split) + (P(),) * 9
    return jax.shard_map(
        local,
        mesh=mesh,
        in_specs=placed,
        out_specs=(split, split) + (P(),) * 9,
        check_vma=False,
    )
```

```python
from functools import partial

import jax
import jax.numpy as jnp
from jax import lax
from jax.experimental import pallas as pl
from jax.experimental.pallas import tpu as pltpu
from jax.sharding import PartitionSpec as P

norm_eps = 1e-05
f32 = jnp.float32
bf16 = jnp.bfloat16

CHUNKS = 8
BLOCKS = 4
BACK_BLOCKS = 2
PARTS = 1
EXTRA = 16
LANES = 128
VMEM_LIMIT = 32 * 1024 * 1024

in_vmem = pl.BlockSpec(memory_space=pltpu.VMEM)
in_smem = pl.BlockSpec(memory_space=pltpu.SMEM)
in_hbm = pl.BlockSpec(memory_space=pltpu.HBM)


def near(shape, dtype):
    return in_vmem, pltpu.VMEM(shape, dtype)


def moved(shape, dtype):
    return in_vmem, jax.ShapeDtypeStruct(shape, dtype)


def copy_parts(source, target, sems):
    size = source.shape[0] // sems.shape[0]
    cuts = [pl.ds(i * size, size) for i in range(sems.shape[0])]
    return [pltpu.make_async_copy(source.at[cut], target.at[cut], sems.at[i]) for i, cut in enumerate(cuts)]


def begin(copies):
    for copy in copies:
        copy.start()


def finished(copies):
    for copy in copies:
        copy.wait()


class Outs(list):
    tick = None


def run(body, info, given, specs, outs, scratch, name, after, aliases=(), us=None):
    cost = None
    if us is not None:
        cost = pl.CostEstimate(flops=int(us * 1.1e9), bytes_accessed=int(us * 3e6), transcendentals=0)
    after = [pltpu.with_memory_space_constraint(t, pltpu.HBM) for t in after]
    n_in, n_out = 1 + len(given), len(outs)

    def ticking(*refs):
        body(*refs[:n_in], *refs[n_in + len(after) : n_in + len(after) + n_out], *refs[n_in + len(after) + n_out + 1 :])

    out = pl.pallas_call(
        ticking,
        in_specs=[in_smem] + specs + [in_hbm] * len(after),
        out_specs=[spec for spec, _ in outs] + [in_hbm],
        out_shape=[shape for _, shape in outs] + [pltpu.HBM((8, LANES), f32)],
        scratch_shapes=scratch,
        input_output_aliases=dict(aliases),
        compiler_params=pltpu.CompilerParams(vmem_limit_bytes=VMEM_LIMIT),
        cost_estimate=cost,
        name=name,
    )(info, *given, *after)
    result = Outs(out[:n_out])
    result.tick = out[n_out]
    return result


def here(x):
    return pltpu.with_memory_space_constraint(x, pltpu.VMEM)


def there(x):
    return pltpu.with_memory_space_constraint(x, pltpu.HBM)


def call(kernel, info, inputs, arrays, away, outs, scratch, name, after=(), fetch=(), spill=(), us=None):
    first = 1 + len(inputs) + len(arrays) + len(away)
    n_copies = len(fetch) + len(spill)
    fetched = [jax.eval_shape(lambda x, at=at: x if at is None else x[at], a) for a, at in fetch]
    outs = list(outs)
    n_outs = len(outs)
    outs += [near(a.shape, a.dtype) for a in fetched] + [(in_hbm, pltpu.HBM(a.shape, a.dtype)) for a in spill]

    def body(*refs):
        ins, rest = refs[: first + n_copies], refs[first + n_copies :]
        sources = list(ins[first:])
        for i, (_, at) in enumerate(fetch):
            if at is not None:
                sources[i] = sources[i].at[at]
        targets = rest[n_outs : n_outs + n_copies]
        rest = rest[:n_outs] + rest[n_outs + n_copies :]
        copies = []
        for i, (x, y) in enumerate(zip(sources, targets)):
            copies += copy_parts(x, y, rest[-1].at[i])
        begin(copies)
        kernel(*ins[:first], *(rest[:-1] if copies else rest))
        finished(copies)

    given = [*inputs, *map(here, arrays), *map(there, away), *(there(a) for a, _ in fetch), *map(here, spill)]
    specs = [in_vmem] * (len(inputs) + len(arrays)) + [in_hbm] * (len(away) + len(fetch)) + [in_vmem] * len(spill)
    scratch = list(scratch) + [pltpu.SemaphoreType.DMA((n_copies, PARTS))] * bool(n_copies)
    return run(body, info, given, specs, outs, scratch, name, after, us=us)


class Pack:
    def __init__(self, *fields):
        self.lanes, self.width = {}, 0
        for name, width in fields:
            self.lanes[name] = slice(self.width, self.width + width)
            self.width += width

    def views(self, ref, *names):
        return [ref.at[:, self.lanes[n]] for n in names]


def kept_pack(width, states):
    return Pack(*((n, width) for n in ("slope", "gate", "gate_slope", "activated")), ("state", states))


def glu_pack(width, states):
    return Pack(("projected", 2 * width), ("mixed", width), ("dh", states), ("back", width))


def lift_pack(width, states):
    return Pack(("lifted", states), ("back_normed", width), ("back", width), ("normed", width))


def wide(mask, width):
    return jnp.concatenate([mask] * (width // LANES), axis=1)


def dot(a, b):
    return lax.dot_general(a, b, (((1,), (0,)), ((), ())), preferred_element_type=f32)


def dot_t(a, b):
    return lax.dot_general(a, b, (((1,), (1,)), ((), ())), preferred_element_type=f32)


def t_dot(a, b):
    return lax.dot_general(a, b, (((0,), (0,)), ((), ())), preferred_element_type=f32)


def cmul(ar, ai, br, bi):
    return ar * br - ai * bi, ar * bi + ai * br


def order(steps, reverse):
    return range(steps - 1, -1, -1) if reverse else range(steps)


def shuffle_matrix(span, back):
    chunk = span // CHUNKS
    place = lax.broadcasted_iota(jnp.int32, (span, span), 0)
    source = lax.broadcasted_iota(jnp.int32, (span, span), 1)
    if back:
        wanted = (place % chunk) * CHUNKS + place // chunk
    else:
        wanted = (place % CHUNKS) * chunk + place // CHUNKS
    return (source == wanted).astype(f32).astype(bf16)


class Where:
    def __init__(self, info_ref, seqs, span):
        self.seq = lax.axis_index("seq")
        self.seqs, self.span = seqs, span
        self.lengths = [info_ref[s] for s in range(seqs)]
        self.lefts = [length - self.seq * span for length in self.lengths]

    def steps_left(self):
        before = (self.span // CHUNKS) * lax.broadcasted_iota(jnp.int32, (CHUNKS, LANES), 0)
        return jnp.concatenate([left - before for left in self.lefts], axis=0)


def valid_rows(left, first, steps):
    return jnp.concatenate([(left > first + t).astype(f32) for t in range(steps)], axis=0)


def shuffle_rows(wide_ref, source_ref):
    steps, seqs, chunks, width = wide_ref.shape
    shuffle = shuffle_matrix(steps * chunks, False)
    for s in range(seqs):
        wide_ref[:, s] = dot(shuffle, source_ref[s]).reshape(steps, chunks, width)


def enter_kernel(info_ref, tokens_ref, sums_ref, here_ref, acc_ref, sems):
    seqs, span, width = tokens_ref.shape
    copies = [copy_parts(tokens_ref.at[s], here_ref.at[s], sems.at[s]) for s in range(seqs)]
    for parts in copies:
        begin(parts)
    where = Where(info_ref, seqs, span)
    step = lax.broadcasted_iota(jnp.int32, (span, 1), 0)
    total = jnp.zeros((1, width), f32)
    squares = jnp.zeros((1, width), f32)
    count = jnp.zeros((1, 1), f32)
    for s in range(seqs):
        valid = (step < where.lefts[s]).astype(f32)
        finished(copies[s])
        x = here_ref[s].astype(f32)
        masked = x * valid
        total += jnp.sum(masked, axis=0, keepdims=True)
        squares += jnp.sum(masked * x, axis=0, keepdims=True)
        count += jnp.sum(valid, axis=0, keepdims=True)
    tail = jnp.broadcast_to(count, (1, LANES))
    acc_ref[0:1, :] = jnp.concatenate([total, tail], axis=1)
    acc_ref[1:2, :] = jnp.concatenate([squares, tail], axis=1)
    for j in range(sums_ref.shape[0]):
        sums_ref[j] = acc_ref[...]


def enter(info, tokens, devices, fetch):
    seqs, _, width = tokens.shape
    outs = [moved((devices, 2, width + LANES), f32), near(tokens.shape, bf16)]
    scratch = [pltpu.VMEM((2, width + LANES), f32), pltpu.SemaphoreType.DMA((seqs, 1))]
    return call(enter_kernel, info, (), (), (tokens,), outs, scratch, "enter", fetch=fetch)


class Powers:
    @staticmethod
    def scratch(seqs, seq_devices, states, leaps):
        tables = [((1, 2 * states), f32), ((1, states), f32), ((2 * states // LANES, seqs * CHUNKS, LANES), f32)]
        if leaps:
            tables.append(((seq_devices * seqs, 2 * states), f32))
        return [pltpu.VMEM(*t) for t in tables]

    def __init__(self, k, back, where, decay_ref, phase_ref, lam_ref, scale_ref, table_ref, leap_ref=None):
        states = scale_ref.shape[1]
        groups, group = states // LANES, table_ref.shape[1]
        seqs, span, limit = where.seqs, where.span, where.span // CHUNKS
        rate = jnp.exp(decay_ref[k : k + 1, :])
        size, angle = jnp.exp(-rate), jnp.exp(phase_ref[k : k + 1, :])
        lam_ref[:, :states] = size * jnp.cos(angle)
        lam_ref[:, states:] = size * jnp.sin(angle) * (-1.0 if back else 1.0)
        scale_ref[...] = jnp.sqrt(1.0 - jnp.exp(-2.0 * rate))
        self.lam, self.scale, self.table, self.leaps = lam_ref, scale_ref, table_ref, leap_ref
        shift = 0 if not back else (-1 if k == 0 else 1)
        chunk_count = jnp.clip(where.steps_left() + shift, 0, limit)
        if leap_ref is not None:
            total = leap_ref.shape[0]
            line = lax.broadcasted_iota(jnp.int32, (total, LANES), 0)
            span_left = jnp.zeros((total, LANES), jnp.int32)
            for s, length in enumerate(where.lengths):
                span_left = jnp.where(line % seqs == s, length - span * (line // seqs), span_left)
            span_count = jnp.clip(span_left + shift, 0, span)
        for low in range(groups):
            real_lanes = slice(low * LANES, (low + 1) * LANES)
            imag_lanes = slice((groups + low) * LANES, (groups + low + 1) * LANES)
            br, bi = lam_ref[:, real_lanes], lam_ref[:, imag_lanes]
            cr = jnp.ones((group, LANES), f32)
            ci = jnp.zeros((group, LANES), f32)
            if leap_ref is not None:
                pr = jnp.ones((total, LANES), f32)
                pi = jnp.zeros((total, LANES), f32)
            for bit in range((limit if leap_ref is None else span).bit_length()):
                if (1 << bit) <= limit:
                    nr, ni = cmul(cr, ci, br, bi)
                    odd = (chunk_count & (1 << bit)) != 0
                    cr, ci = jnp.where(odd, nr, cr), jnp.where(odd, ni, ci)
                if leap_ref is not None:
                    nr, ni = cmul(pr, pi, br, bi)
                    odd = (span_count & (1 << bit)) != 0
                    pr, pi = jnp.where(odd, nr, pr), jnp.where(odd, ni, pi)
                br, bi = cmul(br, bi, br, bi)
            table_ref[low] = cr
            table_ref[groups + low] = ci
            if leap_ref is not None:
                leap_ref[:, real_lanes] = pr
                leap_ref[:, imag_lanes] = pi


def stretch_part(ends_ref, power_ref, reverse, seqs):
    groups = ends_ref.shape[0] // 2
    reals, imags = [], []
    for low in range(groups):
        real = jnp.zeros((seqs, LANES), f32)
        imag = jnp.zeros((seqs, LANES), f32)
        for c in order(CHUNKS, reverse):
            here = pl.ds(c, seqs, stride=CHUNKS)
            real, imag = cmul(power_ref[low, here, :], power_ref[groups + low, here, :], real, imag)
            real += ends_ref[low, here, :]
            imag += ends_ref[groups + low, here, :]
        reals.append(real)
        imags.append(imag)
    return jnp.concatenate(reals + imags, axis=1)


def chunk_starts(start_ref, place, parts_ref, leaps_ref, ends_ref, power_ref, reverse):
    devices, seqs, width = parts_ref.shape
    states = width // 2
    groups = states // LANES
    real = jnp.zeros((seqs, states), f32)
    imag = jnp.zeros((seqs, states), f32)
    for j in order(devices, reverse):
        ahead = (j > place) if reverse else (j < place)
        leap, part = leaps_ref[seqs * j : seqs * (j + 1), :], parts_ref[j]
        next_real, next_imag = cmul(leap[:, :states], leap[:, states:], real, imag)
        real = jnp.where(ahead, next_real + part[:, :states], real)
        imag = jnp.where(ahead, next_imag + part[:, states:], imag)
    for low in range(groups):
        hr = real[:, low * LANES : (low + 1) * LANES]
        hi = imag[:, low * LANES : (low + 1) * LANES]
        for c in order(CHUNKS, reverse):
            here = pl.ds(c, seqs, stride=CHUNKS)
            start_ref[low, here, :] = hr
            start_ref[groups + low, here, :] = hi
            hr, hi = cmul(power_ref[low, here, :], power_ref[groups + low, here, :], hr, hi)
            hr += ends_ref[low, here, :]
            hi += ends_ref[groups + low, here, :]


def scan_block(h_ref, drive, left, lam, shift, first, steps, reverse, out_ref=None):
    groups, group, _ = h_ref.shape
    groups = groups // 2
    masks = [left > first + t + shift for t in range(steps)]
    for low in range(groups):
        real_lanes = slice(low * LANES, (low + 1) * LANES)
        imag_lanes = slice((groups + low) * LANES, (groups + low + 1) * LANES)
        hr, hi = h_ref[low], h_ref[groups + low]
        lr, li = lam[:, real_lanes], lam[:, imag_lanes]
        for t in order(steps, reverse):
            ur, ui = drive(t, real_lanes, imag_lanes)
            nr, ni = cmul(lr, li, hr, hi)
            hr = jnp.where(masks[t], nr, hr) + ur
            hi = jnp.where(masks[t], ni, hi) + ui
            if out_ref is not None:
                out_ref[t * group : (t + 1) * group, real_lanes] = hr
                out_ref[t * group : (t + 1) * group, imag_lanes] = hi
        h_ref[low] = hr
        h_ref[groups + low] = hi


def input_drive(lifted, scale, left, first, steps):
    group = left.shape[0]
    masks = [left > first + t for t in range(steps)]

    def drive(t, real_lanes, imag_lanes):
        here = slice(t * group, (t + 1) * group)
        factor = jnp.where(masks[t], scale[:, real_lanes], 0.0)
        return factor * lifted[here, real_lanes], factor * lifted[here, imag_lanes]

    return drive


def blocks_of(rows, group, reverse, blocks=BLOCKS):
    size = rows // blocks
    for block in order(blocks, reverse):
        yield block, block * (size // group), slice(block * size, (block + 1) * size)


def lift_kernel(k, seqs, info_ref, sums_ref, gain_ref, shift_ref, decay_ref, phase_ref, *refs):
    reverse = k == 1
    if k == 0:
        x_ref, weight_ref, normed_ref, lifted_ref, ends_ref, part_ref, stats_ref, rows_ref, wide_ref = refs[:9]
        refs = refs[9:]
    else:
        count_ref, x_ref, weight_ref, normed_ref, lifted_ref, ends_ref, part_ref, stats_ref = refs[:8]
        refs = refs[8:]
    rows, width = normed_ref.shape
    group = ends_ref.shape[1]
    size = rows // BLOCKS
    steps = size // group
    where = Where(info_ref, seqs, rows // seqs)
    powers = Powers(k, False, where, decay_ref, phase_ref, *refs)
    if k == 0:
        shuffle_rows(wide_ref, x_ref)
    sums = jnp.sum(sums_ref[...], axis=0)
    if k == 0:
        count = sums[0:1, width : width + 1]
    else:
        count = count_ref[2:3, 0:1]
    average = sums[0:1, :width] / count
    root = lax.rsqrt(sums[1:2, :width] / count - average * average + norm_eps)
    stats_ref[0:1, :] = average
    stats_ref[1:2, :] = root
    stats_ref[2:3, :] = jnp.broadcast_to(count, (1, width))
    gain, shift = gain_ref[k : k + 1, :], shift_ref[k : k + 1, :]
    lam, scale = powers.lam[...], powers.scale[...]
    left = where.steps_left()
    ends_ref[...] = jnp.zeros_like(ends_ref)
    for _, first, now in blocks_of(rows, group, reverse):
        if k == 0:
            x = wide_ref[first : first + steps].reshape(size, width)
            rows_ref[now, :] = x.astype(bf16)
        else:
            x = x_ref[now, :]
        normed = ((x - average) * root * gain + shift).astype(bf16)
        normed_ref[now, :] = normed
        lifted = dot(normed, weight_ref[...]).astype(bf16)
        lifted_ref[now, :] = lifted
        drive = input_drive(lifted.astype(f32), scale, left, first, steps)
        scan_block(ends_ref, drive, left, lam, 0, first, steps, reverse)
    part = stretch_part(ends_ref, powers.table, reverse, seqs)
    for j in range(part_ref.shape[0]):
        part_ref[j] = part


def lift(k, seqs, seq_devices, info, inputs, arrays, rows, fetch):
    gain, decay = inputs[1], inputs[3]
    width, states = gain.shape[1], decay.shape[1]
    outs = [
        near((rows, width), bf16),
        near((rows, 2 * states), bf16),
        near((2 * states // LANES, seqs * CHUNKS, LANES), f32),
        moved((seq_devices, seqs, 2 * states), f32),
        moved((8, width), f32),
    ]
    scratch = []
    if k == 0:
        outs.append(near((rows, width), bf16))
        scratch.append(pltpu.VMEM((rows // seqs // CHUNKS, seqs, CHUNKS, width), f32))
    scratch += Powers.scratch(seqs, seq_devices, states, False)
    return call(partial(lift_kernel, k, seqs), info, inputs, arrays, (), outs, scratch, "lift", fetch=fetch)


def mix_kernel(k, info_ref, parts_ref, skip_ref, bias_ref, decay_ref, phase_ref, *refs):
    reverse = k == 1
    (ends_ref, lifted_ref, normed_ref, x_ref, mix_ref, glu_ref) = refs[:6]
    tables, refs = refs[-4:], refs[6:-4]
    if reverse:
        state_ref, activated_ref, slope_ref, gate_ref, gate_slope_ref, masked_ref, h_ref, states_ref = refs
    else:
        next_ref, sums_ref, kept_out, h_ref, states_ref, acc_ref, kept_ref, sems = refs
        pack = kept_pack(x_ref.shape[1], lifted_ref.shape[1])
        state_ref, activated_ref, slope_ref, gate_ref, gate_slope_ref = pack.views(
            kept_ref, "state", "activated", "slope", "gate", "gate_slope"
        )
        copies = []
    seqs = parts_ref.shape[1]
    rows, width = x_ref.shape
    group = ends_ref.shape[1]
    blocks = 2 if reverse else BLOCKS
    steps = rows // blocks // group
    where = Where(info_ref, seqs, rows // seqs)
    powers = Powers(k, False, where, decay_ref, phase_ref, *tables)
    chunk_starts(h_ref, where.seq, parts_ref, powers.leaps, ends_ref, powers.table, reverse)
    left = where.steps_left()
    skip, bias = skip_ref[k : k + 1, :], bias_ref[k : k + 1, :]
    lam, scale = powers.lam[...], powers.scale[...]
    total = jnp.zeros((1, width), f32)
    squares = jnp.zeros((1, width), f32)
    for block, first, now in blocks_of(rows, group, reverse, blocks):
        drive = input_drive(lifted_ref[now, :].astype(f32), scale, left, first, steps)
        scan_block(h_ref, drive, left, lam, 0, first, steps, reverse, states_ref)
        state = states_ref[...].astype(bf16)
        state_ref[now, :] = state
        mixed = dot(state, mix_ref[...]) + skip * normed_ref[now, :].astype(f32)
        base, cube = 0.7978845608028654, 0.044715
        square = mixed * mixed
        bend = jnp.tanh(mixed * (base + (base * cube) * square))
        half = 0.5 + 0.5 * bend
        activated = (mixed * half).astype(bf16)
        activated_ref[now, :] = activated
        slope_ref[now, :] = (
            half + mixed * (half - half * half) * (2.0 * base + (6.0 * base * cube) * square)
        ).astype(bf16)
        projected = dot(activated, glu_ref[...]) + bias
        gate = 0.5 + 0.5 * jnp.tanh(0.5 * projected[:, width:])
        gated = projected[:, :width] * gate
        gate_ref[now, :] = gate.astype(bf16)
        gate_slope_ref[now, :] = (gated - gated * gate).astype(bf16)
        after = x_ref[now, :].astype(f32) + gated
        masked = after * wide(valid_rows(left, first, steps), width)
        if reverse:
            masked_ref[now, :] = masked.astype(bf16)
        else:
            next_ref[now, :] = after
            total += jnp.sum(masked, axis=0, keepdims=True)
            squares += jnp.sum(masked * after, axis=0, keepdims=True)
            parts = copy_parts(kept_ref.at[now, :], kept_out.at[now, :], sems.at[block])
            begin(parts)
            copies += parts
    if not reverse:
        acc_ref[0:1, :] = total
        acc_ref[1:2, :] = squares
        for j in range(sums_ref.shape[0]):
            sums_ref[j] = acc_ref[...]
        finished(copies)


def mix(k, info, inputs, arrays, devices, fetch, spill=()):
    parts = inputs[0]
    ends, lifted, _, x = arrays[:4]
    rows, width = x.shape
    states = lifted.shape[1]
    seq_devices, seqs, _ = parts.shape
    scratch = [pltpu.VMEM(ends.shape, f32), pltpu.VMEM((rows // (2 if k == 1 else BLOCKS), states), f32)]
    if k == 1:
        outs = [near((rows, states), bf16)] + [near((rows, width), bf16)] * 5
    else:
        kept = (rows, kept_pack(width, states).width)
        outs = [near((rows, width), f32), moved((devices, 2, width), f32), (in_hbm, pltpu.HBM(kept, bf16))]
        scratch += [pltpu.VMEM((2, width), f32), pltpu.VMEM(kept, bf16), pltpu.SemaphoreType.DMA((BLOCKS, 1))]
    scratch += Powers.scratch(seqs, seq_devices, states // 2, True)
    return call(
        partial(mix_kernel, k), info, inputs, arrays, (), outs, scratch, "mix", fetch=fetch, spill=spill
    )


def glu_back_kernel(k, seqs, info_ref, decay_ref, phase_ref, *refs):
    reverse = k == 0
    if k == 0:
        sums_ref, stats_ref, gain_ref, shift_ref, lift_pack_ref, kept_ref, normed_in, glu_in, mix_in = refs[:9]
        tables, refs = refs[-3:], refs[9:-3]
    else:
        start_ref, normed_ref, slope_ref, gate_ref, gate_slope_ref, glu_ref, mix_ref = refs[:7]
        tables, refs = refs[-3:], refs[7:-3]
    out_ref, bias_grad_ref, skip_grad_ref, ends_ref, part_ref = refs[:5]
    refs = refs[5:]
    rows, width = out_ref.shape[0], skip_grad_ref.shape[1]
    states = 2 * decay_ref.shape[1]
    names = ("projected", "mixed", "dh", "back")
    projected_ref, mixed_ref, dh_ref, back_ref = glu_pack(width, states).views(out_ref, *names)
    if k == 0:
        total_ref, normed_ref, slopes_ref, glu_ref, mix_ref, sems, weight_sems = refs
        pack = kept_pack(width, states)
        back_normed_ref, start_ref, later_ref = lift_pack(width, states).views(
            lift_pack_ref, "back_normed", "back", "normed"
        )
        slope_ref, gate_ref, gate_slope_ref = pack.views(slopes_ref, "slope", "gate", "gate_slope")
    group = ends_ref.shape[1]
    size = rows // BACK_BLOCKS
    steps = size // group
    where = Where(info_ref, seqs, rows // seqs)
    if k == 1:
        (wide_ref,) = refs
        shuffle_rows(wide_ref, start_ref)
    else:
        copies = {}
        for block, _, now in blocks_of(rows, group, reverse, BACK_BLOCKS):
            lanes = slice(0, 3 * width)
            copies[block] = copy_parts(kept_ref.at[now, lanes], slopes_ref.at[now, :], sems.at[0, block])
            copies[block] += copy_parts(normed_in.at[now, :], normed_ref.at[now, :], sems.at[1, block])
        weights = copy_parts(glu_in.at[k], glu_ref, weight_sems.at[0])
        weights += copy_parts(mix_in.at[k], mix_ref, weight_sems.at[1])
        for n, block in enumerate(order(BACK_BLOCKS, reverse)):
            begin(copies[block])
            if n == 0:
                begin(weights)
        sums = jnp.sum(sums_ref[...], axis=0)
        total_ref[...] = sums
        root, count = stats_ref[1:2, :], stats_ref[2:3, 0:1]
        gain, shift = gain_ref[1:2, :], shift_ref[1:2, :]
        by_normed = sums[0:1] / count
        fixed = (gain * sums[1:2] - shift * sums[0:1]) / count
    powers = Powers(k, True, where, decay_ref, phase_ref, *tables)
    left = where.steps_left()
    lam = powers.lam[...]
    ends_ref[...] = jnp.zeros_like(ends_ref)
    bias_grad = jnp.zeros((1, 2 * width), f32)
    skip_grad = jnp.zeros((1, width), f32)
    for block, first, now in blocks_of(rows, group, reverse, BACK_BLOCKS):
        valid = wide(valid_rows(left, first, steps), width)
        if k == 1:
            back = wide_ref[first : first + steps].reshape(size, width) * valid
        else:
            finished(copies[block])
            back = start_ref[now, :].astype(f32) + root * (
                gain * back_normed_ref[now, :].astype(f32)
                - valid * (fixed + by_normed * later_ref[now, :].astype(f32))
            )
        back_ref[now, :] = back.astype(bf16)
        value_back = (back * gate_ref[now, :].astype(f32)).astype(bf16)
        gate_back = (back * gate_slope_ref[now, :].astype(f32)).astype(bf16)
        back_projected = jnp.concatenate([value_back, gate_back], axis=1)
        projected_ref[now, :] = back_projected
        bias_grad += jnp.sum(back_projected.astype(f32), axis=0, keepdims=True)
        if k == 0 and block == BACK_BLOCKS - 1:
            finished(weights)
        back_activated = dot_t(back_projected, glu_ref[...])
        back_mixed = (slope_ref[now, :].astype(f32) * back_activated).astype(bf16)
        mixed_ref[now, :] = back_mixed
        skip_grad += jnp.sum(back_mixed.astype(f32) * normed_ref[now, :].astype(f32), axis=0, keepdims=True)
        back_state = dot_t(back_mixed, mix_ref[...]).astype(bf16)
        dh_ref[now, :] = back_state
        wide_state = back_state.astype(f32)

        def drive(t, real_lanes, imag_lanes):
            at = slice(t * group, (t + 1) * group)
            return wide_state[at, real_lanes], wide_state[at, imag_lanes]

        shift = 1 if reverse else -1
        scan_block(ends_ref, drive, left, lam, shift, first, steps, reverse)
    bias_grad_ref[...] = bias_grad
    skip_grad_ref[...] = skip_grad
    part = stretch_part(ends_ref, powers.table, reverse, seqs)
    for j in range(part_ref.shape[0]):
        part_ref[j] = part


def glu_back(k, seqs, seq_devices, info, inputs, arrays, away, rows, width, after, fetch, spill=()):
    states = inputs[0].shape[1]
    outs = [
        near((rows, glu_pack(width, 2 * states).width), bf16),
        moved((1, 2 * width), f32),
        moved((1, width), f32),
        near((2 * states // LANES, seqs * CHUNKS, LANES), f32),
        moved((seq_devices, seqs, 2 * states), f32),
    ]
    if k == 1:
        scratch = [pltpu.VMEM((rows // seqs // CHUNKS, seqs, CHUNKS, width), f32)]
    else:
        outs += [moved((2, width), f32), near((rows, width), bf16)]
        scratch = [
            pltpu.VMEM((rows, 3 * width), bf16),
            pltpu.VMEM((width, 2 * width), bf16),
            pltpu.VMEM((2 * states, width), bf16),
            pltpu.SemaphoreType.DMA((2, BACK_BLOCKS, 1)),
            pltpu.SemaphoreType.DMA((2, 1)),
        ]
    scratch += Powers.scratch(seqs, seq_devices, states, False)
    return call(
        partial(glu_back_kernel, k, seqs), info, inputs, arrays, away, outs, scratch, "glu_back", after, fetch, spill
    )


def lift_back_kernel(
    k, info_ref, parts_ref, stats_ref, skip_ref, decay_ref, phase_ref, gain_ref, shift_ref, *refs
):
    reverse = last = k == 0
    ends_ref, glu_pack_ref = refs[:2]
    states, width = 2 * decay_ref.shape[1], stats_ref.shape[1]
    mixed_ref, dh_ref, back_ref = glu_pack(width, states).views(glu_pack_ref, "mixed", "dh", "back")
    normed_ref, state_ref, weight_ref = refs[2:5]
    tables, refs = refs[-4:], refs[5:-4]
    if last:
        back_lifted_ref, sums_ref, lam_grad_ref, scale_grad_ref, ahead_ref = refs[:5]
        refs = refs[5:]
    else:
        out_ref, sums_ref, lam_grad_ref, scale_grad_ref = refs[:4]
        back_lifted_ref, back_normed_ref, kept_back_ref, kept_normed_ref = lift_pack(width, states).views(
            out_ref, "lifted", "back_normed", "back", "normed"
        )
        kept_back_ref[...] = back_ref[...]
        kept_normed_ref[...] = normed_ref[...]
        refs = refs[4:]
    h_ref, low_ref, acc_ref, lam_acc_ref, scale_acc_ref = refs
    rows, width = normed_ref.shape
    group = ends_ref.shape[1]
    seqs = parts_ref.shape[1]
    steps = rows // 1 // group
    states = decay_ref.shape[1]
    where = Where(info_ref, seqs, rows // seqs)
    powers = Powers(k, True, where, decay_ref, phase_ref, *tables)
    chunk_starts(h_ref, where.seq, parts_ref, powers.leaps, ends_ref, powers.table, reverse)
    lam_acc_ref[...] = jnp.zeros_like(lam_acc_ref)
    scale_acc_ref[...] = jnp.zeros_like(scale_acc_ref)
    left = where.steps_left()
    lam, scale = powers.lam[...], powers.scale[...]
    root, gain, shift_row = stats_ref[1:2, :], gain_ref[k : k + 1, :], shift_ref[k : k + 1, :]
    skip = skip_ref[k : k + 1, :]
    gain_sum = jnp.zeros((1, width), f32)
    shift_sum = jnp.zeros((1, width), f32)
    shift = 1 if reverse else -1
    for _, first, now in blocks_of(rows, group, reverse, 1):
        moving = [left > first + t + shift for t in range(steps)]
        valid = [left > first + t for t in range(steps)]
        dh = dh_ref[now, :].astype(f32)
        normed = normed_ref[now, :]
        lifted = dot(normed, weight_ref[...]).astype(bf16).astype(f32)
        state = state_ref[now, :].astype(f32)
        for low in range(0, states, LANES):
            real_lanes = slice(low, low + LANES)
            imag_lanes = slice(states + low, states + low + LANES)
            gr, gi = h_ref[low // LANES], h_ref[(states + low) // LANES]
            lr, li = lam[:, real_lanes], lam[:, imag_lanes]
            part = scale[:, real_lanes]
            sum_r, sum_i = lam_acc_ref[:, real_lanes], lam_acc_ref[:, imag_lanes]
            sum_s = scale_acc_ref[:, real_lanes]
            for t in order(steps, reverse):
                at = slice(t * group, (t + 1) * group)
                hr, hi = state[at, real_lanes], state[at, imag_lanes]
                ur, ui = lifted[at, real_lanes], lifted[at, imag_lanes]
                mr, mi = jnp.where(moving[t], gr, 0.0), jnp.where(moving[t], gi, 0.0)
                sum_r += mr * hr + mi * hi
                sum_i += mi * hr - mr * hi
                nr, ni = cmul(lr, li, gr, gi)
                gr = jnp.where(moving[t], nr, gr) + dh[at, real_lanes]
                gi = jnp.where(moving[t], ni, gi) + dh[at, imag_lanes]
                vr, vi = jnp.where(valid[t], gr, 0.0), jnp.where(valid[t], gi, 0.0)
                sum_s += vr * ur + vi * ui
                low_ref[at, real_lanes] = part * vr
                low_ref[at, imag_lanes] = part * vi
            h_ref[low // LANES] = gr
            h_ref[(states + low) // LANES] = gi
            lam_acc_ref[:, real_lanes] = sum_r
            lam_acc_ref[:, imag_lanes] = sum_i
            scale_acc_ref[:, real_lanes] = sum_s
        back_lifted = low_ref[...].astype(bf16)
        back_lifted_ref[now, :] = back_lifted
        back_normed = dot_t(back_lifted, weight_ref[...]) + skip * mixed_ref[now, :].astype(f32)
        gain_sum += jnp.sum(back_normed * normed.astype(f32), axis=0, keepdims=True)
        shift_sum += jnp.sum(back_normed, axis=0, keepdims=True)
        if last:
            ahead_ref[now, :] = (back_ref[now, :].astype(f32) + (root * gain) * back_normed).astype(bf16)
        else:
            back_normed_ref[now, :] = back_normed.astype(bf16)
    lam_grad = jnp.sum(lam_acc_ref[...], axis=0, keepdims=True)
    scale_grad = jnp.sum(scale_acc_ref[...], axis=0, keepdims=True)
    acc_ref[0:1, :] = (gain_sum - shift_row * shift_sum) / gain
    acc_ref[1:2, :] = shift_sum
    lam_grad_ref[...] = lam_grad
    scale_grad_ref[...] = scale_grad
    for j in range(sums_ref.shape[0]):
        sums_ref[j] = acc_ref[...]


def lift_back(k, info, inputs, arrays, devices, after=(), fetch=()):
    parts, stats, decay = inputs[0], inputs[1], inputs[3]
    ends, packed = arrays[:2]
    rows, width, states = packed.shape[0], stats.shape[1], 2 * decay.shape[1]
    seq_devices, seqs, _ = parts.shape
    table = ends.shape
    acc = (2, width)
    outs = [near((rows, states if k == 0 else lift_pack(width, states).width), bf16), moved((devices,) + acc, f32)]
    outs += [moved((1, states), f32), moved((1, states // 2), f32)]
    if k == 0:
        outs.append(moved((rows, width), bf16))
    scratch = [
        pltpu.VMEM(table, f32),
        pltpu.VMEM((rows // 1, states), f32),
        pltpu.VMEM(acc, f32),
        pltpu.VMEM((table[1], states), f32),
        pltpu.VMEM((table[1], states // 2), f32),
    ]
    scratch += Powers.scratch(seqs, seq_devices, states // 2, True)
    return call(partial(lift_back_kernel, k), info, inputs, arrays, (), outs, scratch, "lift_back", after, fetch)


def two_parts(rows):
    high = rows.astype(bf16).astype(f32)
    return jnp.concatenate([high, rows - high], axis=0)


def one_part(rows):
    half = rows.shape[0] // 2
    return rows[:half] + rows[half:]


def halves_kernel(parts, pairs, small, info_ref, *refs):
    keep_ref, send_ref = refs[-2:]
    width = keep_ref.shape[1]
    even = lax.axis_index("seq") % 2 == 0
    if small:
        small_refs, refs = refs[:4], refs[4:]
    products = [t_dot(*(refs[n][:, lanes] for n, lanes in pair)) for pair in pairs]
    first = 0
    for n, rows, (r, c), (q, d) in parts:
        a = products[n][r : r + rows, c : c + width].astype(bf16)
        b = products[n][q : q + rows, d : d + width].astype(bf16)
        keep_ref[first : first + rows, :] = jnp.where(even, a, b)
        send_ref[first : first + rows, :] = jnp.where(even, b, a)
        first += rows
    if small:
        skip_ref, bias_ref, lam_ref, scale_ref = small_refs
        extra = keep_ref.shape[0] - first
        low = jnp.concatenate([skip_ref[...], bias_ref[:, :width], bias_ref[:, width:]], axis=0)
        scale = jnp.concatenate([scale_ref[...], jnp.zeros((1, width - scale_ref.shape[1]), f32)], axis=1)
        high = jnp.concatenate([lam_ref[...], scale, jnp.zeros((1, width), f32)], axis=0)
        rest = [jnp.zeros((EXTRA // 2 - 3, width), f32)], [jnp.zeros((extra - EXTRA, width), f32)]
        low, high = (two_parts(jnp.concatenate([x, *rest[0]], axis=0)) for x in (low, high))
        low, high = (jnp.concatenate([x, *rest[1]], axis=0).astype(bf16) for x in (low, high))
        keep_ref[first:, :] = jnp.where(even, low, high)
        send_ref[first:, :] = jnp.where(even, high, low)


def halves(info, parts, pairs, small, arrays, width, name, after=()):
    rows = sum(p[1] for p in parts)
    if small:
        rows += EXTRA * (lax.axis_size("seq") // 2)
    outs = [moved((rows, width), bf16)] * 2
    return call(partial(halves_kernel, parts, pairs, bool(small)), info, small, arrays, (), outs, [], name, after)


def place_of(axis):
    return lax.axis_index("batch") if axis == "batch" else lax.axis_index("seq") // 2


def total_of(refs, rows):
    total = refs[0][rows, :].astype(f32)
    for ref in refs[1:]:
        total += ref[rows, :].astype(f32)
    return total


def split_kernel(chips, sets, xor, info_ref, *refs):
    n_in = 2 * len(sets)
    outs = refs[n_in:]
    place = place_of("seq")
    for m in range(chips):
        chip = place ^ m if xor else m
        low = 0
        for n, parts in enumerate(sets):
            first = 0
            for rows in parts:
                share = rows // chips
                start = first + chip * share
                if xor:
                    start = pl.multiple_of(start, 16)
                total = total_of(refs[2 * n : 2 * n + 2], pl.ds(start, share))
                if share == EXTRA:
                    total = two_parts(one_part(total))
                if xor:
                    outs[m][low : low + share, :] = total.astype(outs[m].dtype)
                else:
                    base = m * (outs[0].shape[0] // chips) + low
                    outs[0][base : base + share, :] = total.astype(outs[0].dtype)
                first, low = first + rows, low + share


def split(info, sets, arrays, xor, after=()):
    chips = lax.axis_size("seq") // 2
    width = arrays[0].shape[1]
    rows = sum(map(sum, sets))
    outs = [moved((rows, width), bf16)]
    if xor:
        outs = [moved((rows // chips, width), f32)] + [moved((rows // chips, width), bf16)] * (chips - 1)
    return call(partial(split_kernel, chips, sets, xor), info, arrays, (), (), outs, [], "split", after, us=0.8)


def cut_kernel(extra, info_ref, *refs):
    low_ref, refs = refs[-1], refs[:-1]
    batches, share, width = low_ref.shape
    arrays, outs = refs[:-batches], refs[-batches:]
    place = place_of("batch")
    rows = batches * share
    low_ref[...] = total_of(arrays, slice(0, rows)).reshape(batches, share, width)
    under = two_parts(one_part(total_of(arrays, slice(rows, rows + extra))))
    for m in range(batches):
        outs[m][:share, :] = low_ref[place ^ m].astype(outs[m].dtype)
        outs[m][share:, :] = under.astype(outs[m].dtype)


def cut(info, arrays, extra, after=()):
    batches = lax.axis_size("batch")
    rows, width = arrays[0].shape
    share = (rows - extra) // batches
    outs = [moved((share + extra, width), f32)] + [moved((share + extra, width), bf16)] * (batches - 1)
    scratch = [pltpu.VMEM((batches, share, width), f32)]
    return call(partial(cut_kernel, extra), info, arrays, (), (), outs, scratch, "cut", after, us=1.2)


def sum_kernel(info_ref, *refs):
    total = refs[0][...].astype(f32)
    for ref in refs[1:-1]:
        total += ref[...].astype(f32)
    rows = total.shape[0] - EXTRA
    refs[-1][:rows, :] = total[:rows].astype(bf16)
    refs[-1][rows:, :] = two_parts(one_part(total[rows:])).astype(bf16)


def sum_of(info, arrays, after=()):
    return call(sum_kernel, info, arrays, (), (), [moved(arrays[0].shape, bf16)], [], "total", after, us=0.6)


def join_kernel(info_ref, *refs):
    pieces, out_ref, low_ref = refs[:-2], refs[-2], refs[-1]
    batches, share, width = low_ref.shape
    place = place_of("batch")
    for m, ref in enumerate(pieces):
        low_ref[place ^ m] = ref[:share, :].astype(f32)
    rows = batches * share
    out_ref[:rows, :] = low_ref[...].reshape(rows, width).astype(bf16)
    out_ref[rows:, :] = pieces[0][share:, :]


def join(info, arrays, extra, after=()):
    batches = len(arrays)
    rows, width = arrays[0].shape
    share = rows - extra
    outs = [moved((batches * share + extra, width), bf16)]
    scratch = [pltpu.VMEM((batches, share, width), f32)]
    return call(join_kernel, info, arrays, (), (), outs, scratch, "join", after, us=0.6)


def trade(x, axis, mask):
    size = lax.axis_size(axis)
    return lax.ppermute(x, axis, [(i, i ^ mask) for i in range(size)])


def sent(arrays, axis, masks):
    return [arrays[0]] + [trade(x, axis, m) for x, m in zip(arrays[1:], masks)]


def to_others(x, axis, masks):
    return [x] + [trade(x, axis, m) for m in masks]


def gate_kernel(*refs):
    pass


def gate(info, arrays, after):
    anywhere = pl.BlockSpec(memory_space=pl.ANY)
    outs = [(anywhere, jax.ShapeDtypeStruct(x.shape, x.dtype)) for x in arrays]
    aliases = {1 + i: i for i in range(len(arrays))}
    return run(gate_kernel, info, list(arrays), [anywhere] * len(arrays), outs, [], "gate", after, aliases)


def small_grads(norms, rows, decay_log, phase_log, refs):
    gain_ref, shift_ref, decay_grad_ref, phase_grad_ref, skip_grad_ref, bias_grad_ref = refs
    blocks, states = decay_log.shape
    width = norms[0].shape[1]
    for k in range(blocks):
        gain_ref[k : k + 1, :], shift_ref[k : k + 1, :] = norms[k][0:1], norms[k][1:2]
        low, high = rows[k]
        skip, bias_low, bias_high, lam, scale = low[0:1], low[1:2], low[2:3], high[0:1], high[1:2]
        skip_grad_ref[k : k + 1, :] = skip
        bias_grad_ref[k : k + 1, :width] = bias_low
        bias_grad_ref[k : k + 1, width:] = bias_high
        rate, angle = jnp.exp(decay_log[k : k + 1]), jnp.exp(phase_log[k : k + 1])
        size, fade = jnp.exp(-rate), jnp.exp(-2.0 * rate)
        lam_real, lam_imag = size * jnp.cos(angle), size * jnp.sin(angle)
        real, imag = lam[:, :states], lam[:, states : 2 * states]
        by_rate = scale[:, :states] * fade * lax.rsqrt(1.0 - fade) - (real * lam_real + imag * lam_imag)
        decay_grad_ref[k : k + 1, :] = rate * by_rate
        phase_grad_ref[k : k + 1, :] = angle * (imag * lam_real - real * lam_imag)


def input_grad(where, sums, stats_ref, gain_ref, tokens_ref, wide_ref, grad_ref):
    seqs, span, width = tokens_ref.shape
    shuffle = shuffle_matrix(span, True)
    average, root = stats_ref[0:1, :], stats_ref[1:2, :]
    factor = root * gain_ref[0:1, :] / stats_ref[2:3, 0:1]
    by_gain = factor * sums[0:1] * root
    fixed = factor * sums[1:2] - by_gain * average
    step = lax.broadcasted_iota(jnp.int32, (span, 1), 0)
    for s in range(seqs):
        valid = (step < where.lefts[s]).astype(f32)
        ahead = dot(shuffle, wide_ref[:, s].reshape(span, width).astype(bf16))
        grad_ref[s] = (ahead - valid * (fixed + by_gain * tokens_ref[s].astype(f32))).astype(bf16)


def results_kernel(chips, info_ref, sums_ref, norm1_ref, decay_ref, phase_ref, stats_ref, gain_ref, *refs):
    (tokens_in, ahead_in), pieces, refs = refs[:2], refs[2 : 2 + 4 * chips], refs[2 + 4 * chips :]
    glu_ref, mix_ref, lift_ref, grad_out, *small_refs = refs[:10]
    low_ref, wide_ref, tokens_ref, ahead_ref, rows_ref, grad_ref, in_sems, sems, own_sems = refs[10:]
    own = [
        pltpu.make_async_copy(ahead_in, ahead_ref, own_sems.at[0]),
        pltpu.make_async_copy(tokens_in, tokens_ref, own_sems.at[1]),
    ]
    place = place_of("seq")
    core = lax.axis_index("seq") % 2
    _, rows, width = wide_ref.shape
    half, quarter = rows // 2, rows // 4
    arriving = []
    for n, piece in enumerate(pieces):
        parts = [pltpu.make_async_copy(piece, low_ref.at[n], in_sems.at[n])]
        begin(parts)
        arriving.append(parts)
    begin(own)
    copies = []
    extras = [[jnp.zeros((EXTRA // 2, width), f32)] * 2 for _ in range(2)]
    for n in range(4 * chips):
        finished(arriving[n])
        k, n_in = divmod(n, 2 * chips)
        chip, side = place ^ (n_in % chips), core if n_in < chips else 1 - core
        extra = one_part(low_ref[n, rows:, :].astype(f32))
        extras[k][n_in // chips] = jnp.where(chip == 0, extra, extras[k][n_in // chips])
        column = pl.multiple_of(side * width, width)
        row = pl.multiple_of(chip * half, 8)
        low = pl.multiple_of(side * (quarter * chips) + chip * quarter, 8)
        wide_ref[n] = low_ref[n, :rows, :].astype(f32)
        for i, (first, size, target) in enumerate(
            (
                (0, half, glu_ref.at[k, pl.ds(row, half), pl.ds(column, width)]),
                (half, quarter, mix_ref.at[k, pl.ds(low, quarter), :]),
                (half + quarter, quarter, lift_ref.at[k, pl.ds(low, quarter), :]),
            )
        ):
            copies.append(pltpu.make_async_copy(wide_ref.at[n, pl.ds(first, size), :], target, sems.at[n, i]))
            copies[-1].start()
    even = core == 0
    sums = sums_ref[...]
    finished(own)
    rows_ref[...] = ahead_ref[...].astype(f32).reshape(rows_ref.shape)
    seqs, span, _ = tokens_ref.shape
    input_grad(Where(info_ref, seqs, span), sums, stats_ref, gain_ref, tokens_ref, rows_ref, grad_ref)
    copies.append(pltpu.make_async_copy(grad_ref, grad_out, own_sems.at[2]))
    copies[-1].start()
    small_grads(
        (sums, norm1_ref[...]),
        [(jnp.where(even, mine, other), jnp.where(even, other, mine)) for mine, other in extras],
        decay_ref[...],
        phase_ref[...],
        small_refs,
    )
    finished(copies)


def results(info, sums, norm1, decay_log, phase_log, stats, gain, tokens, ahead, pieces, after=()):
    seqs, span, _ = tokens.shape
    rows, width = pieces[0].shape
    rows -= EXTRA
    count = len(pieces)
    anywhere = pl.BlockSpec(memory_space=pl.ANY)
    shapes = [(2, width, 2 * width), (2, width, width), (2, width, width)]
    outs = [(anywhere, jax.ShapeDtypeStruct(shape, f32)) for shape in shapes]
    outs.append((anywhere, jax.ShapeDtypeStruct(tokens.shape, bf16)))
    blocks, states = decay_log.shape
    outs += [moved((blocks, n), f32) for n in (width, width, states, states, width, 2 * width)]
    scratch = [
        pltpu.VMEM((count, rows + EXTRA, width), bf16),
        pltpu.VMEM((count, rows, width), f32),
        pltpu.VMEM(tokens.shape, bf16),
        pltpu.VMEM(ahead.shape, bf16),
        pltpu.VMEM((span // CHUNKS, seqs, CHUNKS, width), f32),
        pltpu.VMEM(tokens.shape, bf16),
        pltpu.SemaphoreType.DMA((count,)),
        pltpu.SemaphoreType.DMA((count, 3)),
        pltpu.SemaphoreType.DMA((3,)),
    ]
    inputs = [sums, norm1, decay_log, phase_log, stats, gain]
    given = [*inputs, *map(there, (tokens, ahead)), *pieces]
    specs = [in_vmem] * len(inputs) + [in_hbm] * 2 + [anywhere] * count
    return run(partial(results_kernel, count // 4), info, given, specs, outs, scratch, "results", after, us=7.0)


def norms_kernel(info_ref, sums_ref, total_ref):
    total_ref[...] = jnp.sum(sums_ref[...], axis=0)


def norms(info, sums, after=()):
    outs = [moved(sums.shape[1:], f32)]
    return call(norms_kernel, info, (sums,), (), (), outs, [], "norms", after, us=0.6)


def leave_kernel(seqs, info_ref, rows_ref, out_ref, wide_ref):
    _, span, width = out_ref.shape
    wide_ref[...] = rows_ref[...].astype(f32).reshape(wide_ref.shape)
    shuffle = shuffle_matrix(span, True)
    for s in range(seqs):
        out_ref[s] = dot(shuffle, wide_ref[:, s].reshape(span, width).astype(bf16)).astype(bf16)


def leave(info, rows, seqs, after=()):
    span, width = rows.shape[0] // seqs, rows.shape[1]
    scratch = [pltpu.VMEM((span // CHUNKS, seqs, CHUNKS, width), f32)]
    outs = [moved((seqs, span, width), bf16)]
    return call(partial(leave_kernel, seqs), info, (rows,), (), (), outs, scratch, "leave", after)


def to_all(x, axes):
    return lax.all_to_all(x, axes, split_axis=0, concat_axis=0, tiled=True)


def local(
    tokens,
    lengths,
    cotangent,
    norm_gain,
    norm_shift,
    lift_weight,
    decay_log,
    phase_log,
    skip_gain,
    mix_weight,
    glu_weight,
    glu_bias,
):
    both = ("seq", "batch")
    seq_devices, batches = lax.axis_size("seq"), lax.axis_size("batch")
    devices, chips = seq_devices * batches, seq_devices // 2
    seqs, span, width = tokens.shape
    rows = seqs * span
    info = lengths
    turns = (decay_log, phase_log)
    norms_in = (norm_gain, norm_shift)
    states = decay_log.shape[1]
    half = width // 2

    sums, tokens_here, lift_w = enter(info, tokens, devices, [(lift_weight, 0)])
    sums = to_all(sums, both)
    normed, lifted, ends, part, stats0, x, mix_w, glu_w = lift(
        0, seqs, seq_devices, info, (sums, *norms_in, *turns), (tokens_here, lift_w), rows,
        [(mix_weight, 0), (glu_weight, 0)],
    )
    x1, sums, kept, lift_w, normed0 = mix(
        0, info, (to_all(part, "seq"), skip_gain, glu_bias, *turns), (ends, lifted, normed, x, mix_w, glu_w),
        devices, [(lift_weight, 1)], (normed,),
    )
    sums = to_all(sums, both)

    normed1, lifted1, ends, part, stats1, mix_w, glu_w = lift(
        1, seqs, seq_devices, info, (sums, *norms_in, *turns, stats0), (x1, lift_w), rows,
        [(mix_weight, 1), (glu_weight, 1)],
    )
    state1, activated1, slope1, gate1, gate_slope1, masked, cot = mix(
        1, info, (to_all(part, "seq"), skip_gain, glu_bias, *turns), (ends, lifted1, normed1, x1, mix_w, glu_w),
        devices, [(cotangent, None)],
    )

    glu_packed, bias_grad1, skip_grad1, ends, part, lift_w, masked = glu_back(
        1, seqs, seq_devices, info, turns, (cot, normed1, slope1, gate1, gate_slope1, glu_w, mix_w), (), rows, width,
        (), [(lift_weight, 1)], [masked],
    )
    lift_packed, sums, lam_grad1, scale_grad1 = lift_back(
        1, info, (to_all(part, "seq"), stats1, skip_gain, *turns, *norms_in),
        (ends, glu_packed, normed1, state1, lift_w), devices,
    )
    glu_part, mix_part, lift_part = (0, width, (0, 0), (0, width)), (1, half, (0, 0), (half, 0)), (2, half, (0, 0), (half, 0))
    glu_lanes, lift_lanes = glu_pack(width, 2 * states).lanes, lift_pack(width, 2 * states).lanes
    kept_lanes, every = kept_pack(width, 2 * states).lanes, slice(None)
    out = halves(
        info,
        (glu_part, mix_part, lift_part),
        (
            ((0, every), (1, glu_lanes["projected"])),
            ((2, every), (1, glu_lanes["mixed"])),
            ((3, every), (4, lift_lanes["lifted"])),
        ),
        (skip_grad1, bias_grad1, lam_grad1, scale_grad1),
        (activated1, glu_packed, state1, normed1, lift_packed),
        width,
        "halves1",
    )
    keep1, send = out
    got1 = trade(send, "seq", 1)
    (produced,) = out = leave(info, masked, seqs, (out.tick,))
    shares = (width, half, half)
    z, xy = range(1, batches), range(2, seq_devices, 2)
    extra = EXTRA * chips
    out = split(info, ((*shares, extra),), [keep1, got1], True, (out.tick,))
    pieces1 = sent(out, "seq", xy)
    sums = to_all(sums, both)

    state_lanes = (slice(None), kept_lanes["state"])
    out = glu_back(
        0, seqs, seq_devices, info, (*turns, sums, stats1, *norms_in), (lift_packed,),
        (kept, normed0, glu_weight, mix_weight), rows, width, (),
        [(kept, state_lanes), (lift_weight, 0)],
    )
    glu_packed, bias_grad0, skip_grad0, ends, part, norm_sums1, normed, state, lift_w = out
    activated_lanes = (slice(None), kept_lanes["activated"])
    parts, *pieces1 = gate(info, [to_all(part, "seq"), *pieces1], ())
    back_lifted0, sums, lam_grad0, scale_grad0, ahead, activated = out = lift_back(
        0, info, (parts, stats0, skip_gain, *turns, *norms_in),
        (ends, glu_packed, normed, state, lift_w), devices, (), [(kept, activated_lanes)],
    )

    keep0, send = out = halves(
        info,
        (glu_part, mix_part, lift_part),
        (
            ((0, every), (1, glu_lanes["projected"])),
            ((2, every), (1, glu_lanes["mixed"])),
            ((3, every), (4, every)),
        ),
        (skip_grad0, bias_grad0, lam_grad0, scale_grad0),
        (activated, glu_packed, state, normed, back_lifted0),
        width,
        "halves0",
    )
    got0 = trade(send, "seq", 1)
    out1 = cut(info, pieces1, EXTRA, (out.tick,))
    out0 = split(info, ((*shares, extra),), [keep0, got0], True, (out1.tick,))
    sum1 = sum_of(info, sent(out1, "batch", z), (out0.tick,))
    (sums,) = gate(info, [sums], (sum1.tick,))
    sums = to_all(sums, both)
    (own1,) = out = join(info, to_others(sum1[0], "batch", z), EXTRA, (sum1.tick,))
    out0 = cut(info, sent(out0, "seq", xy), EXTRA, (out.tick,))
    sum0 = sum_of(info, sent(out0, "batch", z))
    (own0,) = out = join(info, to_others(sum0[0], "batch", z), EXTRA)
    (sums,) = norms(info, sums, (out.tick,))
    pieces = []
    for own in (own0, own1):
        total = to_others(own, "seq", xy)
        pieces += total + [trade(x, "seq", 1) for x in total]
    out = results(info, sums, norm_sums1, *turns, stats0, norm_gain, tokens, ahead, pieces)
    grad_glu, grad_mix, grad_lift, tokens_grad, grad_gain, grad_shift, grad_decay, grad_phase, grad_skip, grad_bias = out
    return (
        produced,
        tokens_grad,
        grad_gain,
        grad_shift,
        grad_lift,
        grad_decay,
        grad_phase,
        grad_skip,
        grad_mix,
        grad_glu,
        grad_bias,
    )


def solution(mesh):
    split = P("batch", "seq", None)
    placed = (split, P("batch"), split) + (P(),) * 9
    return jax.shard_map(
        local,
        mesh=mesh,
        in_specs=placed,
        out_specs=(split, split) + (P(),) * 9,
        check_vma=False,
    )
```

```python
from functools import partial

import jax
import jax.numpy as jnp
from jax import lax
from jax.experimental import pallas as pl
from jax.experimental.pallas import tpu as pltpu
from jax.sharding import PartitionSpec as P

norm_eps = 1e-05
f32 = jnp.float32
bf16 = jnp.bfloat16

CHUNKS = 8
BLOCKS = 4
BACK_BLOCKS = 2
PARTS = 1
EXTRA = 16
LANES = 128
VMEM_LIMIT = 32 * 1024 * 1024

in_vmem = pl.BlockSpec(memory_space=pltpu.VMEM)
in_smem = pl.BlockSpec(memory_space=pltpu.SMEM)
in_hbm = pl.BlockSpec(memory_space=pltpu.HBM)


def near(shape, dtype):
    return in_vmem, pltpu.VMEM(shape, dtype)


def moved(shape, dtype):
    return in_vmem, jax.ShapeDtypeStruct(shape, dtype)


def copy_parts(source, target, sems):
    size = source.shape[0] // sems.shape[0]
    cuts = [pl.ds(i * size, size) for i in range(sems.shape[0])]
    return [pltpu.make_async_copy(source.at[cut], target.at[cut], sems.at[i]) for i, cut in enumerate(cuts)]


def begin(copies):
    for copy in copies:
        copy.start()


def finished(copies):
    for copy in copies:
        copy.wait()


class Outs(list):
    tick = None


def run(body, info, given, specs, outs, scratch, name, after, aliases=(), us=None):
    cost = None
    if us is not None:
        cost = pl.CostEstimate(flops=int(us * 1.1e9), bytes_accessed=int(us * 3e6), transcendentals=0)
    after = [pltpu.with_memory_space_constraint(t, pltpu.HBM) for t in after]
    n_in, n_out = 1 + len(given), len(outs)

    def ticking(*refs):
        body(*refs[:n_in], *refs[n_in + len(after) : n_in + len(after) + n_out], *refs[n_in + len(after) + n_out + 1 :])

    out = pl.pallas_call(
        ticking,
        in_specs=[in_smem] + specs + [in_hbm] * len(after),
        out_specs=[spec for spec, _ in outs] + [in_hbm],
        out_shape=[shape for _, shape in outs] + [pltpu.HBM((8, LANES), f32)],
        scratch_shapes=scratch,
        input_output_aliases=dict(aliases),
        compiler_params=pltpu.CompilerParams(vmem_limit_bytes=VMEM_LIMIT),
        cost_estimate=cost,
        name=name,
    )(info, *given, *after)
    result = Outs(out[:n_out])
    result.tick = out[n_out]
    return result


def here(x):
    return pltpu.with_memory_space_constraint(x, pltpu.VMEM)


def there(x):
    return pltpu.with_memory_space_constraint(x, pltpu.HBM)


def call(kernel, info, inputs, arrays, away, outs, scratch, name, after=(), fetch=(), spill=(), us=None, late=False):
    first = 1 + len(inputs) + len(arrays) + len(away)
    n_copies = len(fetch) + len(spill)
    fetched = [jax.eval_shape(lambda x, at=at: x if at is None else x[at], a) for a, at in fetch]
    outs = list(outs)
    n_outs = len(outs)
    outs += [near(a.shape, a.dtype) for a in fetched] + [(in_hbm, pltpu.HBM(a.shape, a.dtype)) for a in spill]

    def body(*refs):
        ins, rest = refs[: first + n_copies], refs[first + n_copies :]
        sources = list(ins[first:])
        for i, (_, at) in enumerate(fetch):
            if at is not None:
                sources[i] = sources[i].at[at]
        targets = rest[n_outs : n_outs + n_copies]
        rest = rest[:n_outs] + rest[n_outs + n_copies :]
        copies = []
        for i, (x, y) in enumerate(zip(sources, targets)):
            copies += copy_parts(x, y, rest[-1].at[i])
        own = (*ins[:first], *(rest[:-1] if copies else rest))
        if late:
            kernel(*own, begin_others=lambda: begin(copies))
        else:
            begin(copies)
            kernel(*own)
        finished(copies)

    given = [*inputs, *map(here, arrays), *map(there, away), *(there(a) for a, _ in fetch), *map(here, spill)]
    specs = [in_vmem] * (len(inputs) + len(arrays)) + [in_hbm] * (len(away) + len(fetch)) + [in_vmem] * len(spill)
    scratch = list(scratch) + [pltpu.SemaphoreType.DMA((n_copies, PARTS))] * bool(n_copies)
    return run(body, info, given, specs, outs, scratch, name, after, us=us)


class Pack:
    def __init__(self, *fields):
        self.lanes, self.width = {}, 0
        for name, width in fields:
            self.lanes[name] = slice(self.width, self.width + width)
            self.width += width

    def views(self, ref, *names):
        return [ref.at[:, self.lanes[n]] for n in names]


def kept_pack(width, states):
    return Pack(*((n, width) for n in ("slope", "gate", "gate_slope", "activated")), ("state", states))


def glu_pack(width, states):
    return Pack(("projected", 2 * width), ("mixed", width), ("dh", states), ("back", width))


def lift_pack(width, states):
    return Pack(("lifted", states), ("back_normed", width), ("back", width), ("normed", width))


def wide(mask, width):
    return jnp.concatenate([mask] * (width // LANES), axis=1)


def dot(a, b):
    return lax.dot_general(a, b, (((1,), (0,)), ((), ())), preferred_element_type=f32)


def dot_t(a, b):
    return lax.dot_general(a, b, (((1,), (1,)), ((), ())), preferred_element_type=f32)


def t_dot(a, b):
    return lax.dot_general(a, b, (((0,), (0,)), ((), ())), preferred_element_type=f32)


def cmul(ar, ai, br, bi):
    return ar * br - ai * bi, ar * bi + ai * br


def order(steps, reverse):
    return range(steps - 1, -1, -1) if reverse else range(steps)


def shuffle_matrix(span, back):
    chunk = span // CHUNKS
    place = lax.broadcasted_iota(jnp.int32, (span, span), 0)
    source = lax.broadcasted_iota(jnp.int32, (span, span), 1)
    if back:
        wanted = (place % chunk) * CHUNKS + place // chunk
    else:
        wanted = (place % CHUNKS) * chunk + place // CHUNKS
    return (source == wanted).astype(f32).astype(bf16)


class Where:
    def __init__(self, info_ref, seqs, span):
        self.seq = lax.axis_index("seq")
        self.seqs, self.span = seqs, span
        self.lengths = [info_ref[s] for s in range(seqs)]
        self.lefts = [length - self.seq * span for length in self.lengths]

    def steps_left(self):
        before = (self.span // CHUNKS) * lax.broadcasted_iota(jnp.int32, (CHUNKS, LANES), 0)
        return jnp.concatenate([left - before for left in self.lefts], axis=0)


def valid_rows(left, first, steps):
    return jnp.concatenate([(left > first + t).astype(f32) for t in range(steps)], axis=0)


def shuffle_rows(wide_ref, source_ref):
    steps, seqs, chunks, width = wide_ref.shape
    shuffle = shuffle_matrix(steps * chunks, False)
    for s in range(seqs):
        wide_ref[:, s] = dot(shuffle, source_ref[s]).reshape(steps, chunks, width)


def enter_kernel(info_ref, tokens_ref, sums_ref, here_ref, acc_ref, sems):
    seqs, span, width = tokens_ref.shape
    copies = [copy_parts(tokens_ref.at[s], here_ref.at[s], sems.at[s]) for s in range(seqs)]
    for parts in copies:
        begin(parts)
    where = Where(info_ref, seqs, span)
    step = lax.broadcasted_iota(jnp.int32, (span, 1), 0)
    total = jnp.zeros((1, width), f32)
    squares = jnp.zeros((1, width), f32)
    count = jnp.zeros((1, 1), f32)
    for s in range(seqs):
        valid = (step < where.lefts[s]).astype(f32)
        finished(copies[s])
        x = here_ref[s].astype(f32)
        masked = x * valid
        total += jnp.sum(masked, axis=0, keepdims=True)
        squares += jnp.sum(masked * x, axis=0, keepdims=True)
        count += jnp.sum(valid, axis=0, keepdims=True)
    tail = jnp.broadcast_to(count, (1, LANES))
    acc_ref[0:1, :] = jnp.concatenate([total, tail], axis=1)
    acc_ref[1:2, :] = jnp.concatenate([squares, tail], axis=1)
    for j in range(sums_ref.shape[0]):
        sums_ref[j] = acc_ref[...]


def enter(info, tokens, devices, fetch):
    seqs, _, width = tokens.shape
    outs = [moved((devices, 2, width + LANES), f32), near(tokens.shape, bf16)]
    scratch = [pltpu.VMEM((2, width + LANES), f32), pltpu.SemaphoreType.DMA((seqs, 1))]
    return call(enter_kernel, info, (), (), (tokens,), outs, scratch, "enter", fetch=fetch)


class Powers:
    @staticmethod
    def scratch(seqs, seq_devices, states, leaps):
        tables = [((1, 2 * states), f32), ((1, states), f32), ((2 * states // LANES, seqs * CHUNKS, LANES), f32)]
        if leaps:
            tables.append(((seq_devices * seqs, 2 * states), f32))
        return [pltpu.VMEM(*t) for t in tables]

    def __init__(self, k, back, where, decay_ref, phase_ref, lam_ref, scale_ref, table_ref, leap_ref=None):
        states = scale_ref.shape[1]
        groups, group = states // LANES, table_ref.shape[1]
        seqs, span, limit = where.seqs, where.span, where.span // CHUNKS
        rate = jnp.exp(decay_ref[k : k + 1, :])
        size, angle = jnp.exp(-rate), jnp.exp(phase_ref[k : k + 1, :])
        lam_ref[:, :states] = size * jnp.cos(angle)
        lam_ref[:, states:] = size * jnp.sin(angle) * (-1.0 if back else 1.0)
        scale_ref[...] = jnp.sqrt(1.0 - jnp.exp(-2.0 * rate))
        self.lam, self.scale, self.table, self.leaps = lam_ref, scale_ref, table_ref, leap_ref
        shift = 0 if not back else (-1 if k == 0 else 1)
        chunk_count = jnp.clip(where.steps_left() + shift, 0, limit)
        if leap_ref is not None:
            total = leap_ref.shape[0]
            line = lax.broadcasted_iota(jnp.int32, (total, LANES), 0)
            span_left = jnp.zeros((total, LANES), jnp.int32)
            for s, length in enumerate(where.lengths):
                span_left = jnp.where(line % seqs == s, length - span * (line // seqs), span_left)
            span_count = jnp.clip(span_left + shift, 0, span)
        for low in range(groups):
            real_lanes = slice(low * LANES, (low + 1) * LANES)
            imag_lanes = slice((groups + low) * LANES, (groups + low + 1) * LANES)
            br, bi = lam_ref[:, real_lanes], lam_ref[:, imag_lanes]
            cr = jnp.ones((group, LANES), f32)
            ci = jnp.zeros((group, LANES), f32)
            if leap_ref is not None:
                pr = jnp.ones((total, LANES), f32)
                pi = jnp.zeros((total, LANES), f32)
            for bit in range((limit if leap_ref is None else span).bit_length()):
                if (1 << bit) <= limit:
                    nr, ni = cmul(cr, ci, br, bi)
                    odd = (chunk_count & (1 << bit)) != 0
                    cr, ci = jnp.where(odd, nr, cr), jnp.where(odd, ni, ci)
                if leap_ref is not None:
                    nr, ni = cmul(pr, pi, br, bi)
                    odd = (span_count & (1 << bit)) != 0
                    pr, pi = jnp.where(odd, nr, pr), jnp.where(odd, ni, pi)
                br, bi = cmul(br, bi, br, bi)
            table_ref[low] = cr
            table_ref[groups + low] = ci
            if leap_ref is not None:
                leap_ref[:, real_lanes] = pr
                leap_ref[:, imag_lanes] = pi


def stretch_part(ends_ref, power_ref, reverse, seqs):
    groups = ends_ref.shape[0] // 2
    reals, imags = [], []
    for low in range(groups):
        real = jnp.zeros((seqs, LANES), f32)
        imag = jnp.zeros((seqs, LANES), f32)
        for c in order(CHUNKS, reverse):
            here = pl.ds(c, seqs, stride=CHUNKS)
            real, imag = cmul(power_ref[low, here, :], power_ref[groups + low, here, :], real, imag)
            real += ends_ref[low, here, :]
            imag += ends_ref[groups + low, here, :]
        reals.append(real)
        imags.append(imag)
    return jnp.concatenate(reals + imags, axis=1)


def chunk_starts(start_ref, place, parts_ref, leaps_ref, ends_ref, power_ref, reverse):
    devices, seqs, width = parts_ref.shape
    states = width // 2
    groups = states // LANES
    real = jnp.zeros((seqs, states), f32)
    imag = jnp.zeros((seqs, states), f32)
    for j in order(devices, reverse):
        ahead = (j > place) if reverse else (j < place)
        leap, part = leaps_ref[seqs * j : seqs * (j + 1), :], parts_ref[j]
        next_real, next_imag = cmul(leap[:, :states], leap[:, states:], real, imag)
        real = jnp.where(ahead, next_real + part[:, :states], real)
        imag = jnp.where(ahead, next_imag + part[:, states:], imag)
    for low in range(groups):
        hr = real[:, low * LANES : (low + 1) * LANES]
        hi = imag[:, low * LANES : (low + 1) * LANES]
        for c in order(CHUNKS, reverse):
            here = pl.ds(c, seqs, stride=CHUNKS)
            start_ref[low, here, :] = hr
            start_ref[groups + low, here, :] = hi
            hr, hi = cmul(power_ref[low, here, :], power_ref[groups + low, here, :], hr, hi)
            hr += ends_ref[low, here, :]
            hi += ends_ref[groups + low, here, :]


def scan_block(h_ref, drive, left, lam, shift, first, steps, reverse, out_ref=None):
    groups, group, _ = h_ref.shape
    groups = groups // 2
    masks = [left > first + t + shift for t in range(steps)]
    for low in range(groups):
        real_lanes = slice(low * LANES, (low + 1) * LANES)
        imag_lanes = slice((groups + low) * LANES, (groups + low + 1) * LANES)
        hr, hi = h_ref[low], h_ref[groups + low]
        lr, li = lam[:, real_lanes], lam[:, imag_lanes]
        for t in order(steps, reverse):
            ur, ui = drive(t, real_lanes, imag_lanes)
            nr, ni = cmul(lr, li, hr, hi)
            hr = jnp.where(masks[t], nr, hr) + ur
            hi = jnp.where(masks[t], ni, hi) + ui
            if out_ref is not None:
                out_ref[t * group : (t + 1) * group, real_lanes] = hr
                out_ref[t * group : (t + 1) * group, imag_lanes] = hi
        h_ref[low] = hr
        h_ref[groups + low] = hi


def input_drive(lifted, scale, left, first, steps):
    group = left.shape[0]
    masks = [left > first + t for t in range(steps)]

    def drive(t, real_lanes, imag_lanes):
        here = slice(t * group, (t + 1) * group)
        factor = jnp.where(masks[t], scale[:, real_lanes], 0.0)
        return factor * lifted[here, real_lanes], factor * lifted[here, imag_lanes]

    return drive


def blocks_of(rows, group, reverse, blocks=BLOCKS):
    size = rows // blocks
    for block in order(blocks, reverse):
        yield block, block * (size // group), slice(block * size, (block + 1) * size)


def lift_kernel(k, seqs, info_ref, sums_ref, gain_ref, shift_ref, decay_ref, phase_ref, *refs):
    reverse = k == 1
    if k == 0:
        x_ref, weight_ref, normed_ref, lifted_ref, ends_ref, part_ref, stats_ref, rows_ref, wide_ref = refs[:9]
        refs = refs[9:]
    else:
        count_ref, x_ref, weight_ref, normed_ref, lifted_ref, ends_ref, part_ref, stats_ref = refs[:8]
        refs = refs[8:]
    rows, width = normed_ref.shape
    group = ends_ref.shape[1]
    size = rows // BLOCKS
    steps = size // group
    where = Where(info_ref, seqs, rows // seqs)
    powers = Powers(k, False, where, decay_ref, phase_ref, *refs)
    if k == 0:
        shuffle_rows(wide_ref, x_ref)
    sums = jnp.sum(sums_ref[...], axis=0)
    if k == 0:
        count = sums[0:1, width : width + 1]
    else:
        count = count_ref[2:3, 0:1]
    average = sums[0:1, :width] / count
    root = lax.rsqrt(sums[1:2, :width] / count - average * average + norm_eps)
    stats_ref[0:1, :] = average
    stats_ref[1:2, :] = root
    stats_ref[2:3, :] = jnp.broadcast_to(count, (1, width))
    gain, shift = gain_ref[k : k + 1, :], shift_ref[k : k + 1, :]
    lam, scale = powers.lam[...], powers.scale[...]
    left = where.steps_left()
    ends_ref[...] = jnp.zeros_like(ends_ref)
    for _, first, now in blocks_of(rows, group, reverse):
        if k == 0:
            x = wide_ref[first : first + steps].reshape(size, width)
            rows_ref[now, :] = x.astype(bf16)
        else:
            x = x_ref[now, :]
        normed = ((x - average) * root * gain + shift).astype(bf16)
        normed_ref[now, :] = normed
        lifted = dot(normed, weight_ref[...]).astype(bf16)
        lifted_ref[now, :] = lifted
        drive = input_drive(lifted.astype(f32), scale, left, first, steps)
        scan_block(ends_ref, drive, left, lam, 0, first, steps, reverse)
    part = stretch_part(ends_ref, powers.table, reverse, seqs)
    for j in range(part_ref.shape[0]):
        part_ref[j] = part


def lift(k, seqs, seq_devices, info, inputs, arrays, rows, fetch):
    gain, decay = inputs[1], inputs[3]
    width, states = gain.shape[1], decay.shape[1]
    outs = [
        near((rows, width), bf16),
        near((rows, 2 * states), bf16),
        near((2 * states // LANES, seqs * CHUNKS, LANES), f32),
        moved((seq_devices, seqs, 2 * states), f32),
        moved((8, width), f32),
    ]
    scratch = []
    if k == 0:
        outs.append(near((rows, width), bf16))
        scratch.append(pltpu.VMEM((rows // seqs // CHUNKS, seqs, CHUNKS, width), f32))
    scratch += Powers.scratch(seqs, seq_devices, states, False)
    return call(partial(lift_kernel, k, seqs), info, inputs, arrays, (), outs, scratch, "lift", fetch=fetch)


def mix_kernel(k, info_ref, parts_ref, skip_ref, bias_ref, decay_ref, phase_ref, *refs):
    reverse = k == 1
    (ends_ref, lifted_ref, normed_ref, x_ref, mix_ref, glu_ref) = refs[:6]
    tables, refs = refs[-4:], refs[6:-4]
    if reverse:
        state_ref, activated_ref, slope_ref, gate_ref, gate_slope_ref, masked_ref, h_ref, states_ref = refs
    else:
        next_ref, sums_ref, kept_out, h_ref, states_ref, acc_ref, kept_ref, sems = refs
        pack = kept_pack(x_ref.shape[1], lifted_ref.shape[1])
        state_ref, activated_ref, slope_ref, gate_ref, gate_slope_ref = pack.views(
            kept_ref, "state", "activated", "slope", "gate", "gate_slope"
        )
        copies = []
    seqs = parts_ref.shape[1]
    rows, width = x_ref.shape
    group = ends_ref.shape[1]
    blocks = 2 if reverse else BLOCKS
    steps = rows // blocks // group
    where = Where(info_ref, seqs, rows // seqs)
    powers = Powers(k, False, where, decay_ref, phase_ref, *tables)
    chunk_starts(h_ref, where.seq, parts_ref, powers.leaps, ends_ref, powers.table, reverse)
    left = where.steps_left()
    skip, bias = skip_ref[k : k + 1, :], bias_ref[k : k + 1, :]
    lam, scale = powers.lam[...], powers.scale[...]
    total = jnp.zeros((1, width), f32)
    squares = jnp.zeros((1, width), f32)
    for block, first, now in blocks_of(rows, group, reverse, blocks):
        drive = input_drive(lifted_ref[now, :].astype(f32), scale, left, first, steps)
        scan_block(h_ref, drive, left, lam, 0, first, steps, reverse, states_ref)
        state = states_ref[...].astype(bf16)
        state_ref[now, :] = state
        mixed = dot(state, mix_ref[...]) + skip * normed_ref[now, :].astype(f32)
        base, cube = 0.7978845608028654, 0.044715
        square = mixed * mixed
        bend = jnp.tanh(mixed * (base + (base * cube) * square))
        half = 0.5 + 0.5 * bend
        activated = (mixed * half).astype(bf16)
        activated_ref[now, :] = activated
        slope_ref[now, :] = (
            half + mixed * (half - half * half) * (2.0 * base + (6.0 * base * cube) * square)
        ).astype(bf16)
        projected = dot(activated, glu_ref[...]) + bias
        gate = 0.5 + 0.5 * jnp.tanh(0.5 * projected[:, width:])
        gated = projected[:, :width] * gate
        gate_ref[now, :] = gate.astype(bf16)
        gate_slope_ref[now, :] = (gated - gated * gate).astype(bf16)
        after = x_ref[now, :].astype(f32) + gated
        masked = after * wide(valid_rows(left, first, steps), width)
        if reverse:
            masked_ref[now, :] = masked.astype(bf16)
        else:
            next_ref[now, :] = after
            total += jnp.sum(masked, axis=0, keepdims=True)
            squares += jnp.sum(masked * after, axis=0, keepdims=True)
            parts = copy_parts(kept_ref.at[now, :], kept_out.at[now, :], sems.at[block])
            begin(parts)
            copies += parts
    if not reverse:
        acc_ref[0:1, :] = total
        acc_ref[1:2, :] = squares
        for j in range(sums_ref.shape[0]):
            sums_ref[j] = acc_ref[...]
        finished(copies)


def mix(k, info, inputs, arrays, devices, fetch, spill=()):
    parts = inputs[0]
    ends, lifted, _, x = arrays[:4]
    rows, width = x.shape
    states = lifted.shape[1]
    seq_devices, seqs, _ = parts.shape
    scratch = [pltpu.VMEM(ends.shape, f32), pltpu.VMEM((rows // (2 if k == 1 else BLOCKS), states), f32)]
    if k == 1:
        outs = [near((rows, states), bf16)] + [near((rows, width), bf16)] * 5
    else:
        kept = (rows, kept_pack(width, states).width)
        outs = [near((rows, width), f32), moved((devices, 2, width), f32), (in_hbm, pltpu.HBM(kept, bf16))]
        scratch += [pltpu.VMEM((2, width), f32), pltpu.VMEM(kept, bf16), pltpu.SemaphoreType.DMA((BLOCKS, 1))]
    scratch += Powers.scratch(seqs, seq_devices, states // 2, True)
    return call(
        partial(mix_kernel, k), info, inputs, arrays, (), outs, scratch, "mix", fetch=fetch, spill=spill
    )


def glu_back_kernel(k, seqs, info_ref, decay_ref, phase_ref, *refs, begin_others):
    reverse = k == 0
    if k == 0:
        sums_ref, stats_ref, gain_ref, shift_ref, lift_pack_ref, kept_ref, normed_in, glu_in, mix_in = refs[:9]
        tables, refs = refs[-3:], refs[9:-3]
    else:
        start_ref, normed_ref, slope_ref, gate_ref, gate_slope_ref, glu_ref, mix_ref = refs[:7]
        tables, refs = refs[-3:], refs[7:-3]
    out_ref, bias_grad_ref, skip_grad_ref, ends_ref, part_ref = refs[:5]
    refs = refs[5:]
    rows, width = out_ref.shape[0], skip_grad_ref.shape[1]
    states = 2 * decay_ref.shape[1]
    names = ("projected", "mixed", "dh", "back")
    projected_ref, mixed_ref, dh_ref, back_ref = glu_pack(width, states).views(out_ref, *names)
    if k == 0:
        total_ref, normed_ref, slopes_ref, glu_ref, mix_ref, sems, weight_sems = refs
        pack = kept_pack(width, states)
        back_normed_ref, start_ref, later_ref = lift_pack(width, states).views(
            lift_pack_ref, "back_normed", "back", "normed"
        )
        slope_ref, gate_ref, gate_slope_ref = pack.views(slopes_ref, "slope", "gate", "gate_slope")
    group = ends_ref.shape[1]
    size = rows // BACK_BLOCKS
    steps = size // group
    where = Where(info_ref, seqs, rows // seqs)
    if k == 1:
        (wide_ref,) = refs
        begin_others()
        shuffle_rows(wide_ref, start_ref)
    else:
        copies = {}
        for block, _, now in blocks_of(rows, group, reverse, BACK_BLOCKS):
            lanes = slice(0, 3 * width)
            copies[block] = copy_parts(kept_ref.at[now, lanes], slopes_ref.at[now, :], sems.at[0, block])
            copies[block] += copy_parts(normed_in.at[now, :], normed_ref.at[now, :], sems.at[1, block])
        weights = copy_parts(glu_in.at[k], glu_ref, weight_sems.at[0])
        weights += copy_parts(mix_in.at[k], mix_ref, weight_sems.at[1])
        for n, block in enumerate(order(BACK_BLOCKS, reverse)):
            begin(copies[block])
            if n == 0:
                begin(weights)
        begin_others()
        sums = jnp.sum(sums_ref[...], axis=0)
        total_ref[...] = sums
        root, count = stats_ref[1:2, :], stats_ref[2:3, 0:1]
        gain, shift = gain_ref[1:2, :], shift_ref[1:2, :]
        by_normed = sums[0:1] / count
        fixed = (gain * sums[1:2] - shift * sums[0:1]) / count
    powers = Powers(k, True, where, decay_ref, phase_ref, *tables)
    left = where.steps_left()
    lam = powers.lam[...]
    ends_ref[...] = jnp.zeros_like(ends_ref)
    bias_grad = jnp.zeros((1, 2 * width), f32)
    skip_grad = jnp.zeros((1, width), f32)
    for block, first, now in blocks_of(rows, group, reverse, BACK_BLOCKS):
        valid = wide(valid_rows(left, first, steps), width)
        if k == 1:
            back = wide_ref[first : first + steps].reshape(size, width) * valid
        else:
            finished(copies[block])
            back = start_ref[now, :].astype(f32) + root * (
                gain * back_normed_ref[now, :].astype(f32)
                - valid * (fixed + by_normed * later_ref[now, :].astype(f32))
            )
        back_ref[now, :] = back.astype(bf16)
        value_back = (back * gate_ref[now, :].astype(f32)).astype(bf16)
        gate_back = (back * gate_slope_ref[now, :].astype(f32)).astype(bf16)
        back_projected = jnp.concatenate([value_back, gate_back], axis=1)
        projected_ref[now, :] = back_projected
        bias_grad += jnp.sum(back_projected.astype(f32), axis=0, keepdims=True)
        if k == 0 and block == BACK_BLOCKS - 1:
            finished(weights)
        back_activated = dot_t(back_projected, glu_ref[...])
        back_mixed = (slope_ref[now, :].astype(f32) * back_activated).astype(bf16)
        mixed_ref[now, :] = back_mixed
        skip_grad += jnp.sum(back_mixed.astype(f32) * normed_ref[now, :].astype(f32), axis=0, keepdims=True)
        back_state = dot_t(back_mixed, mix_ref[...]).astype(bf16)
        dh_ref[now, :] = back_state
        wide_state = back_state.astype(f32)

        def drive(t, real_lanes, imag_lanes):
            at = slice(t * group, (t + 1) * group)
            return wide_state[at, real_lanes], wide_state[at, imag_lanes]

        shift = 1 if reverse else -1
        scan_block(ends_ref, drive, left, lam, shift, first, steps, reverse)
    bias_grad_ref[...] = bias_grad
    skip_grad_ref[...] = skip_grad
    part = stretch_part(ends_ref, powers.table, reverse, seqs)
    for j in range(part_ref.shape[0]):
        part_ref[j] = part


def glu_back(k, seqs, seq_devices, info, inputs, arrays, away, rows, width, after, fetch, spill=()):
    states = inputs[0].shape[1]
    outs = [
        near((rows, glu_pack(width, 2 * states).width), bf16),
        moved((1, 2 * width), f32),
        moved((1, width), f32),
        near((2 * states // LANES, seqs * CHUNKS, LANES), f32),
        moved((seq_devices, seqs, 2 * states), f32),
    ]
    if k == 1:
        scratch = [pltpu.VMEM((rows // seqs // CHUNKS, seqs, CHUNKS, width), f32)]
    else:
        outs += [moved((2, width), f32), near((rows, width), bf16)]
        scratch = [
            pltpu.VMEM((rows, 3 * width), bf16),
            pltpu.VMEM((width, 2 * width), bf16),
            pltpu.VMEM((2 * states, width), bf16),
            pltpu.SemaphoreType.DMA((2, BACK_BLOCKS, 1)),
            pltpu.SemaphoreType.DMA((2, 1)),
        ]
    scratch += Powers.scratch(seqs, seq_devices, states, False)
    return call(
        partial(glu_back_kernel, k, seqs), info, inputs, arrays, away, outs, scratch, "glu_back", after, fetch, spill,
        late=True,
    )


def lift_back_kernel(
    k, info_ref, parts_ref, stats_ref, skip_ref, decay_ref, phase_ref, gain_ref, shift_ref, *refs
):
    reverse = last = k == 0
    ends_ref, glu_pack_ref = refs[:2]
    states, width = 2 * decay_ref.shape[1], stats_ref.shape[1]
    mixed_ref, dh_ref, back_ref = glu_pack(width, states).views(glu_pack_ref, "mixed", "dh", "back")
    normed_ref, state_ref, weight_ref = refs[2:5]
    tables, refs = refs[-4:], refs[5:-4]
    if last:
        back_lifted_ref, sums_ref, lam_grad_ref, scale_grad_ref, ahead_ref = refs[:5]
        refs = refs[5:]
    else:
        out_ref, sums_ref, lam_grad_ref, scale_grad_ref = refs[:4]
        back_lifted_ref, back_normed_ref, kept_back_ref, kept_normed_ref = lift_pack(width, states).views(
            out_ref, "lifted", "back_normed", "back", "normed"
        )
        kept_back_ref[...] = back_ref[...]
        kept_normed_ref[...] = normed_ref[...]
        refs = refs[4:]
    h_ref, low_ref, acc_ref, lam_acc_ref, scale_acc_ref = refs
    rows, width = normed_ref.shape
    group = ends_ref.shape[1]
    seqs = parts_ref.shape[1]
    steps = rows // 1 // group
    states = decay_ref.shape[1]
    where = Where(info_ref, seqs, rows // seqs)
    powers = Powers(k, True, where, decay_ref, phase_ref, *tables)
    chunk_starts(h_ref, where.seq, parts_ref, powers.leaps, ends_ref, powers.table, reverse)
    lam_acc_ref[...] = jnp.zeros_like(lam_acc_ref)
    scale_acc_ref[...] = jnp.zeros_like(scale_acc_ref)
    left = where.steps_left()
    lam, scale = powers.lam[...], powers.scale[...]
    root, gain, shift_row = stats_ref[1:2, :], gain_ref[k : k + 1, :], shift_ref[k : k + 1, :]
    skip = skip_ref[k : k + 1, :]
    gain_sum = jnp.zeros((1, width), f32)
    shift_sum = jnp.zeros((1, width), f32)
    shift = 1 if reverse else -1
    for _, first, now in blocks_of(rows, group, reverse, 1):
        moving = [left > first + t + shift for t in range(steps)]
        valid = [left > first + t for t in range(steps)]
        dh = dh_ref[now, :].astype(f32)
        normed = normed_ref[now, :]
        lifted = dot(normed, weight_ref[...]).astype(bf16).astype(f32)
        state = state_ref[now, :].astype(f32)
        for low in range(0, states, LANES):
            real_lanes = slice(low, low + LANES)
            imag_lanes = slice(states + low, states + low + LANES)
            gr, gi = h_ref[low // LANES], h_ref[(states + low) // LANES]
            lr, li = lam[:, real_lanes], lam[:, imag_lanes]
            part = scale[:, real_lanes]
            sum_r, sum_i = lam_acc_ref[:, real_lanes], lam_acc_ref[:, imag_lanes]
            sum_s = scale_acc_ref[:, real_lanes]
            for t in order(steps, reverse):
                at = slice(t * group, (t + 1) * group)
                hr, hi = state[at, real_lanes], state[at, imag_lanes]
                ur, ui = lifted[at, real_lanes], lifted[at, imag_lanes]
                mr, mi = jnp.where(moving[t], gr, 0.0), jnp.where(moving[t], gi, 0.0)
                sum_r += mr * hr + mi * hi
                sum_i += mi * hr - mr * hi
                nr, ni = cmul(lr, li, gr, gi)
                gr = jnp.where(moving[t], nr, gr) + dh[at, real_lanes]
                gi = jnp.where(moving[t], ni, gi) + dh[at, imag_lanes]
                vr, vi = jnp.where(valid[t], gr, 0.0), jnp.where(valid[t], gi, 0.0)
                sum_s += vr * ur + vi * ui
                low_ref[at, real_lanes] = part * vr
                low_ref[at, imag_lanes] = part * vi
            h_ref[low // LANES] = gr
            h_ref[(states + low) // LANES] = gi
            lam_acc_ref[:, real_lanes] = sum_r
            lam_acc_ref[:, imag_lanes] = sum_i
            scale_acc_ref[:, real_lanes] = sum_s
        back_lifted = low_ref[...].astype(bf16)
        back_lifted_ref[now, :] = back_lifted
        back_normed = dot_t(back_lifted, weight_ref[...]) + skip * mixed_ref[now, :].astype(f32)
        gain_sum += jnp.sum(back_normed * normed.astype(f32), axis=0, keepdims=True)
        shift_sum += jnp.sum(back_normed, axis=0, keepdims=True)
        if last:
            ahead_ref[now, :] = (back_ref[now, :].astype(f32) + (root * gain) * back_normed).astype(bf16)
        else:
            back_normed_ref[now, :] = back_normed.astype(bf16)
    lam_grad = jnp.sum(lam_acc_ref[...], axis=0, keepdims=True)
    scale_grad = jnp.sum(scale_acc_ref[...], axis=0, keepdims=True)
    acc_ref[0:1, :] = (gain_sum - shift_row * shift_sum) / gain
    acc_ref[1:2, :] = shift_sum
    lam_grad_ref[...] = lam_grad
    scale_grad_ref[...] = scale_grad
    for j in range(sums_ref.shape[0]):
        sums_ref[j] = acc_ref[...]


def lift_back(k, info, inputs, arrays, devices, after=(), fetch=()):
    parts, stats, decay = inputs[0], inputs[1], inputs[3]
    ends, packed = arrays[:2]
    rows, width, states = packed.shape[0], stats.shape[1], 2 * decay.shape[1]
    seq_devices, seqs, _ = parts.shape
    table = ends.shape
    acc = (2, width)
    outs = [near((rows, states if k == 0 else lift_pack(width, states).width), bf16), moved((devices,) + acc, f32)]
    outs += [moved((1, states), f32), moved((1, states // 2), f32)]
    if k == 0:
        outs.append(moved((rows, width), bf16))
    scratch = [
        pltpu.VMEM(table, f32),
        pltpu.VMEM((rows // 1, states), f32),
        pltpu.VMEM(acc, f32),
        pltpu.VMEM((table[1], states), f32),
        pltpu.VMEM((table[1], states // 2), f32),
    ]
    scratch += Powers.scratch(seqs, seq_devices, states // 2, True)
    return call(partial(lift_back_kernel, k), info, inputs, arrays, (), outs, scratch, "lift_back", after, fetch)


def two_parts(rows):
    high = rows.astype(bf16).astype(f32)
    return jnp.concatenate([high, rows - high], axis=0)


def one_part(rows):
    half = rows.shape[0] // 2
    return rows[:half] + rows[half:]


def halves_kernel(parts, pairs, small, info_ref, *refs):
    keep_ref, send_ref = refs[-2:]
    width = keep_ref.shape[1]
    even = lax.axis_index("seq") % 2 == 0
    if small:
        small_refs, refs = refs[:4], refs[4:]
    products = [t_dot(*(refs[n][:, lanes] for n, lanes in pair)) for pair in pairs]
    first = 0
    for n, rows, (r, c), (q, d) in parts:
        a = products[n][r : r + rows, c : c + width].astype(bf16)
        b = products[n][q : q + rows, d : d + width].astype(bf16)
        keep_ref[first : first + rows, :] = jnp.where(even, a, b)
        send_ref[first : first + rows, :] = jnp.where(even, b, a)
        first += rows
    if small:
        skip_ref, bias_ref, lam_ref, scale_ref = small_refs
        extra = keep_ref.shape[0] - first
        low = jnp.concatenate([skip_ref[...], bias_ref[:, :width], bias_ref[:, width:]], axis=0)
        scale = jnp.concatenate([scale_ref[...], jnp.zeros((1, width - scale_ref.shape[1]), f32)], axis=1)
        high = jnp.concatenate([lam_ref[...], scale, jnp.zeros((1, width), f32)], axis=0)
        rest = [jnp.zeros((EXTRA // 2 - 3, width), f32)], [jnp.zeros((extra - EXTRA, width), f32)]
        low, high = (two_parts(jnp.concatenate([x, *rest[0]], axis=0)) for x in (low, high))
        low, high = (jnp.concatenate([x, *rest[1]], axis=0).astype(bf16) for x in (low, high))
        keep_ref[first:, :] = jnp.where(even, low, high)
        send_ref[first:, :] = jnp.where(even, high, low)


def halves(info, parts, pairs, small, arrays, width, name, after=()):
    rows = sum(p[1] for p in parts)
    if small:
        rows += EXTRA * (lax.axis_size("seq") // 2)
    outs = [moved((rows, width), bf16)] * 2
    return call(partial(halves_kernel, parts, pairs, bool(small)), info, small, arrays, (), outs, [], name, after)


def place_of(axis):
    return lax.axis_index("batch") if axis == "batch" else lax.axis_index("seq") // 2


def total_of(refs, rows):
    total = refs[0][rows, :].astype(f32)
    for ref in refs[1:]:
        total += ref[rows, :].astype(f32)
    return total


def split_kernel(chips, sets, xor, info_ref, *refs):
    n_in = 2 * len(sets)
    outs = refs[n_in:]
    place = place_of("seq")
    for m in range(chips):
        chip = place ^ m if xor else m
        low = 0
        for n, parts in enumerate(sets):
            first = 0
            for rows in parts:
                share = rows // chips
                start = first + chip * share
                if xor:
                    start = pl.multiple_of(start, 16)
                total = total_of(refs[2 * n : 2 * n + 2], pl.ds(start, share))
                if share == EXTRA:
                    total = two_parts(one_part(total))
                if xor:
                    outs[m][low : low + share, :] = total.astype(outs[m].dtype)
                else:
                    base = m * (outs[0].shape[0] // chips) + low
                    outs[0][base : base + share, :] = total.astype(outs[0].dtype)
                first, low = first + rows, low + share


def split(info, sets, arrays, xor, after=()):
    chips = lax.axis_size("seq") // 2
    width = arrays[0].shape[1]
    rows = sum(map(sum, sets))
    outs = [moved((rows, width), bf16)]
    if xor:
        outs = [moved((rows // chips, width), f32)] + [moved((rows // chips, width), bf16)] * (chips - 1)
    return call(partial(split_kernel, chips, sets, xor), info, arrays, (), (), outs, [], "split", after, us=0.8)


def cut_kernel(extra, info_ref, *refs):
    low_ref, refs = refs[-1], refs[:-1]
    batches, share, width = low_ref.shape
    arrays, outs = refs[:-batches], refs[-batches:]
    place = place_of("batch")
    rows = batches * share
    low_ref[...] = total_of(arrays, slice(0, rows)).reshape(batches, share, width)
    under = two_parts(one_part(total_of(arrays, slice(rows, rows + extra))))
    for m in range(batches):
        outs[m][:share, :] = low_ref[place ^ m].astype(outs[m].dtype)
        outs[m][share:, :] = under.astype(outs[m].dtype)


def cut(info, arrays, extra, after=()):
    batches = lax.axis_size("batch")
    rows, width = arrays[0].shape
    share = (rows - extra) // batches
    outs = [moved((share + extra, width), f32)] + [moved((share + extra, width), bf16)] * (batches - 1)
    scratch = [pltpu.VMEM((batches, share, width), f32)]
    return call(partial(cut_kernel, extra), info, arrays, (), (), outs, scratch, "cut", after, us=1.2)


def sum_kernel(info_ref, *refs):
    total = refs[0][...].astype(f32)
    for ref in refs[1:-1]:
        total += ref[...].astype(f32)
    rows = total.shape[0] - EXTRA
    refs[-1][:rows, :] = total[:rows].astype(bf16)
    refs[-1][rows:, :] = two_parts(one_part(total[rows:])).astype(bf16)


def sum_of(info, arrays, after=()):
    return call(sum_kernel, info, arrays, (), (), [moved(arrays[0].shape, bf16)], [], "total", after, us=0.6)


def join_kernel(info_ref, *refs):
    pieces, out_ref, low_ref = refs[:-2], refs[-2], refs[-1]
    batches, share, width = low_ref.shape
    place = place_of("batch")
    for m, ref in enumerate(pieces):
        low_ref[place ^ m] = ref[:share, :].astype(f32)
    rows = batches * share
    out_ref[:rows, :] = low_ref[...].reshape(rows, width).astype(bf16)
    out_ref[rows:, :] = pieces[0][share:, :]


def join(info, arrays, extra, after=()):
    batches = len(arrays)
    rows, width = arrays[0].shape
    share = rows - extra
    outs = [moved((batches * share + extra, width), bf16)]
    scratch = [pltpu.VMEM((batches, share, width), f32)]
    return call(join_kernel, info, arrays, (), (), outs, scratch, "join", after, us=0.6)


def trade(x, axis, mask):
    size = lax.axis_size(axis)
    return lax.ppermute(x, axis, [(i, i ^ mask) for i in range(size)])


def sent(arrays, axis, masks):
    return [arrays[0]] + [trade(x, axis, m) for x, m in zip(arrays[1:], masks)]


def to_others(x, axis, masks):
    return [x] + [trade(x, axis, m) for m in masks]


def gate_kernel(*refs):
    pass


def gate(info, arrays, after):
    anywhere = pl.BlockSpec(memory_space=pl.ANY)
    outs = [(anywhere, jax.ShapeDtypeStruct(x.shape, x.dtype)) for x in arrays]
    aliases = {1 + i: i for i in range(len(arrays))}
    return run(gate_kernel, info, list(arrays), [anywhere] * len(arrays), outs, [], "gate", after, aliases)


def small_grads(norms, rows, decay_log, phase_log, refs):
    gain_ref, shift_ref, decay_grad_ref, phase_grad_ref, skip_grad_ref, bias_grad_ref = refs
    blocks, states = decay_log.shape
    width = norms[0].shape[1]
    for k in range(blocks):
        gain_ref[k : k + 1, :], shift_ref[k : k + 1, :] = norms[k][0:1], norms[k][1:2]
        low, high = rows[k]
        skip, bias_low, bias_high, lam, scale = low[0:1], low[1:2], low[2:3], high[0:1], high[1:2]
        skip_grad_ref[k : k + 1, :] = skip
        bias_grad_ref[k : k + 1, :width] = bias_low
        bias_grad_ref[k : k + 1, width:] = bias_high
        rate, angle = jnp.exp(decay_log[k : k + 1]), jnp.exp(phase_log[k : k + 1])
        size, fade = jnp.exp(-rate), jnp.exp(-2.0 * rate)
        lam_real, lam_imag = size * jnp.cos(angle), size * jnp.sin(angle)
        real, imag = lam[:, :states], lam[:, states : 2 * states]
        by_rate = scale[:, :states] * fade * lax.rsqrt(1.0 - fade) - (real * lam_real + imag * lam_imag)
        decay_grad_ref[k : k + 1, :] = rate * by_rate
        phase_grad_ref[k : k + 1, :] = angle * (imag * lam_real - real * lam_imag)


def input_grad(where, sums, stats_ref, gain_ref, tokens_ref, wide_ref, grad_ref):
    seqs, span, width = tokens_ref.shape
    shuffle = shuffle_matrix(span, True)
    average, root = stats_ref[0:1, :], stats_ref[1:2, :]
    factor = root * gain_ref[0:1, :] / stats_ref[2:3, 0:1]
    by_gain = factor * sums[0:1] * root
    fixed = factor * sums[1:2] - by_gain * average
    step = lax.broadcasted_iota(jnp.int32, (span, 1), 0)
    for s in range(seqs):
        valid = (step < where.lefts[s]).astype(f32)
        ahead = dot(shuffle, wide_ref[:, s].reshape(span, width).astype(bf16))
        grad_ref[s] = (ahead - valid * (fixed + by_gain * tokens_ref[s].astype(f32))).astype(bf16)


def results_kernel(chips, info_ref, sums_ref, norm1_ref, decay_ref, phase_ref, stats_ref, gain_ref, *refs):
    (tokens_in, ahead_in), pieces, refs = refs[:2], refs[2 : 2 + 4 * chips], refs[2 + 4 * chips :]
    glu_ref, mix_ref, lift_ref, grad_out, *small_refs = refs[:10]
    low_ref, wide_ref, tokens_ref, ahead_ref, rows_ref, grad_ref, in_sems, sems, own_sems = refs[10:]
    own = [
        pltpu.make_async_copy(ahead_in, ahead_ref, own_sems.at[0]),
        pltpu.make_async_copy(tokens_in, tokens_ref, own_sems.at[1]),
    ]
    place = place_of("seq")
    core = lax.axis_index("seq") % 2
    _, rows, width = wide_ref.shape
    half, quarter = rows // 2, rows // 4
    arriving = []
    for n, piece in enumerate(pieces):
        parts = [pltpu.make_async_copy(piece, low_ref.at[n], in_sems.at[n])]
        begin(parts)
        arriving.append(parts)
    begin(own)
    copies = []
    extras = [[jnp.zeros((EXTRA // 2, width), f32)] * 2 for _ in range(2)]
    for n in range(4 * chips):
        finished(arriving[n])
        k, n_in = divmod(n, 2 * chips)
        chip, side = place ^ (n_in % chips), core if n_in < chips else 1 - core
        extra = one_part(low_ref[n, rows:, :].astype(f32))
        extras[k][n_in // chips] = jnp.where(chip == 0, extra, extras[k][n_in // chips])
        column = pl.multiple_of(side * width, width)
        row = pl.multiple_of(chip * half, 8)
        low = pl.multiple_of(side * (quarter * chips) + chip * quarter, 8)
        wide_ref[n] = low_ref[n, :rows, :].astype(f32)
        for i, (first, size, target) in enumerate(
            (
                (0, half, glu_ref.at[k, pl.ds(row, half), pl.ds(column, width)]),
                (half, quarter, mix_ref.at[k, pl.ds(low, quarter), :]),
                (half + quarter, quarter, lift_ref.at[k, pl.ds(low, quarter), :]),
            )
        ):
            copies.append(pltpu.make_async_copy(wide_ref.at[n, pl.ds(first, size), :], target, sems.at[n, i]))
            copies[-1].start()
    even = core == 0
    sums = sums_ref[...]
    finished(own)
    rows_ref[...] = ahead_ref[...].astype(f32).reshape(rows_ref.shape)
    seqs, span, _ = tokens_ref.shape
    input_grad(Where(info_ref, seqs, span), sums, stats_ref, gain_ref, tokens_ref, rows_ref, grad_ref)
    copies.append(pltpu.make_async_copy(grad_ref, grad_out, own_sems.at[2]))
    copies[-1].start()
    small_grads(
        (sums, norm1_ref[...]),
        [(jnp.where(even, mine, other), jnp.where(even, other, mine)) for mine, other in extras],
        decay_ref[...],
        phase_ref[...],
        small_refs,
    )
    finished(copies)


def results(info, sums, norm1, decay_log, phase_log, stats, gain, tokens, ahead, pieces, after=()):
    seqs, span, _ = tokens.shape
    rows, width = pieces[0].shape
    rows -= EXTRA
    count = len(pieces)
    anywhere = pl.BlockSpec(memory_space=pl.ANY)
    shapes = [(2, width, 2 * width), (2, width, width), (2, width, width)]
    outs = [(anywhere, jax.ShapeDtypeStruct(shape, f32)) for shape in shapes]
    outs.append((anywhere, jax.ShapeDtypeStruct(tokens.shape, bf16)))
    blocks, states = decay_log.shape
    outs += [moved((blocks, n), f32) for n in (width, width, states, states, width, 2 * width)]
    scratch = [
        pltpu.VMEM((count, rows + EXTRA, width), bf16),
        pltpu.VMEM((count, rows, width), f32),
        pltpu.VMEM(tokens.shape, bf16),
        pltpu.VMEM(ahead.shape, bf16),
        pltpu.VMEM((span // CHUNKS, seqs, CHUNKS, width), f32),
        pltpu.VMEM(tokens.shape, bf16),
        pltpu.SemaphoreType.DMA((count,)),
        pltpu.SemaphoreType.DMA((count, 3)),
        pltpu.SemaphoreType.DMA((3,)),
    ]
    inputs = [sums, norm1, decay_log, phase_log, stats, gain]
    given = [*inputs, *map(there, (tokens, ahead)), *pieces]
    specs = [in_vmem] * len(inputs) + [in_hbm] * 2 + [anywhere] * count
    return run(partial(results_kernel, count // 4), info, given, specs, outs, scratch, "results", after, us=7.0)


def norms_kernel(info_ref, sums_ref, total_ref):
    total_ref[...] = jnp.sum(sums_ref[...], axis=0)


def norms(info, sums, after=()):
    outs = [moved(sums.shape[1:], f32)]
    return call(norms_kernel, info, (sums,), (), (), outs, [], "norms", after, us=0.6)


def leave_kernel(seqs, info_ref, rows_ref, out_ref, wide_ref):
    _, span, width = out_ref.shape
    wide_ref[...] = rows_ref[...].astype(f32).reshape(wide_ref.shape)
    shuffle = shuffle_matrix(span, True)
    for s in range(seqs):
        out_ref[s] = dot(shuffle, wide_ref[:, s].reshape(span, width).astype(bf16)).astype(bf16)


def leave(info, rows, seqs, after=()):
    span, width = rows.shape[0] // seqs, rows.shape[1]
    scratch = [pltpu.VMEM((span // CHUNKS, seqs, CHUNKS, width), f32)]
    outs = [moved((seqs, span, width), bf16)]
    return call(partial(leave_kernel, seqs), info, (rows,), (), (), outs, scratch, "leave", after)


def to_all(x, axes):
    return lax.all_to_all(x, axes, split_axis=0, concat_axis=0, tiled=True)


def local(
    tokens,
    lengths,
    cotangent,
    norm_gain,
    norm_shift,
    lift_weight,
    decay_log,
    phase_log,
    skip_gain,
    mix_weight,
    glu_weight,
    glu_bias,
):
    both = ("seq", "batch")
    seq_devices, batches = lax.axis_size("seq"), lax.axis_size("batch")
    devices, chips = seq_devices * batches, seq_devices // 2
    seqs, span, width = tokens.shape
    rows = seqs * span
    info = lengths
    turns = (decay_log, phase_log)
    norms_in = (norm_gain, norm_shift)
    states = decay_log.shape[1]
    half = width // 2

    sums, tokens_here, lift_w = enter(info, tokens, devices, [(lift_weight, 0)])
    sums = to_all(sums, both)
    normed, lifted, ends, part, stats0, x, mix_w, glu_w = lift(
        0, seqs, seq_devices, info, (sums, *norms_in, *turns), (tokens_here, lift_w), rows,
        [(mix_weight, 0), (glu_weight, 0)],
    )
    x1, sums, kept, lift_w, normed0 = mix(
        0, info, (to_all(part, "seq"), skip_gain, glu_bias, *turns), (ends, lifted, normed, x, mix_w, glu_w),
        devices, [(lift_weight, 1)], (normed,),
    )
    sums = to_all(sums, both)

    normed1, lifted1, ends, part, stats1, mix_w, glu_w = lift(
        1, seqs, seq_devices, info, (sums, *norms_in, *turns, stats0), (x1, lift_w), rows,
        [(mix_weight, 1), (glu_weight, 1)],
    )
    state1, activated1, slope1, gate1, gate_slope1, masked, cot = mix(
        1, info, (to_all(part, "seq"), skip_gain, glu_bias, *turns), (ends, lifted1, normed1, x1, mix_w, glu_w),
        devices, [(cotangent, None)],
    )

    glu_packed, bias_grad1, skip_grad1, ends, part, lift_w, masked = glu_back(
        1, seqs, seq_devices, info, turns, (cot, normed1, slope1, gate1, gate_slope1, glu_w, mix_w), (), rows, width,
        (), [(lift_weight, 1)], [masked],
    )
    lift_packed, sums, lam_grad1, scale_grad1 = lift_back(
        1, info, (to_all(part, "seq"), stats1, skip_gain, *turns, *norms_in),
        (ends, glu_packed, normed1, state1, lift_w), devices,
    )
    glu_part, mix_part, lift_part = (0, width, (0, 0), (0, width)), (1, half, (0, 0), (half, 0)), (2, half, (0, 0), (half, 0))
    glu_lanes, lift_lanes = glu_pack(width, 2 * states).lanes, lift_pack(width, 2 * states).lanes
    kept_lanes, every = kept_pack(width, 2 * states).lanes, slice(None)
    out = halves(
        info,
        (glu_part, mix_part, lift_part),
        (
            ((0, every), (1, glu_lanes["projected"])),
            ((2, every), (1, glu_lanes["mixed"])),
            ((3, every), (4, lift_lanes["lifted"])),
        ),
        (skip_grad1, bias_grad1, lam_grad1, scale_grad1),
        (activated1, glu_packed, state1, normed1, lift_packed),
        width,
        "halves1",
    )
    keep1, send = out
    got1 = trade(send, "seq", 1)
    (produced,) = out = leave(info, masked, seqs, (out.tick,))
    shares = (width, half, half)
    z, xy = range(1, batches), range(2, seq_devices, 2)
    extra = EXTRA * chips
    out = split(info, ((*shares, extra),), [keep1, got1], True, (out.tick,))
    pieces1 = sent(out, "seq", xy)
    sums = to_all(sums, both)

    state_lanes = (slice(None), kept_lanes["state"])
    out = glu_back(
        0, seqs, seq_devices, info, (*turns, sums, stats1, *norms_in), (lift_packed,),
        (kept, normed0, glu_weight, mix_weight), rows, width, (),
        [(kept, state_lanes), (lift_weight, 0)],
    )
    glu_packed, bias_grad0, skip_grad0, ends, part, norm_sums1, normed, state, lift_w = out
    activated_lanes = (slice(None), kept_lanes["activated"])
    parts, *pieces1 = gate(info, [to_all(part, "seq"), *pieces1], ())
    back_lifted0, sums, lam_grad0, scale_grad0, ahead, activated = out = lift_back(
        0, info, (parts, stats0, skip_gain, *turns, *norms_in),
        (ends, glu_packed, normed, state, lift_w), devices, (), [(kept, activated_lanes)],
    )

    keep0, send = out = halves(
        info,
        (glu_part, mix_part, lift_part),
        (
            ((0, every), (1, glu_lanes["projected"])),
            ((2, every), (1, glu_lanes["mixed"])),
            ((3, every), (4, every)),
        ),
        (skip_grad0, bias_grad0, lam_grad0, scale_grad0),
        (activated, glu_packed, state, normed, back_lifted0),
        width,
        "halves0",
    )
    got0 = trade(send, "seq", 1)
    out1 = cut(info, pieces1, EXTRA, (out.tick,))
    out0 = split(info, ((*shares, extra),), [keep0, got0], True, (out1.tick,))
    sum1 = sum_of(info, sent(out1, "batch", z), (out0.tick,))
    (sums,) = gate(info, [sums], (sum1.tick,))
    sums = to_all(sums, both)
    (own1,) = out = join(info, to_others(sum1[0], "batch", z), EXTRA, (sum1.tick,))
    out0 = cut(info, sent(out0, "seq", xy), EXTRA, (out.tick,))
    sum0 = sum_of(info, sent(out0, "batch", z))
    (own0,) = out = join(info, to_others(sum0[0], "batch", z), EXTRA)
    (sums,) = norms(info, sums, (out.tick,))
    pieces = []
    for own in (own0, own1):
        total = to_others(own, "seq", xy)
        pieces += total + [trade(x, "seq", 1) for x in total]
    out = results(info, sums, norm_sums1, *turns, stats0, norm_gain, tokens, ahead, pieces)
    grad_glu, grad_mix, grad_lift, tokens_grad, grad_gain, grad_shift, grad_decay, grad_phase, grad_skip, grad_bias = out
    return (
        produced,
        tokens_grad,
        grad_gain,
        grad_shift,
        grad_lift,
        grad_decay,
        grad_phase,
        grad_skip,
        grad_mix,
        grad_glu,
        grad_bias,
    )


def solution(mesh):
    split = P("batch", "seq", None)
    placed = (split, P("batch"), split) + (P(),) * 9
    return jax.shard_map(
        local,
        mesh=mesh,
        in_specs=placed,
        out_specs=(split, split) + (P(),) * 9,
        check_vma=False,
    )
```
